512 devices in a mesh: ys: 16 (over z_lo, x), xs: 32 (over y, z_hi, core).
Axes of the slice: x: 4, y: 8, z: 8 (z_hi: 2, z_lo: 4; z = z_hi * 4 + z_lo), core: 2. Of those that a mesh axis runs over, the one named last changes fastest.
Arguments:
- forward_u: float32 [48, 128, 1024], P(None, 'ys', 'xs'), may hold values from -6 to 6
- forward_v: float32 [48, 128, 1024], P(None, 'ys', 'xs'), may hold values from -6 to 6
- forward_w: float32 [48, 128, 1024], P(None, 'ys', 'xs'), may hold values from -6 to 6
- forward_tracer: float32 [48, 128, 1024], P(None, 'ys', 'xs'), may hold values from -6 to 6
- incoming_u: float32 [48, 128, 1024], P(None, 'ys', 'xs'), may hold values from -6 to 6
- incoming_v: float32 [48, 128, 1024], P(None, 'ys', 'xs'), may hold values from -6 to 6
- incoming_w: float32 [48, 128, 1024], P(None, 'ys', 'xs'), may hold values from -6 to 6
- incoming_tracer: float32 [48, 128, 1024], P(None, 'ys', 'xs'), may hold values from -6 to 6
- diffusion_inverse: float32 [48, 48], replicated, may hold values from -1.5 to 2.5, as said below
- mode_vectors: float32 [48, 48], replicated, may hold values from -1.5 to 2.5, as said below
- mode_inverse: float32 [48, 48], replicated, may hold values from -1.5 to 2.5, as said below
- mode_eigen: float32 [48], replicated, may hold values from 0.0003 to 4
Outputs:
- adjoint_u: float32 [48, 128, 1024], P(None, 'ys', 'xs')
- adjoint_v: float32 [48, 128, 1024], P(None, 'ys', 'xs')
- adjoint_w: float32 [48, 128, 1024], P(None, 'ys', 'xs')
- adjoint_tracer: float32 [48, 128, 1024], P(None, 'ys', 'xs')
The draws below stay inside these ranges and needn't reach their ends.
Inputs may be any that keep to these rules, and one draw needn't show every extreme that they name: `diffusion_inverse`: a given 48 x 48 matrix. `mode_vectors`: a given 48 x 48 matrix. `mode_inverse`: a given 48 x 48 matrix.
All inputs are finite; a program needn't handle non-finite values.
Results may differ from the reference program's by a relative error of at most 0.0003.
Values sent between devices are 32-bit elements; how exact they have to be, the bound alone decides.
A program may use at most 64 MiB of HBM per device.

```python
import math
import jax
import jax.numpy as jnp
from jax import lax

NZ = 48
NX = 1024
NY = 128


def square_draw(key, spread):
    noise = jnp.clip(jax.random.normal(key, (NZ, NZ), jnp.float32), -3.0, 3.0)
    return jnp.eye(NZ, dtype=jnp.float32) + spread * NZ ** (-0.5) * noise


def draw_diffusion_inverse(key, part):
    key = jax.random.fold_in(key, 11)
    return square_draw(key, 0.5)


def draw_mode_vectors(key, part):
    key = jax.random.fold_in(key, 12)
    return square_draw(key, 0.5)


def draw_mode_inverse(key, part):
    key = jax.random.fold_in(key, 13)
    return square_draw(key, 0.5)


def level_of(own_key, shape, pieces, least, largest):
    def one(dim, parts):
        heights = jax.random.uniform(jax.random.fold_in(jax.random.fold_in(own_key, 6), dim), (parts,), jnp.float32, least / len(pieces), largest / len(pieces))
        return jnp.repeat(jnp.exp(heights), shape[dim] // parts).reshape((-1,) + (1,) * (len(shape) - dim - 1))

    level = one(*pieces[0])
    for cut in pieces[1:]:
        level = level * one(*cut)
    return level


def centred(own_key, shape, width, most, cuts=(), kind=jnp.bfloat16):
    factor_of = level_of(own_key, shape, cuts, -0.22, 0.18) if cuts else 1.0
    entries = jax.random.normal(own_key, shape, jnp.float32) * width * factor_of
    return jnp.minimum(jnp.maximum(entries, -most), most).astype(kind)


def setup_inputs(seed: int = 0) -> dict:
    key_list = jax.random.split(jax.random.key(seed), 13)
    forward_u = centred(key_list[0], (NZ, NY, NX), 1.0, 6.0, ((1, 16), (2, 32)), jnp.float32)
    forward_v = centred(key_list[1], (NZ, NY, NX), 1.0, 6.0, ((1, 16), (2, 32)), jnp.float32)
    forward_w = centred(key_list[2], (NZ, NY, NX), 1.0, 6.0, ((1, 16), (2, 32)), jnp.float32)
    forward_tracer = centred(key_list[3], (NZ, NY, NX), 1.0, 6.0, ((1, 16), (2, 32)), jnp.float32)
    incoming_u = centred(key_list[4], (NZ, NY, NX), 1.0, 6.0, ((1, 16), (2, 32)), jnp.float32)
    incoming_v = centred(key_list[5], (NZ, NY, NX), 1.0, 6.0, ((1, 16), (2, 32)), jnp.float32)
    incoming_w = centred(key_list[6], (NZ, NY, NX), 1.0, 6.0, ((1, 16), (2, 32)), jnp.float32)
    incoming_tracer = centred(key_list[7], (NZ, NY, NX), 1.0, 6.0, ((1, 16), (2, 32)), jnp.float32)
    diffusion_inverse = draw_diffusion_inverse(jax.random.fold_in(key_list[12], 71), 0)
    mode_vectors = draw_mode_vectors(jax.random.fold_in(key_list[12], 71), 0)
    mode_inverse = draw_mode_inverse(jax.random.fold_in(key_list[12], 71), 0)
    mode_eigen = jnp.clip(jnp.exp(jax.random.uniform(key_list[11], (NZ,), jnp.float32, math.log(0.0003), math.log(4.0))), 0.0003, 4.0)
    return dict(forward_u=forward_u, forward_v=forward_v, forward_w=forward_w, forward_tracer=forward_tracer, incoming_u=incoming_u, incoming_v=incoming_v, incoming_w=incoming_w, incoming_tracer=incoming_tracer, diffusion_inverse=diffusion_inverse, mode_vectors=mode_vectors, mode_inverse=mode_inverse, mode_eigen=mode_eigen)


time_step = 0.25
viscosity = 0.1
diffusivity = 0.1
buoyancy = 1.0
weno_eps = 1e-06
highest = lax.Precision.HIGHEST

def slab(values, start, length, axis):
    return lax.slice_in_dim(values, start, start + length, axis=axis)

def weno_value(far_left, near_left, center, near_right, far_right):
    first = (2.0 * far_left - 7.0 * near_left + 11.0 * center) / 6.0
    second = (-near_left + 5.0 * center + 2.0 * near_right) / 6.0
    third = (2.0 * center + 5.0 * near_right - far_right) / 6.0
    smooth_first = 13.0 / 12.0 * jnp.square(far_left - 2.0 * near_left + center) + 0.25 * jnp.square(far_left - 4.0 * near_left + 3.0 * center)
    smooth_second = 13.0 / 12.0 * jnp.square(near_left - 2.0 * center + near_right) + 0.25 * jnp.square(near_left - near_right)
    smooth_third = 13.0 / 12.0 * jnp.square(center - 2.0 * near_right + far_right) + 0.25 * jnp.square(3.0 * center - 4.0 * near_right + far_right)
    weight_first = 0.1 / jnp.square(weno_eps + smooth_first)
    weight_second = 0.6 / jnp.square(weno_eps + smooth_second)
    weight_third = 0.3 / jnp.square(weno_eps + smooth_third)
    total = weight_first + weight_second + weight_third
    return (weight_first * first + weight_second * second + weight_third * third) / total

def face_flux(velocity, tracer, axis):
    face_count = tracer.shape[axis] - 5
    stencil = [slab(tracer, offset, face_count, axis) for offset in range(6)]
    upwind = weno_value(stencil[0], stencil[1], stencil[2], stencil[3], stencil[4])
    downwind = weno_value(stencil[5], stencil[4], stencil[3], stencil[2], stencil[1])
    speed = slab(velocity, 2, face_count, axis)
    return speed * jnp.where(speed >= 0.0, upwind, downwind)

def horizontal_tendency(vel_x, vel_y, tracer):
    last = tracer.ndim - 1
    before = tracer.ndim - 2
    rows = tracer.shape[before] - 6
    cols = tracer.shape[last] - 6
    flux_x = face_flux(vel_x, tracer, last)
    flux_y = face_flux(vel_y, tracer, before)
    change_x = slab(flux_x, 1, cols, last) - slab(flux_x, 0, cols, last)
    change_y = slab(flux_y, 1, rows, before) - slab(flux_y, 0, rows, before)
    change_x = slab(change_x, 3, rows, before)
    change_y = slab(change_y, 3, cols, last)
    middle = slab(tracer, 3, rows, before)
    center = slab(middle, 3, cols, last)
    spread = slab(middle, 2, cols, last) + slab(middle, 4, cols, last)
    spread = spread + slab(slab(tracer, 2, rows, before), 3, cols, last) + slab(slab(tracer, 4, rows, before), 3, cols, last)
    spread = spread - 4.0 * center
    return diffusivity * spread - (change_x + change_y)

def vertical_tendency(vel_z, tracer):
    faces = vel_z[:-1] * (0.5 * (tracer[:-1] + tracer[1:]))
    zero_face = jnp.zeros_like(faces[:1])
    return -(jnp.concatenate([faces, zero_face], 0) - jnp.concatenate([zero_face, faces], 0))

def periodic_spread(field):
    return jnp.roll(field, 1, 2) + jnp.roll(field, -1, 2) + jnp.roll(field, 1, 1) + jnp.roll(field, -1, 1) - 4.0 * field

def pressure_adjoint(source, mode_vectors, mode_inverse, mode_eigen):
    in_modes = jnp.einsum('zm,zyx->myx', mode_vectors, source, precision=highest)
    spectrum = jnp.fft.rfft2(in_modes, axes=(1, 2))
    wave_y = jnp.arange(NY).astype(jnp.float32)
    wave_x = jnp.arange(NX // 2 + 1).astype(jnp.float32)
    lam_y = 4.0 * jnp.square(jnp.sin(jnp.pi * wave_y / NY))
    lam_x = 4.0 * jnp.square(jnp.sin(jnp.pi * wave_x / NX))
    denom = mode_eigen[:, None, None] + lam_y[None, :, None] + lam_x[None, None, :]
    solved = jnp.fft.irfft2(-spectrum / denom, s=(NY, NX), axes=(1, 2))
    return jnp.einsum('mz,myx->zyx', mode_inverse, solved, precision=highest)

def reference(forward_u, forward_v, forward_w, forward_tracer, incoming_u, incoming_v, incoming_w, incoming_tracer, diffusion_inverse, mode_vectors, mode_inverse, mode_eigen):
    zero_level = jnp.zeros_like(incoming_w[:1])
    divergence = incoming_u - jnp.roll(incoming_u, 1, 2) + (incoming_v - jnp.roll(incoming_v, 1, 1))
    divergence = divergence + (incoming_w - jnp.concatenate([zero_level, incoming_w[:-1]], 0))
    pressure = pressure_adjoint(divergence, mode_vectors, mode_inverse, mode_eigen)
    upper = jnp.concatenate([pressure[1:], jnp.zeros_like(pressure[:1])], 0)
    mid_u = incoming_u - (jnp.roll(pressure, -1, 2) - pressure)
    mid_v = incoming_v - (jnp.roll(pressure, -1, 1) - pressure)
    mid_w = incoming_w - (upper - pressure)
    lifted = incoming_tracer + buoyancy * time_step * mid_w
    diffused = jnp.einsum('lk,lyx->kyx', diffusion_inverse, lifted, precision=highest)

    def level_adjoint(items):
        vel_x, vel_y, tracer, weight = items

        def tendency(first, second, third):
            return horizontal_tendency(jnp.pad(first, 3, mode='wrap'), jnp.pad(second, 3, mode='wrap'), jnp.pad(third, 3, mode='wrap'))
        _, pull = jax.vjp(tendency, vel_x, vel_y, tracer)
        return pull(weight)
    grad_u, grad_v, grad_c = lax.map(level_adjoint, (forward_u, forward_v, forward_tracer, diffused))
    _, pull_vertical = jax.vjp(vertical_tendency, forward_w, forward_tracer)
    grad_w, grad_cz = pull_vertical(diffused)
    factor = time_step * viscosity
    adjoint_u = mid_u + factor * periodic_spread(mid_u) + time_step * grad_u
    adjoint_v = mid_v + factor * periodic_spread(mid_v) + time_step * grad_v
    adjoint_w = mid_w + factor * periodic_spread(mid_w) + time_step * grad_w
    adjoint_tracer = diffused + time_step * (grad_c + grad_cz)
    return (adjoint_u, adjoint_v, adjoint_w, adjoint_tracer)
```

```python
import functools

import jax
import jax.numpy as jnp
import numpy as np
from jax import lax
from jax.experimental import pallas as pl
from jax.experimental.pallas import tpu as pltpu
from jax.sharding import PartitionSpec as P

MESH = pl.DeviceIdType.MESH
DT = 0.25
NU = 0.1
KAPPA = 0.1
GRAV = 1.0
EPS = 1e-6
F32 = jnp.float32
HI = lax.Precision.HIGHEST
ROWS, COLS = 8, 32


def tables(ns, nt):
    nx, ny = COLS * nt, ROWS * ns
    t = np.arange(nt)
    ring = np.zeros((2, ns, nt))
    ring[0, 0] = 1 / np.sqrt(nt)
    ring[1, 0] = (-1.0) ** t / np.sqrt(nt)
    for j in range(1, ns):
        ring[0, j] = np.sqrt(2 / nt) * np.cos(2 * np.pi * j * t / nt)
        ring[1, j] = np.sqrt(2 / nt) * np.sin(2 * np.pi * j * t / nt)

    def basis(n, k):
        z = np.arange(n)
        if k == 0 or 2 * k == n:
            return [np.cos(2 * np.pi * k * z / n) / np.sqrt(n)]
        return [
            np.sqrt(2 / n) * np.cos(2 * np.pi * k * z / n),
            np.sqrt(2 / n) * np.sin(2 * np.pi * k * z / n),
        ]

    inner = np.zeros((ns, 2, 2, COLS, 2, 2, COLS))
    lamx = np.zeros((ns, 2, 2, COLS))
    for j in range(ns):
        found, lam = [], []
        for k in range(nx // 2 + 1):
            res = k % nt
            own = res in (0, nt // 2) if j == 0 else res in (j, nt - j)
            if own:
                for vec in basis(nx, k):
                    found.append(np.einsum("qt,tc->qc", ring[:, j], vec.reshape(nt, COLS)))
                    lam.append(4 * np.sin(np.pi * k / nx) ** 2)
        block = np.stack(found, -1).reshape(2, COLS, 2, COLS)
        for m in range(2):
            inner[j, :, m, :, :, m, :] = block
            lamx[j, :, m, :] = np.array(lam).reshape(2, COLS)
    inner = inner.reshape(ns, 4 * COLS, 4 * COLS)
    lamx = np.broadcast_to(lamx.reshape(ns, 1, 4 * COLS), (ns, 8, 4 * COLS))
    spectral = np.concatenate([inner, lamx], 1)

    ybase, ylam = [], []
    for k in range(ny // 2 + 1):
        for vec in basis(ny, k):
            ybase.append(vec)
            ylam.append(4 * np.sin(np.pi * k / ny) ** 2)
    ybase = np.stack(ybase)
    lamy = np.broadcast_to(np.array(ylam)[:, None], (ny, 128))
    yfwd = ybase.reshape(ny, ns, 4, 2).transpose(0, 3, 2, 1).reshape(ny, ny)
    yinv = np.zeros((ns, 16, ny))
    for s in range(ns):
        for r in range(14):
            yinv[s, r] = ybase[:, (ROWS * s - 3 + r) % ny]
    yinv = yinv.reshape(16 * ns, ny)
    ring = ring.reshape(nt, nt)
    out = (ring, ring.T, yfwd, yinv, spectral, lamy)
    return tuple(np.ascontiguousarray(v).astype(np.float32) for v in out)


def dot(a, b):
    return lax.dot_general(a, b, (((1,), (0,)), ((), ())), precision=HI, preferred_element_type=F32)


def dot_tn(a, b):
    return lax.dot_general(a, b, (((0,), (0,)), ((), ())), precision=HI, preferred_element_type=F32)


def dot_nt(a, b):
    return lax.dot_general(a, b, (((1,), (1,)), ((), ())), precision=HI, preferred_element_type=F32)


def roll(v, shift, axis=1):
    shift = shift % v.shape[axis]
    return v if shift == 0 else pltpu.roll(v, shift, axis)


def weno_parts(c, u, step, cut):
    stencil = [cut(roll(c, -k * step)) for k in range(-2, 4)]
    pos = u >= 0.0
    a = jnp.where(pos, stencil[0], stencil[5])
    b = jnp.where(pos, stencil[1], stencil[4])
    m = jnp.where(pos, stencil[2], stencil[3])
    p = jnp.where(pos, stencil[3], stencil[2])
    q = jnp.where(pos, stencil[4], stencil[1])
    e0, f0 = a - 2.0 * b + m, a - 4.0 * b + 3.0 * m
    e1, f1 = b - 2.0 * m + p, b - p
    e2, f2 = m - 2.0 * p + q, 3.0 * m - 4.0 * p + q
    r0 = 1.0 / (EPS + (13.0 / 12.0 * e0 * e0 + 0.25 * f0 * f0))
    r1 = 1.0 / (EPS + (13.0 / 12.0 * e1 * e1 + 0.25 * f1 * f1))
    r2 = 1.0 / (EPS + (13.0 / 12.0 * e2 * e2 + 0.25 * f2 * f2))
    w0, w1, w2 = 0.1 * r0 * r0, 0.6 * r1 * r1, 0.3 * r2 * r2
    inv = 1.0 / (w0 + w1 + w2)
    w0, w1, w2 = w0 * inv, w1 * inv, w2 * inv
    v0 = (2.0 * a - 7.0 * b + 11.0 * m) * (1.0 / 6.0)
    v1 = (5.0 * m - b + 2.0 * p) * (1.0 / 6.0)
    v2 = (2.0 * m + 5.0 * p - q) * (1.0 / 6.0)
    value = w0 * v0 + w1 * v1 + w2 * v2
    w0, w1, w2 = w0 * u, w1 * u, w2 * u
    h0 = -2.0 * w0 * r0 * (v0 - value)
    h1 = -2.0 * w1 * r1 * (v1 - value)
    h2 = -2.0 * w2 * r2 * (v2 - value)
    e0, f0 = h0 * e0 * (13.0 / 6.0), h0 * f0 * 0.5
    e1, f1 = h1 * e1 * (13.0 / 6.0), h1 * f1 * 0.5
    e2, f2 = h2 * e2 * (13.0 / 6.0), h2 * f2 * 0.5
    w0, w1, w2 = w0 * (1.0 / 6.0), w1 * (1.0 / 6.0), w2 * (1.0 / 6.0)
    ga = 2.0 * w0 + e0 + f0
    gb = -7.0 * w0 - w1 - 2.0 * e0 - 4.0 * f0 + e1 + f1
    gm = 11.0 * w0 + 5.0 * w1 + 2.0 * w2 + e0 + 3.0 * f0 - 2.0 * e1 + e2 + 3.0 * f2
    gp = 2.0 * w1 + 5.0 * w2 + e1 - f1 - 2.0 * e2 - 4.0 * f2
    gq = e2 + f2 - w2
    zero = jnp.zeros_like(ga)
    return value, (
        jnp.where(pos, ga, zero),
        jnp.where(pos, gb, gq),
        jnp.where(pos, gm, gp),
        jnp.where(pos, gp, gm),
        jnp.where(pos, gq, gb),
        jnp.where(pos, zero, ga),
    )


def spread(f):
    return roll(f, 1) + roll(f, -1) + roll(f, 64) + roll(f, -64) - 4.0 * f


def kernel(
    ns, nt, nz,
    fu_h, fv_h, fw_h, fc_h, iu_h, iv_h, iw_h, it_h, dinv, vecs, minv, eig, ring, ring_t, yfwd, yinv, spec_h, lamy,
    out_u, out_v, out_w, out_c,
    raw, spec, u10, v14, w10, c18, iu10, iv10, iw14, it14, modal,
    xe, xw, xfw, xfe, yn1, ys1, yfs1, yfn1, yn2, ys2, yfs2, yfn2,
    s1, r1, s2, r2, s3, r3, s4, r4,
    ax, wx, ay, wy, ch, d_buf, p_buf, mw_buf, ou, ov, ow, oc,
    in_sem, h_send, h_recv, p_send, p_recv,
):
    ng = nz // 2
    s, t = lax.axis_index("ys"), lax.axis_index("xs")
    owner = t < ng

    loads = []
    for n, src in enumerate((iu_h, iv_h, iw_h, it_h, fc_h, fu_h, fv_h, fw_h)):
        loads.append(pltpu.make_async_copy(src, raw.at[n], in_sem.at[n]))
    loads.append(pltpu.make_async_copy(spec_h.at[s], spec, in_sem.at[8]))
    for copy in loads:
        copy.start()

    barrier = pltpu.get_barrier_semaphore()

    def greet_x(i, _):
        pl.semaphore_signal(barrier, 1, device_id=(s, lax.rem(t + i, nt)), device_id_type=MESH)
        return 0

    def greet_y(i, _):
        pl.semaphore_signal(barrier, 1, device_id=(lax.rem(s + i, ns), t), device_id_type=MESH)
        return 0

    lax.fori_loop(1, nt, greet_x, 0)
    lax.fori_loop(1, ns, greet_y, 0)

    lane = lax.broadcasted_iota(jnp.int32, (nz, 128), 1)
    slot = lane & 63
    low = lane < 64
    core = (slot >= 8) & (slot < 40)
    lane_g = lax.broadcasted_iota(jnp.int32, (ng, 128), 1)
    level = lax.broadcasted_iota(jnp.int32, (nz, 640), 0)

    def rows(n, count):
        return pl.ds(pl.multiple_of(n * count, count), count)

    def tile(n):
        return slice(128 * n, 128 * n + 128)

    def place(n, buf, first):
        loads[n].wait()
        for r in range(ROWS):
            at = 128 * first + 64 * (r + 1) + 8
            buf[:, at : at + COLS] = raw[n, pl.ds(r, nz, stride=ROWS), :]

    def pack_x(fields, out):
        total = jnp.zeros((nz, 128), F32)
        for buf, first, col, at, count in fields:
            for k in range(4):
                if k == 0:
                    v = jnp.where(low, buf[:, tile(first + 4)], buf[:, tile(first)])
                else:
                    v = buf[:, tile(first + k)]
                to = 16 * k + at
                total = jnp.where((slot >= to) & (slot < to + count), roll(v, to - 8 - col), total)
        out[...] = total

    def unpack_x(src, fields):
        v = src[...]
        for buf, first, col, at, count in fields:
            here = (slot >= 8 + col) & (slot < 8 + col + count)
            for k in range(4):
                w = roll(v, 8 + col - 16 * k - at)
                if k == 0:
                    z = tile(first + 4)
                    buf[:, z] = jnp.where(here & low, w, buf[:, z])
                    z = tile(first)
                    buf[:, z] = jnp.where(here & ~low, w, buf[:, z])
                else:
                    z = tile(first + k)
                    buf[:, z] = jnp.where(here, w, buf[:, z])

    def pair(one, two):
        return jnp.where(core, one, roll(two, 32))

    def remote(src, dst, ds, dt, send, recv):
        return pltpu.make_async_remote_copy(
            src_ref=src, dst_ref=dst, send_sem=send, recv_sem=recv, device_id=(ds, dt), device_id_type=MESH
        )

    east, west = lax.rem(t + 1, nt), lax.rem(t + nt - 1, nt)
    north, south = lax.rem(s + 1, ns), lax.rem(s + ns - 1, ns)

    place(0, iu10, 0)
    place(1, iv10, 0)
    pack_x(((iu10, 0, 31, 6, 1), (iv10, 0, 31, 7, 1)), xe.at[0])
    pack_x(((iu10, 0, 0, 6, 1), (iv10, 0, 0, 7, 1)), xw.at[0])
    yn1[...] = pair(iu10[:, tile(4)], iv10[:, tile(4)])
    ys1[...] = pair(iu10[:, tile(0)], iv10[:, tile(0)])

    pl.semaphore_wait(barrier, nt - 1 + ns - 1)
    first_halo = [
        remote(xe.at[0], xfw.at[0], s, east, h_send.at[0], h_recv.at[0]),
        remote(yn1, yfs1, north, t, h_send.at[1], h_recv.at[1]),
        remote(xw.at[0], xfe.at[0], s, west, h_send.at[2], h_recv.at[2]),
        remote(ys1, yfn1, south, t, h_send.at[3], h_recv.at[3]),
    ]
    for copy in first_halo:
        copy.start()

    place(2, iw14, 1)
    place(3, it14, 1)
    place(4, c18, 2)
    place(5, u10, 0)
    place(6, v14, 1)
    place(7, w10, 0)

    pack_x(((iw14, 1, 29, 0, 3), (it14, 1, 29, 3, 3), (u10, 0, 29, 8, 3), (c18, 2, 27, 11, 5)), xe.at[1])
    pack_x(((iw14, 1, 0, 0, 3), (it14, 1, 0, 3, 3), (u10, 0, 0, 8, 2), (c18, 2, 0, 11, 5)), xw.at[1])
    for n in range(3):
        yn2[n] = pair(c18[:, tile(4 + n)], v14[:, tile(3 + n)])
        ys2[n] = pair(c18[:, tile(2 + n)], v14[:, tile(1 + n)])
    for n in range(2):
        yn2[3 + n] = pair(iw14[:, tile(4 + n)], it14[:, tile(4 + n)])
        ys2[3 + n] = pair(iw14[:, tile(1 + n)], it14[:, tile(1 + n)])

    first_halo[0].wait_recv()
    unpack_x(xfw.at[0], ((iu10, 0, -1, 6, 1), (iv10, 0, -1, 7, 1)))
    first_halo[1].wait_recv()
    v = yfs1[...]
    iu10[:, tile(0)] = jnp.where(low, v, iu10[:, tile(0)])
    iv10[:, tile(0)] = jnp.where(low, roll(v, -32), iv10[:, tile(0)])

    iu, iv, iw = iu10[...], iv10[...], iw14[:, 128:768]
    below = jnp.where(level == 0, 0.0, roll(iw, 1, 0))
    div = iu - roll(iu, 1) + (iv - roll(iv, 64)) + (iw - below)
    div = roll(div, -64)[:, :512]
    div = dot_tn(vecs[...], div)
    half = (lane_g & 63) < 32
    for i in range(4):
        modal[i] = div[:, tile(i)]
        even = modal[i, pl.ds(0, ng, stride=2), :]
        odd = modal[i, pl.ds(1, ng, stride=2), :]
        s1[:, i, :] = jnp.where(half, roll(even, -8), roll(odd, 24))

    def send1(i, _):
        g = lax.rem(t + i, ng)

        @pl.when(g != t)
        def _():
            remote(s1.at[g], r1.at[t], s, g, p_send.at[0], p_recv.at[0]).start()

        return 0

    lax.fori_loop(0, ng, send1, 0)

    @pl.when(owner)
    def _():
        pltpu.make_async_copy(s1.at[t], r1.at[t], p_recv.at[0]).start()

    second_halo = [
        remote(xe.at[1], xfw.at[1], s, east, h_send.at[4], h_recv.at[4]),
        remote(yn2, yfs2, north, t, h_send.at[5], h_recv.at[5]),
        remote(xw.at[1], xfe.at[1], s, west, h_send.at[6], h_recv.at[6]),
        remote(ys2, yfn2, south, t, h_send.at[7], h_recv.at[7]),
    ]
    for copy in second_halo:
        copy.start()

    @pl.when(owner)
    def _():
        pltpu.make_async_copy(r1, r1, p_recv.at[0]).wait()
        x = jnp.concatenate([r1[:, i, :] for i in range(4)], 1)
        y = dot(ring[...], x)
        for q in range(2):
            for i in range(4):
                s2[pl.ds(4 * q + i, ns, stride=8), :] = y[q * ns : (q + 1) * ns, tile(i)]

        def send2(i, _):
            j = lax.rem(s + i, ns)
            remote(s2.at[rows(j, 8)], r2.at[rows(s, 8)], j, t, p_send.at[1], p_recv.at[1]).start()
            return 0

        lax.fori_loop(1, ns, send2, 0)
        pltpu.make_async_copy(s2.at[rows(s, 8)], r2.at[rows(s, 8)], p_recv.at[1]).start()

    first_halo[2].wait_recv()
    unpack_x(xfe.at[0], ((iu10, 0, 32, 6, 1), (iv10, 0, 32, 7, 1)))
    first_halo[3].wait_recv()
    v = yfn1[...]
    iu10[:, tile(4)] = jnp.where(low, iu10[:, tile(4)], v)
    iv10[:, tile(4)] = jnp.where(low, iv10[:, tile(4)], roll(v, -32))
    second_halo[0].wait_recv()
    unpack_x(xfw.at[1], ((iw14, 1, -3, 0, 3), (it14, 1, -3, 3, 3), (u10, 0, -3, 8, 3), (c18, 2, -5, 11, 5)))
    second_halo[2].wait_recv()
    unpack_x(xfe.at[1], ((iw14, 1, 32, 0, 3), (it14, 1, 32, 3, 3), (u10, 0, 32, 8, 2), (c18, 2, 32, 11, 5)))

    def x_faces(n, _):
        at = pl.ds(pl.multiple_of(8 * n, 8), 8)
        value, parts = weno_parts(c18[at, 256:896], u10[at, :], 1, lambda f: f)
        wx[at, :] = value
        for o in range(6):
            ax[o, at, :] = parts[o]
        return 0

    lax.fori_loop(0, nz // 8, x_faces, 0)

    @pl.when(owner)
    def _():
        loads[8].wait()
        pltpu.make_async_copy(r2, r2, p_recv.at[1]).wait()
        part = [
            jnp.concatenate([r2[pl.ds(4 * q + i, ns, stride=8), :] for i in range(4)], 0) for q in range(2)
        ]
        left = lax.broadcasted_iota(jnp.int32, (4 * ns, 128), 1) < 64
        x = jnp.concatenate(
            [
                jnp.where(left, part[0], roll(part[1], 64)),
                jnp.where(left, roll(part[0], 64), part[1]),
            ],
            0,
        )
        inner = spec[0:128, :]
        y = dot(dot(yfwd[...], x), inner)
        wide = lax.broadcasted_iota(jnp.int32, (1, 128), 1)
        own = jnp.where((wide & 32) == 0, eig[2 * t], eig[2 * t + 1])
        y = -y / (own + lamy[...] + spec[128:129, :])
        y = dot(yinv[...], dot_nt(y, inner))
        s3[...] = y

        def send3(i, _):
            j = lax.rem(s + i, ns)
            remote(s3.at[rows(j, 16)], r3.at[rows(s, 16)], j, t, p_send.at[2], p_recv.at[2]).start()
            return 0

        lax.fori_loop(1, ns, send3, 0)
        pltpu.make_async_copy(s3.at[rows(s, 16)], r3.at[rows(s, 16)], p_recv.at[2]).start()

    second_halo[1].wait_recv()
    second_halo[3].wait_recv()
    for n in range(3):
        v = yfs2[n]
        for buf, k, f in ((c18, n, v), (v14, n - 1, roll(v, -32))):
            if k >= 0:
                buf[:, tile(k)] = f if n < 2 else jnp.where(low, f, buf[:, tile(k)])
        v = yfn2[n]
        for buf, k, f in ((c18, 6 + n, v), (v14, 5 + n, roll(v, -32))):
            if k < buf.shape[1] // 128:
                buf[:, tile(k)] = f if n > 0 else jnp.where(low, buf[:, tile(k)], f)
    for n in range(2):
        v = yfs2[3 + n]
        for buf, f in ((iw14, v), (it14, roll(v, -32))):
            buf[:, tile(n)] = f if n < 1 else jnp.where(low, f, buf[:, tile(n)])
        v = yfn2[3 + n]
        for buf, f in ((iw14, v), (it14, roll(v, -32))):
            buf[:, tile(5 + n)] = f if n > 0 else jnp.where(low, buf[:, tile(5 + n)], f)

    def y_faces(n, _):
        at = pl.ds(pl.multiple_of(8 * n, 8), 8)
        value, parts = weno_parts(c18[at, :], v14[at, :], 64, lambda f: f[:, 128:1024])
        wy[at, :] = value
        for o in range(6):
            ay[o, at, :] = parts[o]
        return 0

    lax.fori_loop(0, nz // 8, y_faces, 0)

    @pl.when(owner)
    def _():
        pltpu.make_async_copy(r3, r3, p_recv.at[2]).wait()
        left = lax.broadcasted_iota(jnp.int32, (ns, 128), 1) < 64
        cols = []
        for i in range(7):
            one = r3[pl.ds(2 * i, ns, stride=16), :]
            two = r3[pl.ds(2 * i + 1, ns, stride=16), :]
            cols.append(
                jnp.concatenate(
                    [
                        jnp.where(left, one, roll(two, 64)),
                        jnp.where(left, roll(one, 64), two),
                    ],
                    0,
                )
            )
        y = dot(ring_t[...], jnp.concatenate(cols, 1))
        at = lax.broadcasted_iota(jnp.int32, (nt, 128), 1) & 31
        edge = jnp.zeros((nt, 128), F32)
        before, after = roll(y, 1, 0), roll(y, -1, 0)
        for i in range(7):
            s4[pl.ds(i, nt, stride=8), :] = y[:, tile(i)]
            if 1 <= i <= 5:
                k = 3 * (i - 1)
                edge = jnp.where((at >= k) & (at < k + 3), roll(before[:, tile(i)], k - 29), edge)
                edge = jnp.where((at >= 16 + k) & (at < 19 + k), roll(after[:, tile(i)], 16 + k), edge)
        s4[pl.ds(7, nt, stride=8), :] = edge

        def send4(i, _):
            g = lax.rem(t + i, nt)
            remote(s4.at[rows(g, 8)], r4.at[rows(t, 8)], s, g, p_send.at[3], p_recv.at[3]).start()
            return 0

        lax.fori_loop(1, nt, send4, 0)
        pltpu.make_async_copy(s4.at[rows(t, 8)], r4.at[rows(t, 8)], p_recv.at[3]).start()

    c10, w = c18[:, 256:896], w10[...]
    ch[0] = jnp.where(level == nz - 1, 0.0, 0.5 * (c10 + roll(c10, -1, 0)))
    ch[1] = jnp.where(level == nz - 1, 0.0, 0.5 * w)

    pltpu.make_async_copy(r4, r4, p_recv.at[3]).wait()
    cols = []
    for i in range(8):
        one = r4[pl.ds(i, ng, stride=8), :]
        modal[i, pl.ds(0, ng, stride=2), :] = roll(one, 8)
        modal[i, pl.ds(1, ng, stride=2), :] = roll(one, -24)
        cols.append(modal[i])
    p = dot_tn(minv[...], jnp.concatenate(cols, 1))
    edge = p[:, tile(7)]
    for i in range(7):
        v = p[:, tile(i)]
        if 1 <= i <= 5:
            k = 3 * (i - 1)
            v = jnp.where((slot >= 5) & (slot < 8), roll(edge, -3 - k), v)
            v = jnp.where((slot >= 40) & (slot < 43), roll(edge, 16 - k), v)
        p_buf[:, tile(i)] = v
    p = p_buf[...]
    upper = jnp.where(lax.broadcasted_iota(jnp.int32, p.shape, 0) == nz - 1, 0.0, roll(p, -1, 0))
    mid = iw14[...] - (upper - p)
    mw_buf[...] = mid[:, 128:768]
    d = dot_tn(dinv[...], it14[...] + GRAV * DT * mid)
    d_buf[...] = d
    d10 = d[:, 128:768]
    gz = roll(d10, -1, 0) - d10
    wz = ch[1] * gz
    oc[...] = d10 + DT * (wz + roll(wz, 1, 0))
    mw = mw_buf[...]
    ow[...] = mw + DT * NU * spread(mw) + DT * (ch[0] * gz)

    def last(n, _):
        at = pl.ds(pl.multiple_of(8 * n, 8), 8)
        p14, d14 = p_buf[at, :], d_buf[at, :]
        p10, dx = p14[:, 128:768], d14[:, 128:768]
        mu = iu10[at, :] - (roll(p10, -1) - p10)
        mv = iv10[at, :] - (roll(p14, -64)[:, 128:768] - p10)
        gx = roll(dx, -1) - dx
        gy = roll(d14, -64) - d14
        total = KAPPA * spread(dx)
        ty = jnp.zeros_like(d14)
        for o in range(6):
            total = total + roll(ax[o, at, :] * gx, o - 2)
            ty = ty + roll(ay[o, at, :] * gy, 64 * (o - 2))
        ou[at, :] = mu + DT * NU * spread(mu) + DT * (wx[at, :] * gx)
        ov[at, :] = mv + DT * NU * spread(mv) + DT * (wy[at, :] * gy)[:, 128:768]
        oc[at, :] = oc[at, :] + DT * (total + ty[:, 128:768])
        return 0

    lax.fori_loop(0, nz // 8, last, 0)

    for src, dst in ((ou, out_u), (ov, out_v), (ow, out_w), (oc, out_c)):
        for r in range(ROWS):
            v = roll(src[:, tile((r + 1) // 2)], -8 - 64 * ((r + 1) % 2))
            dst[pl.ds(r, nz, stride=ROWS), :] = v[:, :COLS]

    for copy in first_halo + second_halo:
        copy.wait_send()

    @pl.when(owner)
    def _():
        for n, buf, count in ((0, s1, ng - 1), (1, s2, 8 * (ns - 1)), (2, s3, 16 * (ns - 1)), (3, s4, 8 * (nt - 1))):
            part = buf.at[pl.ds(0, count)]
            pltpu.make_async_copy(part, part, p_send.at[n]).wait()

    @pl.when(t >= ng)
    def _():
        pltpu.make_async_copy(s1, s1, p_send.at[0]).wait()
        loads[8].wait()


def call(ns, nt, nz, consts, *args):
    ng = nz // 2
    vmem, anywhere = pl.BlockSpec(memory_space=pltpu.VMEM), pl.BlockSpec(memory_space=pl.ANY)
    smem = pl.BlockSpec(memory_space=pltpu.SMEM)

    def buf(*shape):
        return pltpu.VMEM(shape, F32)

    out = jax.ShapeDtypeStruct((nz * ROWS, COLS), F32)
    return pl.pallas_call(
        functools.partial(kernel, ns, nt, nz),
        out_shape=[out] * 4,
        in_specs=[anywhere] * 8 + [vmem] * 3 + [smem] + [vmem] * 4 + [anywhere, vmem],
        out_specs=[vmem] * 4,
        scratch_shapes=[
            buf(8, nz * ROWS, COLS), buf(136, 128),
            buf(nz, 640), buf(nz, 896), buf(nz, 640), buf(nz, 1152),
            buf(nz, 640), buf(nz, 640), buf(nz, 896), buf(nz, 896), buf(8, nz, 128),
            buf(2, nz, 128), buf(2, nz, 128), buf(2, nz, 128), buf(2, nz, 128),
            buf(nz, 128), buf(nz, 128), buf(nz, 128), buf(nz, 128),
            buf(5, nz, 128), buf(5, nz, 128), buf(5, nz, 128), buf(5, nz, 128),
            buf(ng, 4, 128), buf(nt, 4, 128), buf(8 * ns, 128), buf(8 * ns, 128),
            buf(16 * ns, 128), buf(16 * ns, 128), buf(8 * nt, 128), buf(8 * ng, 128),
            buf(6, nz, 640), buf(nz, 640), buf(6, nz, 896), buf(nz, 896), buf(2, nz, 640),
            buf(nz, 896), buf(nz, 896), buf(nz, 640),
            buf(nz, 640), buf(nz, 640), buf(nz, 640), buf(nz, 640),
            pltpu.SemaphoreType.DMA((9,)), pltpu.SemaphoreType.DMA((8,)), pltpu.SemaphoreType.DMA((8,)),
            pltpu.SemaphoreType.DMA((4,)), pltpu.SemaphoreType.DMA((4,)),
        ],
        compiler_params=pltpu.CompilerParams(
            collective_id=0, has_side_effects=True, vmem_limit_bytes=40 * 1024 * 1024
        ),
    )(*args, *consts)


def solution(mesh):
    ns, nt = mesh.shape["ys"], mesh.shape["xs"]
    consts = tables(ns, nt)

    def shards(*args):
        nz = args[0].shape[0]
        flat = [v.reshape(nz * ROWS, COLS) for v in args[:8]]
        out = call(ns, nt, nz, [jnp.asarray(v) for v in consts], *flat, *args[8:])
        return tuple(v.reshape(nz, ROWS, COLS) for v in out)

    block = P(None, "ys", "xs")
    return jax.shard_map(
        shards, mesh=mesh, in_specs=(block,) * 8 + (P(),) * 4, out_specs=(block,) * 4, check_vma=False
    )
```

```python
import functools

import jax
import jax.numpy as jnp
import numpy as np
from jax import lax
from jax.experimental import pallas as pl
from jax.experimental.pallas import tpu as pltpu
from jax.sharding import PartitionSpec as P

MESH = pl.DeviceIdType.MESH
DT = 0.25
NU = 0.1
KAPPA = 0.1
GRAV = 1.0
EPS = 1e-6
F32 = jnp.float32
HI = lax.Precision.HIGHEST
ROWS, COLS = 8, 32


def tables(ns, nt):
    nx, ny = COLS * nt, ROWS * ns
    t = np.arange(nt)
    ring = np.zeros((2, ns, nt))
    ring[0, 0] = 1 / np.sqrt(nt)
    ring[1, 0] = (-1.0) ** t / np.sqrt(nt)
    for j in range(1, ns):
        ring[0, j] = np.sqrt(2 / nt) * np.cos(2 * np.pi * j * t / nt)
        ring[1, j] = np.sqrt(2 / nt) * np.sin(2 * np.pi * j * t / nt)

    def basis(n, k):
        z = np.arange(n)
        if k == 0 or 2 * k == n:
            return [np.cos(2 * np.pi * k * z / n) / np.sqrt(n)]
        return [
            np.sqrt(2 / n) * np.cos(2 * np.pi * k * z / n),
            np.sqrt(2 / n) * np.sin(2 * np.pi * k * z / n),
        ]

    inner = np.zeros((ns, 2, 2, COLS, 2, 2, COLS))
    lamx = np.zeros((ns, 2, 2, COLS))
    for j in range(ns):
        found, lam = [], []
        for k in range(nx // 2 + 1):
            res = k % nt
            own = res in (0, nt // 2) if j == 0 else res in (j, nt - j)
            if own:
                for vec in basis(nx, k):
                    found.append(np.einsum("qt,tc->qc", ring[:, j], vec.reshape(nt, COLS)))
                    lam.append(4 * np.sin(np.pi * k / nx) ** 2)
        block = np.stack(found, -1).reshape(2, COLS, 2, COLS)
        for m in range(2):
            inner[j, :, m, :, :, m, :] = block
            lamx[j, :, m, :] = np.array(lam).reshape(2, COLS)
    inner = inner.reshape(ns, 4 * COLS, 4 * COLS)
    lamx = np.broadcast_to(lamx.reshape(ns, 1, 4 * COLS), (ns, 8, 4 * COLS))
    spectral = np.concatenate([inner, lamx], 1)

    ybase, ylam = [], []
    for k in range(ny // 2 + 1):
        for vec in basis(ny, k):
            ybase.append(vec)
            ylam.append(4 * np.sin(np.pi * k / ny) ** 2)
    ybase = np.stack(ybase)
    lamy = np.broadcast_to(np.array(ylam)[:, None], (ny, 128))
    yfwd = ybase.reshape(ny, ns, 2, 4).transpose(0, 3, 2, 1).reshape(ny, ny)
    yinv = np.zeros((ns, 16, ny))
    for s in range(ns):
        for r in range(14):
            yinv[s, r] = ybase[:, (ROWS * s - 3 + r) % ny]
    after = ybase[:, (ROWS * np.arange(ns) + ROWS) % ny]
    ring = ring.reshape(nt, nt)
    parts = (lamy, yinv.reshape(16 * ns, ny), yfwd, after, ring, np.roll(ring, -1, 1), ring.T)
    packed = np.zeros((sum(len(v) for v in parts), 128))
    at, places = 0, []
    for v in parts:
        packed[at : at + len(v), : v.shape[1]] = v
        places.append((at, at + len(v), v.shape[1]))
        at += len(v)
    return packed.astype(np.float32), np.ascontiguousarray(spectral).astype(np.float32), tuple(places)


def owners(nt, ng):
    if (nt, ng) != (32, 24):
        return (lambda n: n), (lambda t: t), (lambda t: t < ng)

    def index_of(n):
        h = n // 2
        late = h // 8
        y = h - 8 * late
        y = y + late * 4 * (y // 2)
        return 4 * y + 2 * late + n % 2

    def pair_of(t):
        y, late = t // 4, (t // 2) % 2
        return 2 * (y - late * 4 * (y // 4)) + 16 * late + t % 2

    def has(t):
        y, late = t // 4, (t // 2) % 2
        return (late == 0) | ((y + 2) % 8 < 4)

    return index_of, pair_of, has


def dot(a, b):
    return lax.dot_general(a, b, (((1,), (0,)), ((), ())), precision=HI, preferred_element_type=F32)


def dot_tn(a, b):
    return lax.dot_general(a, b, (((0,), (0,)), ((), ())), precision=HI, preferred_element_type=F32)


def dot_nt(a, b):
    return lax.dot_general(a, b, (((1,), (1,)), ((), ())), precision=HI, preferred_element_type=F32)


def roll(v, shift, axis=1):
    shift = shift % v.shape[axis]
    return v if shift == 0 else pltpu.roll(v, shift, axis)


def weno_parts(c, u, step, cut):
    stencil = [cut(roll(c, -k * step)) for k in range(-2, 4)]
    pos = u >= 0.0
    a = jnp.where(pos, stencil[0], stencil[5])
    b = jnp.where(pos, stencil[1], stencil[4])
    m = jnp.where(pos, stencil[2], stencil[3])
    p = jnp.where(pos, stencil[3], stencil[2])
    q = jnp.where(pos, stencil[4], stencil[1])
    e0, f0 = a - 2.0 * b + m, a - 4.0 * b + 3.0 * m
    e1, f1 = b - 2.0 * m + p, b - p
    e2, f2 = m - 2.0 * p + q, 3.0 * m - 4.0 * p + q
    r0 = 1.0 / (EPS + (13.0 / 12.0 * e0 * e0 + 0.25 * f0 * f0))
    r1 = 1.0 / (EPS + (13.0 / 12.0 * e1 * e1 + 0.25 * f1 * f1))
    r2 = 1.0 / (EPS + (13.0 / 12.0 * e2 * e2 + 0.25 * f2 * f2))
    w0, w1, w2 = 0.1 * r0 * r0, 0.6 * r1 * r1, 0.3 * r2 * r2
    inv = 1.0 / (w0 + w1 + w2)
    w0, w1, w2 = w0 * inv, w1 * inv, w2 * inv
    v0 = (2.0 * a - 7.0 * b + 11.0 * m) * (1.0 / 6.0)
    v1 = (5.0 * m - b + 2.0 * p) * (1.0 / 6.0)
    v2 = (2.0 * m + 5.0 * p - q) * (1.0 / 6.0)
    value = w0 * v0 + w1 * v1 + w2 * v2
    w0, w1, w2 = w0 * u, w1 * u, w2 * u
    h0 = -2.0 * w0 * r0 * (v0 - value)
    h1 = -2.0 * w1 * r1 * (v1 - value)
    h2 = -2.0 * w2 * r2 * (v2 - value)
    e0, f0 = h0 * e0 * (13.0 / 6.0), h0 * f0 * 0.5
    e1, f1 = h1 * e1 * (13.0 / 6.0), h1 * f1 * 0.5
    e2, f2 = h2 * e2 * (13.0 / 6.0), h2 * f2 * 0.5
    w0, w1, w2 = w0 * (1.0 / 6.0), w1 * (1.0 / 6.0), w2 * (1.0 / 6.0)
    ga = 2.0 * w0 + e0 + f0
    gb = -7.0 * w0 - w1 - 2.0 * e0 - 4.0 * f0 + e1 + f1
    gm = 11.0 * w0 + 5.0 * w1 + 2.0 * w2 + e0 + 3.0 * f0 - 2.0 * e1 + e2 + 3.0 * f2
    gp = 2.0 * w1 + 5.0 * w2 + e1 - f1 - 2.0 * e2 - 4.0 * f2
    gq = e2 + f2 - w2
    zero = jnp.zeros_like(ga)
    return value, (
        jnp.where(pos, ga, zero),
        jnp.where(pos, gb, gq),
        jnp.where(pos, gm, gp),
        jnp.where(pos, gp, gm),
        jnp.where(pos, gq, gb),
        jnp.where(pos, zero, ga),
    )


def spread(f):
    return roll(f, 1) + roll(f, -1) + roll(f, 64) + roll(f, -64) - 4.0 * f


def kernel(
    ns, nt, nz, places,
    fu_h, fv_h, fw_h, fc_h, iu_h, iv_h, iw_h, it_h, dinv_h, vecs_h, minv_h, eig, packed_h, spec_h,
    out_u, out_v, out_w, out_c,
    raw, mats, packed, spec, rhs, u10, v14, w10, c18, iu10, iv10, iw14, it14, modal,
    xe, xw, xfw, xfe, yn2, ys2, yfs2, yfn2,
    s1, r1, s2, r2, s3, r3, s4, r4,
    ax, wx, ay, wy, ch, d_buf, p_buf, mw_buf, ou, ov, ow, oc,
    in_sem, h_send, h_recv, p_send, p_recv, ready,
):
    ng = nz // 2
    s, t = lax.axis_index("ys"), lax.axis_index("xs")
    index_of, pair_of, has = owners(nt, ng)
    owner = has(t)
    other = jnp.logical_not(owner)
    mine = pair_of(t)
    late = nt - ng

    barrier = pltpu.get_barrier_semaphore()

    def greet(a, b):
        pl.semaphore_signal(barrier, 1, device_id=(a, b), device_id_type=MESH)

    def greet_x(i, _):
        greet(s, lax.rem(t + i, nt))
        return 0

    def greet_y(i, _):
        greet(lax.rem(s + i, ns), t)
        return 0

    east, west = lax.rem(t + 1, nt), lax.rem(t + nt - 1, nt)
    north, south = lax.rem(s + 1, ns), lax.rem(s + ns - 1, ns)
    twin = t + 1 - 2 * lax.rem(t, 2)

    @pl.when(owner)
    def _():
        lax.fori_loop(1, nt, greet_x, 0)
        lax.fori_loop(1, ns, greet_y, 0)

    if late:

        @pl.when(other)
        def _():
            greet(north, t)
            greet(south, t)
            greet(s, twin)

    loads = []
    for n, src in enumerate((iu_h, iv_h, iw_h, it_h, fc_h, fu_h, fv_h, fw_h)):
        dst = raw.at[n, pl.ds(1, ROWS), pl.ds(8, COLS)]
        loads.append(pltpu.make_async_copy(src, dst, in_sem.at[n]))
    loads.append(pltpu.make_async_copy(spec_h.at[s], spec, in_sem.at[8]))
    loads.append(pltpu.make_async_copy(packed_h, packed, in_sem.at[9]))
    for n, src in enumerate((vecs_h, minv_h, dinv_h)):
        loads.append(pltpu.make_async_copy(src, mats.at[n], in_sem.at[10 + n]))
    order = (0, 1, 2, 10, 9, 8, 3, 4, 5, 6, 7, 11, 12)
    for n in order:
        loads[n].start()

    lane = lax.broadcasted_iota(jnp.int32, (nz, 128), 1)
    slot = lane & 63
    low = lane < 64
    core = (slot >= 8) & (slot < 40)
    lane_g = lax.broadcasted_iota(jnp.int32, (ng, 128), 1)
    level = lax.broadcasted_iota(jnp.int32, (nz, 640), 0)

    def rows(n, count):
        return pl.ds(pl.multiple_of(n * count, count), count)

    def tile(n):
        return slice(128 * n, 128 * n + 128)

    def table(n):
        first, end, width = places[n]
        return packed[first:end, :width]

    def place(n, buf, first):
        for k in range(5):
            v = raw[n, 2 * k : 2 * k + 2].reshape(128, nz)
            buf[:, tile(first + k)] = v.T

    def pack_x(fields, out):
        total = jnp.zeros((nz, 128), F32)
        for buf, first, col, at, count in fields:
            for k in range(4):
                if k == 0:
                    v = jnp.where(low, buf[:, tile(first + 4)], buf[:, tile(first)])
                else:
                    v = buf[:, tile(first + k)]
                to = 16 * k + at
                total = jnp.where((slot >= to) & (slot < to + count), roll(v, to - 8 - col), total)
        out[...] = total

    def unpack_x(src, fields):
        v = src[...]
        for buf, first, col, at, count in fields:
            here = (slot >= 8 + col) & (slot < 8 + col + count)
            for k in range(4):
                w = roll(v, 8 + col - 16 * k - at)
                if k == 0:
                    z = tile(first + 4)
                    buf[:, z] = jnp.where(here & low, w, buf[:, z])
                    z = tile(first)
                    buf[:, z] = jnp.where(here & ~low, w, buf[:, z])
                else:
                    z = tile(first + k)
                    buf[:, z] = jnp.where(here, w, buf[:, z])

    def pair(one, two):
        return jnp.where(core, one, roll(two, 32))

    def remote(src, dst, ds, dt, send, recv):
        return pltpu.make_async_remote_copy(
            src_ref=src, dst_ref=dst, send_sem=send, recv_sem=recv, device_id=(ds, dt), device_id_type=MESH
        )

    loads[0].wait()
    loads[1].wait()
    loads[2].wait()
    iu = raw[0, 1:9, 8:40].reshape(ROWS * COLS, nz)
    iv = raw[1, 1:9, 8:40].reshape(ROWS * COLS, nz)
    iw = raw[2, 1:9, 8:40].reshape(ROWS * COLS, nz)
    first_col = lax.broadcasted_iota(jnp.int32, iu.shape, 0) % COLS == 0
    before = jnp.where(first_col, 0.0, roll(iu, 1, 0))
    behind = jnp.concatenate([jnp.zeros((COLS, nz), F32), iv[: 7 * COLS]], 0)
    rhs[0:256, :] = (iu - before) + (iv - behind)
    rhs[256:288, :] = -iv[7 * COLS :]
    rhs[288:416, :] = jnp.zeros((128, nz), F32)
    for r in range(ROWS):
        at = 288 + 32 * (r % 4) + r // 4
        rhs[at : at + 1, :] = -raw[0, r + 1, 39:40, :]
    loads[10].wait()
    vt = mats[0].T
    next_vt = jnp.concatenate([vt[:, 1:], jnp.zeros((nz, 1), F32)], 1)
    main = dot_nt(vt, rhs[0:256, :]) + dot_nt(vt - next_vt, iw)
    extra = dot_nt(vt, rhs[256:416, :])
    modal[0] = main[:, :128]
    modal[1] = main[:, 128:]
    modal[2] = jnp.concatenate([extra[:, :32], jnp.zeros((nz, 96), F32)], 1)
    modal[3] = extra[:, 32:]
    for i in range(4):
        even = modal[i, pl.ds(0, ng, stride=2), :]
        odd = modal[i, pl.ds(1, ng, stride=2), :]
        if i < 2:
            s1[pl.ds(i, ng, stride=8), :] = even
            s1[pl.ds(2 + i, ng, stride=8), :] = odd
        elif i == 2:
            s1[pl.ds(4, ng, stride=8), :] = jnp.where(lane_g < 32, even, roll(odd, 32))
        else:
            s1[pl.ds(5, ng, stride=8), :] = jnp.where((lane_g & 31) < 2, even, roll(odd, 2))
            s1[pl.ds(6, ng, stride=8), :] = jnp.zeros((ng, 128), F32)
            s1[pl.ds(7, ng, stride=8), :] = jnp.zeros((ng, 128), F32)

    @pl.when(owner)
    def _():
        pl.semaphore_wait(barrier, ng - 1 + ns - 1)

    if late:

        @pl.when(other)
        def _():
            pl.semaphore_wait(barrier, ng + 3)

    def send1(i, _):
        g = lax.rem(t + i, ng)
        to = index_of(g)

        @pl.when(to != t)
        def _():
            remote(s1.at[rows(g, 8)], r1.at[rows(t, 8)], s, to, p_send.at[0], p_recv.at[0]).start()

        return 0

    lax.fori_loop(0, ng, send1, 0)

    @pl.when(owner)
    def _():
        pltpu.make_async_copy(s1.at[rows(mine, 8)], r1.at[rows(t, 8)], p_recv.at[0]).start()

    if late:

        @pl.when(other)
        def _():
            def report(i, _):
                g = index_of(i)
                pl.semaphore_signal(ready, 1, device_id=(s, g), device_id_type=MESH)
                return 0

            lax.fori_loop(0, ng, report, 0)

    for n, buf, first in ((3, it14, 1), (4, c18, 2), (5, u10, 0), (6, v14, 1), (7, w10, 0)):
        loads[n].wait()
        place(n, buf, first)
    place(0, iu10, 0)
    place(1, iv10, 0)
    place(2, iw14, 1)

    pack_x(((iw14, 1, 29, 0, 3), (it14, 1, 29, 3, 3), (iu10, 0, 31, 6, 1), (iv10, 0, 31, 7, 1), (u10, 0, 29, 8, 3), (c18, 2, 27, 11, 5)), xe)
    pack_x(((iw14, 1, 0, 0, 3), (it14, 1, 0, 3, 3), (iu10, 0, 0, 6, 1), (iv10, 0, 0, 7, 1), (u10, 0, 0, 8, 2), (c18, 2, 0, 11, 5)), xw)
    for n in range(3):
        yn2[n] = pair(c18[:, tile(4 + n)], v14[:, tile(3 + n)])
        ys2[n] = pair(c18[:, tile(2 + n)], v14[:, tile(1 + n)])
    for n in range(2):
        yn2[3 + n] = pair(iw14[:, tile(4 + n)], it14[:, tile(4 + n)])
        ys2[3 + n] = pair(iw14[:, tile(1 + n)], it14[:, tile(1 + n)])
    yn2[5] = pair(iu10[:, tile(4)], iv10[:, tile(4)])
    ys2[5] = pair(iu10[:, tile(0)], iv10[:, tile(0)])
    loads[9].wait()

    @pl.when(owner)
    def _():
        pltpu.make_async_copy(r1, r1, p_recv.at[0]).wait()
        x = jnp.concatenate([r1[pl.ds(i, nt, stride=8), :] for i in range(5)], 1)
        y = dot(table(4), x)
        z = dot(table(5), r1[pl.ds(5, nt, stride=8), :])
        first = (lax.broadcasted_iota(jnp.int32, (nt, 128), 1) & 31) == 0
        at = lax.broadcasted_iota(jnp.int32, (ns, 128), 1)
        parts = [y[:, tile(i)] + jnp.where(first, roll(z, -i), 0.0) for i in range(4)]
        for q in range(2):
            for i in range(4):
                s2[pl.ds(4 * q + i, ns, stride=16), :] = parts[i][q * ns : (q + 1) * ns]
        s2[pl.ds(8, ns, stride=16), :] = jnp.where(at < 64, y[:ns, tile(4)], roll(y[ns:, tile(4)], 64))
        for i in range(9, 16):
            s2[pl.ds(i, ns, stride=16), :] = jnp.zeros((ns, 128), F32)

        def send2(i, _):
            j = lax.rem(s + i, ns)
            remote(s2.at[rows(j, 16)], r2.at[rows(s, 16)], j, t, p_send.at[1], p_recv.at[1]).start()
            return 0

        lax.fori_loop(1, ns, send2, 0)
        pltpu.make_async_copy(s2.at[rows(s, 16)], r2.at[rows(s, 16)], p_recv.at[1]).start()

    if late:

        @pl.when(owner)
        def _():
            pl.semaphore_wait(ready, late)

    halos = [
        remote(xe, xfw, s, east, h_send.at[0], h_recv.at[0]),
        remote(yn2, yfs2, north, t, h_send.at[1], h_recv.at[1]),
        remote(xw, xfe, s, west, h_send.at[2], h_recv.at[2]),
        remote(ys2, yfn2, south, t, h_send.at[3], h_recv.at[3]),
    ]
    for copy in halos:
        copy.start()

    @pl.when(owner)
    def _():
        loads[8].wait()
        pltpu.make_async_copy(r2, r2, p_recv.at[1]).wait()
        part = [
            jnp.concatenate([r2[pl.ds(2 * n + i, ns, stride=16), :] for i in range(2)], 0) for n in range(4)
        ]
        group = lax.broadcasted_iota(jnp.int32, (2 * ns, 128), 1) // 32
        x = []
        for r in range(4):
            v = roll(part[0], -32 * r)
            for n in range(1, 4):
                v = jnp.where(group == n, roll(part[n], 32 * (n - r)), v)
            x.append(v)
        x = jnp.concatenate(x, 0)
        y = dot(table(2), x) + dot(table(3), r2[pl.ds(8, ns, stride=16), :])
        inner = spec[0:128, :]
        y = dot(y, inner)
        wide = lax.broadcasted_iota(jnp.int32, (1, 128), 1)
        own = jnp.where((wide & 32) == 0, eig[2 * mine], eig[2 * mine + 1])
        y = -y / (own + table(0) + spec[128:129, :])
        y = dot(table(1), dot_nt(y, inner))
        s3[...] = y

        def send3(i, _):
            j = lax.rem(s + i, ns)
            remote(s3.at[rows(j, 16)], r3.at[rows(s, 16)], j, t, p_send.at[2], p_recv.at[2]).start()
            return 0

        lax.fori_loop(1, ns, send3, 0)
        pltpu.make_async_copy(s3.at[rows(s, 16)], r3.at[rows(s, 16)], p_recv.at[2]).start()

    halos[0].wait_recv()
    unpack_x(xfw, ((iw14, 1, -3, 0, 3), (it14, 1, -3, 3, 3), (iu10, 0, -1, 6, 1), (iv10, 0, -1, 7, 1), (u10, 0, -3, 8, 3), (c18, 2, -5, 11, 5)))
    halos[2].wait_recv()
    unpack_x(xfe, ((iw14, 1, 32, 0, 3), (it14, 1, 32, 3, 3), (iu10, 0, 32, 6, 1), (iv10, 0, 32, 7, 1), (u10, 0, 32, 8, 2), (c18, 2, 32, 11, 5)))

    def x_faces(n, _):
        at = pl.ds(pl.multiple_of(8 * n, 8), 8)
        value, parts = weno_parts(c18[at, 256:896], u10[at, :], 1, lambda f: f)
        wx[at, :] = value
        for o in range(6):
            ax[o, at, :] = parts[o]
        return 0

    lax.fori_loop(0, nz // 8, x_faces, 0)

    halos[1].wait_recv()
    halos[3].wait_recv()
    v = yfs2[5]
    iu10[:, tile(0)] = jnp.where(low, v, iu10[:, tile(0)])
    iv10[:, tile(0)] = jnp.where(low, roll(v, -32), iv10[:, tile(0)])
    v = yfn2[5]
    iu10[:, tile(4)] = jnp.where(low, iu10[:, tile(4)], v)
    iv10[:, tile(4)] = jnp.where(low, iv10[:, tile(4)], roll(v, -32))
    for n in range(3):
        v = yfs2[n]
        for buf, k, f in ((c18, n, v), (v14, n - 1, roll(v, -32))):
            if k >= 0:
                buf[:, tile(k)] = f if n < 2 else jnp.where(low, f, buf[:, tile(k)])
        v = yfn2[n]
        for buf, k, f in ((c18, 6 + n, v), (v14, 5 + n, roll(v, -32))):
            if k < buf.shape[1] // 128:
                buf[:, tile(k)] = f if n > 0 else jnp.where(low, buf[:, tile(k)], f)
    for n in range(2):
        v = yfs2[3 + n]
        for buf, f in ((iw14, v), (it14, roll(v, -32))):
            buf[:, tile(n)] = f if n < 1 else jnp.where(low, f, buf[:, tile(n)])
        v = yfn2[3 + n]
        for buf, f in ((iw14, v), (it14, roll(v, -32))):
            buf[:, tile(5 + n)] = f if n > 0 else jnp.where(low, buf[:, tile(5 + n)], f)

    def y_faces(n, _):
        at = pl.ds(pl.multiple_of(8 * n, 8), 8)
        value, parts = weno_parts(c18[at, :], v14[at, :], 64, lambda f: f[:, 128:1024])
        wy[at, :] = value
        for o in range(6):
            ay[o, at, :] = parts[o]
        return 0

    lax.fori_loop(0, nz // 8, y_faces, 0)

    @pl.when(owner)
    def _():
        pltpu.make_async_copy(r3, r3, p_recv.at[2]).wait()
        left = lax.broadcasted_iota(jnp.int32, (ns, 128), 1) < 64
        cols = []
        for i in range(7):
            one = r3[pl.ds(2 * i, ns, stride=16), :]
            two = r3[pl.ds(2 * i + 1, ns, stride=16), :]
            cols.append(
                jnp.concatenate(
                    [
                        jnp.where(left, one, roll(two, 64)),
                        jnp.where(left, roll(one, 64), two),
                    ],
                    0,
                )
            )
        y = dot(table(6), jnp.concatenate(cols, 1))
        at = lax.broadcasted_iota(jnp.int32, (nt, 128), 1) & 31
        edge = jnp.zeros((nt, 128), F32)
        before, after = roll(y, 1, 0), roll(y, -1, 0)
        for i in range(7):
            s4[pl.ds(i, nt, stride=8), :] = y[:, tile(i)]
            if 1 <= i <= 5:
                k = 3 * (i - 1)
                edge = jnp.where((at >= k) & (at < k + 3), roll(before[:, tile(i)], k - 29), edge)
                edge = jnp.where((at >= 16 + k) & (at < 19 + k), roll(after[:, tile(i)], 16 + k), edge)
        s4[pl.ds(7, nt, stride=8), :] = edge

        def send4(i, _):
            g = lax.rem(t + i, nt)
            remote(s4.at[rows(g, 8)], r4.at[rows(mine, 8)], s, g, p_send.at[3], p_recv.at[3]).start()
            return 0

        lax.fori_loop(1, nt, send4, 0)
        pltpu.make_async_copy(s4.at[rows(t, 8)], r4.at[rows(mine, 8)], p_recv.at[3]).start()

    c10, w = c18[:, 256:896], w10[...]
    ch[0] = jnp.where(level == nz - 1, 0.0, 0.5 * (c10 + roll(c10, -1, 0)))
    ch[1] = jnp.where(level == nz - 1, 0.0, 0.5 * w)

    loads[11].wait()
    loads[12].wait()
    pltpu.make_async_copy(r4, r4, p_recv.at[3]).wait()
    cols = []
    for i in range(8):
        one = r4[pl.ds(i, ng, stride=8), :]
        modal[i, pl.ds(0, ng, stride=2), :] = roll(one, 8)
        modal[i, pl.ds(1, ng, stride=2), :] = roll(one, -24)
        cols.append(modal[i])
    p = dot_tn(mats[1], jnp.concatenate(cols, 1))
    edge = p[:, tile(7)]
    for i in range(7):
        v = p[:, tile(i)]
        if 1 <= i <= 5:
            k = 3 * (i - 1)
            v = jnp.where((slot >= 5) & (slot < 8), roll(edge, -3 - k), v)
            v = jnp.where((slot >= 40) & (slot < 43), roll(edge, 16 - k), v)
        p_buf[:, tile(i)] = v
    p = p_buf[...]
    upper = jnp.where(lax.broadcasted_iota(jnp.int32, p.shape, 0) == nz - 1, 0.0, roll(p, -1, 0))
    mid = iw14[...] - (upper - p)
    mw_buf[...] = mid[:, 128:768]
    d = dot_tn(mats[2], it14[...] + GRAV * DT * mid)
    d_buf[...] = d
    d10 = d[:, 128:768]
    gz = roll(d10, -1, 0) - d10
    wz = ch[1] * gz
    oc[...] = d10 + DT * (wz + roll(wz, 1, 0))
    mw = mw_buf[...]
    ow[...] = mw + DT * NU * spread(mw) + DT * (ch[0] * gz)

    def last(n, _):
        at = pl.ds(pl.multiple_of(8 * n, 8), 8)
        p14, d14 = p_buf[at, :], d_buf[at, :]
        p10, dx = p14[:, 128:768], d14[:, 128:768]
        mu = iu10[at, :] - (roll(p10, -1) - p10)
        mv = iv10[at, :] - (roll(p14, -64)[:, 128:768] - p10)
        gx = roll(dx, -1) - dx
        gy = roll(d14, -64) - d14
        total = KAPPA * spread(dx)
        ty = jnp.zeros_like(d14)
        for o in range(6):
            total = total + roll(ax[o, at, :] * gx, o - 2)
            ty = ty + roll(ay[o, at, :] * gy, 64 * (o - 2))
        ou[at, :] = mu + DT * NU * spread(mu) + DT * (wx[at, :] * gx)
        ov[at, :] = mv + DT * NU * spread(mv) + DT * (wy[at, :] * gy)[:, 128:768]
        oc[at, :] = oc[at, :] + DT * (total + ty[:, 128:768])
        return 0

    lax.fori_loop(0, nz // 8, last, 0)

    for src, dst in ((ou, out_u), (ov, out_v), (ow, out_w), (oc, out_c)):
        for k in range(5):
            v = src[:, tile(k)].T
            if k > 0:
                dst[2 * k - 1] = v[8:40]
            if k < 4:
                dst[2 * k] = v[72:104]

    for copy in halos:
        copy.wait_send()

    @pl.when(owner)
    def _():
        for n, buf, count in ((0, s1, 8 * (ng - 1)), (1, s2, 16 * (ns - 1)), (2, s3, 16 * (ns - 1)), (3, s4, 8 * (nt - 1))):
            part = buf.at[pl.ds(0, count)]
            pltpu.make_async_copy(part, part, p_send.at[n]).wait()

    if late:

        @pl.when(other)
        def _():
            pltpu.make_async_copy(s1, s1, p_send.at[0]).wait()
            loads[8].wait()


def call(ns, nt, nz, consts, *args):
    ng = nz // 2
    packed, spectral, places = consts
    vmem, anywhere = pl.BlockSpec(memory_space=pltpu.VMEM), pl.BlockSpec(memory_space=pl.ANY)
    smem = pl.BlockSpec(memory_space=pltpu.SMEM)

    def buf(*shape):
        return pltpu.VMEM(shape, F32)

    out = jax.ShapeDtypeStruct((ROWS, COLS, nz), F32)
    return pl.pallas_call(
        functools.partial(kernel, ns, nt, nz, places),
        out_shape=[out] * 4,
        in_specs=[anywhere] * 11 + [smem] + [anywhere] * 2,
        out_specs=[vmem] * 4,
        scratch_shapes=[
            buf(8, 10, 64, nz), buf(3, nz, nz), buf(*packed.shape), buf(136, 128), buf(416, nz),
            buf(nz, 640), buf(nz, 896), buf(nz, 640), buf(nz, 1152),
            buf(nz, 640), buf(nz, 640), buf(nz, 896), buf(nz, 896), buf(8, nz, 128),
            buf(nz, 128), buf(nz, 128), buf(nz, 128), buf(nz, 128),
            buf(6, nz, 128), buf(6, nz, 128), buf(6, nz, 128), buf(6, nz, 128),
            buf(8 * ng, 128), buf(8 * nt, 128), buf(16 * ns, 128), buf(16 * ns, 128),
            buf(16 * ns, 128), buf(16 * ns, 128), buf(8 * nt, 128), buf(8 * ng, 128),
            buf(6, nz, 640), buf(nz, 640), buf(6, nz, 896), buf(nz, 896), buf(2, nz, 640),
            buf(nz, 896), buf(nz, 896), buf(nz, 640),
            buf(nz, 640), buf(nz, 640), buf(nz, 640), buf(nz, 640),
            pltpu.SemaphoreType.DMA((13,)), pltpu.SemaphoreType.DMA((4,)), pltpu.SemaphoreType.DMA((4,)),
            pltpu.SemaphoreType.DMA((4,)), pltpu.SemaphoreType.DMA((4,)), pltpu.SemaphoreType.REGULAR,
        ],
        compiler_params=pltpu.CompilerParams(
            collective_id=0, has_side_effects=True, vmem_limit_bytes=60 * 1024 * 1024
        ),
    )(*args, jnp.asarray(packed), jnp.asarray(spectral))


def solution(mesh):
    ns, nt = mesh.shape["ys"], mesh.shape["xs"]
    consts = tables(ns, nt)

    def shards(*args):
        flat = [v.transpose(1, 2, 0) for v in args[:8]]
        out = call(ns, nt, args[0].shape[0], consts, *flat, *args[8:])
        return tuple(v.transpose(2, 0, 1) for v in out)

    block = P(None, "ys", "xs")
    return jax.shard_map(
        shards, mesh=mesh, in_specs=(block,) * 8 + (P(),) * 4, out_specs=(block,) * 4, check_vma=False
    )
```

```python
import functools

import jax
import jax.numpy as jnp
import numpy as np
from jax import lax
from jax.experimental import pallas as pl
from jax.experimental.pallas import tpu as pltpu
from jax.sharding import PartitionSpec as P

MESH = pl.DeviceIdType.MESH
DT = 0.25
NU = 0.1
KAPPA = 0.1
GRAV = 1.0
EPS = 1e-6
F32 = jnp.float32
HI = lax.Precision.HIGHEST
ROWS, COLS = 8, 32


def tables(ns, nt):
    nx, ny = COLS * nt, ROWS * ns
    t = np.arange(nt)
    ring = np.zeros((2, ns, nt))
    ring[0, 0] = 1 / np.sqrt(nt)
    ring[1, 0] = (-1.0) ** t / np.sqrt(nt)
    for j in range(1, ns):
        ring[0, j] = np.sqrt(2 / nt) * np.cos(2 * np.pi * j * t / nt)
        ring[1, j] = np.sqrt(2 / nt) * np.sin(2 * np.pi * j * t / nt)

    def basis(n, k):
        z = np.arange(n)
        if k == 0 or 2 * k == n:
            return [np.cos(2 * np.pi * k * z / n) / np.sqrt(n)]
        return [
            np.sqrt(2 / n) * np.cos(2 * np.pi * k * z / n),
            np.sqrt(2 / n) * np.sin(2 * np.pi * k * z / n),
        ]

    inner = np.zeros((ns, 2, 2, COLS, 2, 2, COLS))
    lamx = np.zeros((ns, 2, 2, COLS))
    for j in range(ns):
        found, lam = [], []
        for k in range(nx // 2 + 1):
            res = k % nt
            own = res in (0, nt // 2) if j == 0 else res in (j, nt - j)
            if own:
                for vec in basis(nx, k):
                    found.append(np.einsum("qt,tc->qc", ring[:, j], vec.reshape(nt, COLS)))
                    lam.append(4 * np.sin(np.pi * k / nx) ** 2)
        block = np.stack(found, -1).reshape(2, COLS, 2, COLS)
        for m in range(2):
            inner[j, :, m, :, :, m, :] = block
            lamx[j, :, m, :] = np.array(lam).reshape(2, COLS)
    inner = inner.reshape(ns, 4 * COLS, 4 * COLS)
    lamx = np.broadcast_to(lamx.reshape(ns, 1, 4 * COLS), (ns, 8, 4 * COLS))
    spectral = np.concatenate([inner, lamx], 1)

    ybase, ylam = [], []
    for k in range(ny // 2 + 1):
        for vec in basis(ny, k):
            ybase.append(vec)
            ylam.append(4 * np.sin(np.pi * k / ny) ** 2)
    ybase = np.stack(ybase)
    lamy = np.broadcast_to(np.array(ylam)[:, None], (ny, 128))
    yfwd = ybase.reshape(ny, ns, 2, 4).transpose(0, 3, 2, 1).reshape(ny, ny)
    yinv = np.zeros((ns, 16, ny))
    for s in range(ns):
        for r in range(14):
            yinv[s, r] = ybase[:, (ROWS * s - 3 + r) % ny]
    after = ybase[:, (ROWS * np.arange(ns) + ROWS) % ny]
    ring = ring.reshape(nt, nt)
    parts = (lamy, yinv.reshape(16 * ns, ny), yfwd, after, ring, np.roll(ring, -1, 1), ring.T)
    packed = np.zeros((sum(len(v) for v in parts), 128))
    at, places = 0, []
    for v in parts:
        packed[at : at + len(v), : v.shape[1]] = v
        places.append((at, at + len(v), v.shape[1]))
        at += len(v)
    return packed.astype(np.float32), np.ascontiguousarray(spectral).astype(np.float32), tuple(places)


def owners(nt, ng):
    if (nt, ng) != (32, 24):
        return (lambda n: n), (lambda t: t), (lambda t: t < ng)

    def index_of(n):
        h = n // 2
        late = h // 8
        y = h - 8 * late
        y = y + late * 4 * (y // 2)
        return 4 * y + 2 * late + n % 2

    def pair_of(t):
        y, late = t // 4, (t // 2) % 2
        return 2 * (y - late * 4 * (y // 4)) + 16 * late + t % 2

    def has(t):
        y, late = t // 4, (t // 2) % 2
        return (late == 0) | ((y + 2) % 8 < 4)

    return index_of, pair_of, has


def dot(a, b):
    return lax.dot_general(a, b, (((1,), (0,)), ((), ())), precision=HI, preferred_element_type=F32)


def dot_tn(a, b):
    return lax.dot_general(a, b, (((0,), (0,)), ((), ())), precision=HI, preferred_element_type=F32)


def dot_nt(a, b):
    return lax.dot_general(a, b, (((1,), (1,)), ((), ())), precision=HI, preferred_element_type=F32)


def roll(v, shift, axis=1):
    shift = shift % v.shape[axis]
    return v if shift == 0 else pltpu.roll(v, shift, axis)


def weno_parts(c, u, step, cut):
    stencil = [cut(roll(c, -k * step)) for k in range(-2, 4)]
    pos = u >= 0.0
    a = jnp.where(pos, stencil[0], stencil[5])
    b = jnp.where(pos, stencil[1], stencil[4])
    m = jnp.where(pos, stencil[2], stencil[3])
    p = jnp.where(pos, stencil[3], stencil[2])
    q = jnp.where(pos, stencil[4], stencil[1])
    e0, f0 = a - 2.0 * b + m, a - 4.0 * b + 3.0 * m
    e1, f1 = b - 2.0 * m + p, b - p
    e2, f2 = m - 2.0 * p + q, 3.0 * m - 4.0 * p + q
    r0 = 1.0 / (EPS + (13.0 / 12.0 * e0 * e0 + 0.25 * f0 * f0))
    r1 = 1.0 / (EPS + (13.0 / 12.0 * e1 * e1 + 0.25 * f1 * f1))
    r2 = 1.0 / (EPS + (13.0 / 12.0 * e2 * e2 + 0.25 * f2 * f2))
    w0, w1, w2 = 0.1 * r0 * r0, 0.6 * r1 * r1, 0.3 * r2 * r2
    inv = 1.0 / (w0 + w1 + w2)
    w0, w1, w2 = w0 * inv, w1 * inv, w2 * inv
    v0 = (2.0 * a - 7.0 * b + 11.0 * m) * (1.0 / 6.0)
    v1 = (5.0 * m - b + 2.0 * p) * (1.0 / 6.0)
    v2 = (2.0 * m + 5.0 * p - q) * (1.0 / 6.0)
    value = w0 * v0 + w1 * v1 + w2 * v2
    w0, w1, w2 = w0 * u, w1 * u, w2 * u
    h0 = -2.0 * w0 * r0 * (v0 - value)
    h1 = -2.0 * w1 * r1 * (v1 - value)
    h2 = -2.0 * w2 * r2 * (v2 - value)
    e0, f0 = h0 * e0 * (13.0 / 6.0), h0 * f0 * 0.5
    e1, f1 = h1 * e1 * (13.0 / 6.0), h1 * f1 * 0.5
    e2, f2 = h2 * e2 * (13.0 / 6.0), h2 * f2 * 0.5
    w0, w1, w2 = w0 * (1.0 / 6.0), w1 * (1.0 / 6.0), w2 * (1.0 / 6.0)
    ga = 2.0 * w0 + e0 + f0
    gb = -7.0 * w0 - w1 - 2.0 * e0 - 4.0 * f0 + e1 + f1
    gm = 11.0 * w0 + 5.0 * w1 + 2.0 * w2 + e0 + 3.0 * f0 - 2.0 * e1 + e2 + 3.0 * f2
    gp = 2.0 * w1 + 5.0 * w2 + e1 - f1 - 2.0 * e2 - 4.0 * f2
    gq = e2 + f2 - w2
    zero = jnp.zeros_like(ga)
    return value, (
        jnp.where(pos, ga, zero),
        jnp.where(pos, gb, gq),
        jnp.where(pos, gm, gp),
        jnp.where(pos, gp, gm),
        jnp.where(pos, gq, gb),
        jnp.where(pos, zero, ga),
    )


def spread(f):
    return roll(f, 1) + roll(f, -1) + roll(f, 64) + roll(f, -64) - 4.0 * f


def kernel(
    ns, nt, nz, places,
    fu_h, fv_h, fw_h, fc_h, iu_h, iv_h, iw_h, it_h, dinv_h, vecs_h, minv_h, eig, packed_h, spec_h,
    out_u, out_v, out_w, out_c,
    raw, mats, packed, spec, rhs, u10, v14, w10, c18, iu10, iv10, iw14, it14, modal,
    xe, xw, xfw, xfe, yn2, ys2, yfs2, yfn2,
    s1, r1, s2, r2, s3, r3, s4, r4,
    ax, wx, ay, wy, ch, d_buf, p_buf, mw_buf, ou, ov, ow, oc,
    in_sem, h_send, h_recv, p_send, p_recv, ready,
):
    ng = nz // 2
    s, t = lax.axis_index("ys"), lax.axis_index("xs")
    index_of, pair_of, has = owners(nt, ng)
    owner = has(t)
    other = jnp.logical_not(owner)
    mine = pair_of(t)
    late = nt - ng

    barrier = pltpu.get_barrier_semaphore()

    def greet(a, b):
        pl.semaphore_signal(barrier, 1, device_id=(a, b), device_id_type=MESH)

    def greet_x(i, _):
        greet(s, lax.rem(t + i, nt))
        return 0

    def greet_y(i, _):
        greet(lax.rem(s + i, ns), t)
        return 0

    east, west = lax.rem(t + 1, nt), lax.rem(t + nt - 1, nt)
    north, south = lax.rem(s + 1, ns), lax.rem(s + ns - 1, ns)
    twin = t + 1 - 2 * lax.rem(t, 2)

    @pl.when(owner)
    def _():
        lax.fori_loop(1, nt, greet_x, 0)
        lax.fori_loop(1, ns, greet_y, 0)

    if late:

        @pl.when(other)
        def _():
            greet(north, t)
            greet(south, t)
            greet(s, twin)

    loads = []
    for n, src in enumerate((iu_h, iv_h, iw_h, it_h, fc_h, fu_h, fv_h, fw_h)):
        dst = raw.at[n, pl.ds(1, ROWS), pl.ds(8, COLS)]
        loads.append(pltpu.make_async_copy(src, dst, in_sem.at[n]))
    loads.append(pltpu.make_async_copy(spec_h.at[s], spec, in_sem.at[8]))
    loads.append(pltpu.make_async_copy(packed_h, packed, in_sem.at[9]))
    for n, src in enumerate((vecs_h, minv_h, dinv_h)):
        loads.append(pltpu.make_async_copy(src, mats.at[n], in_sem.at[10 + n]))
    order = (0, 1, 2, 10, 9, 8, 3, 4, 5, 6, 7, 11, 12)
    for n in order:
        loads[n].start()

    lane = lax.broadcasted_iota(jnp.int32, (nz, 128), 1)
    slot = lane & 63
    low = lane < 64
    core = (slot >= 8) & (slot < 40)
    lane_g = lax.broadcasted_iota(jnp.int32, (ng, 128), 1)
    level = lax.broadcasted_iota(jnp.int32, (nz, 640), 0)

    def rows(n, count):
        return pl.ds(pl.multiple_of(n * count, count), count)

    def tile(n):
        return slice(128 * n, 128 * n + 128)

    def table(n):
        first, end, width = places[n]
        return packed[first:end, :width]

    def place(n, buf, first):
        for k in range(5):
            v = raw[n, 2 * k : 2 * k + 2].reshape(128, nz)
            buf[:, tile(first + k)] = v.T

    def pack_x(fields, out):
        total = jnp.zeros((nz, 128), F32)
        for buf, first, col, at, count in fields:
            for k in range(4):
                if k == 0:
                    v = jnp.where(low, buf[:, tile(first + 4)], buf[:, tile(first)])
                else:
                    v = buf[:, tile(first + k)]
                to = 16 * k + at
                total = jnp.where((slot >= to) & (slot < to + count), roll(v, to - 8 - col), total)
        out[...] = total

    def unpack_x(src, fields):
        v = src[...]
        for buf, first, col, at, count in fields:
            here = (slot >= 8 + col) & (slot < 8 + col + count)
            for k in range(4):
                w = roll(v, 8 + col - 16 * k - at)
                if k == 0:
                    z = tile(first + 4)
                    buf[:, z] = jnp.where(here & low, w, buf[:, z])
                    z = tile(first)
                    buf[:, z] = jnp.where(here & ~low, w, buf[:, z])
                else:
                    z = tile(first + k)
                    buf[:, z] = jnp.where(here, w, buf[:, z])

    def pair(one, two):
        return jnp.where(core, one, roll(two, 32))

    def remote(src, dst, ds, dt, send, recv):
        return pltpu.make_async_remote_copy(
            src_ref=src, dst_ref=dst, send_sem=send, recv_sem=recv, device_id=(ds, dt), device_id_type=MESH
        )

    loads[0].wait()
    loads[1].wait()
    loads[2].wait()
    iu = raw[0, 1:9, 8:40].reshape(ROWS * COLS, nz)
    iv = raw[1, 1:9, 8:40].reshape(ROWS * COLS, nz)
    iw = raw[2, 1:9, 8:40].reshape(ROWS * COLS, nz)
    first_col = lax.broadcasted_iota(jnp.int32, iu.shape, 0) % COLS == 0
    before = jnp.where(first_col, 0.0, roll(iu, 1, 0))
    behind = jnp.concatenate([jnp.zeros((COLS, nz), F32), iv[: 7 * COLS]], 0)
    rhs[0:256, :] = (iu - before) + (iv - behind)
    rhs[256:288, :] = -iv[7 * COLS :]
    rhs[288:416, :] = jnp.zeros((128, nz), F32)
    for r in range(ROWS):
        at = 288 + 32 * (r % 4) + r // 4
        rhs[at : at + 1, :] = -raw[0, r + 1, 39:40, :]
    loads[10].wait()
    vt = mats[0].T
    next_vt = jnp.concatenate([vt[:, 1:], jnp.zeros((nz, 1), F32)], 1)
    main = dot_nt(vt, rhs[0:256, :]) + dot_nt(vt - next_vt, iw)
    extra = dot_nt(vt, rhs[256:416, :])
    modal[0] = main[:, :128]
    modal[1] = main[:, 128:]
    modal[2] = jnp.concatenate([extra[:, :32], jnp.zeros((nz, 96), F32)], 1)
    modal[3] = extra[:, 32:]
    for i in range(4):
        even = modal[i, pl.ds(0, ng, stride=2), :]
        odd = modal[i, pl.ds(1, ng, stride=2), :]
        if i < 2:
            s1[pl.ds(i, ng, stride=8), :] = even
            s1[pl.ds(2 + i, ng, stride=8), :] = odd
        elif i == 2:
            s1[pl.ds(4, ng, stride=8), :] = jnp.where(lane_g < 32, even, roll(odd, 32))
        else:
            s1[pl.ds(5, ng, stride=8), :] = jnp.where((lane_g & 31) < 2, even, roll(odd, 2))
            s1[pl.ds(6, ng, stride=8), :] = jnp.zeros((ng, 128), F32)
            s1[pl.ds(7, ng, stride=8), :] = jnp.zeros((ng, 128), F32)

    @pl.when(owner)
    def _():
        pl.semaphore_wait(barrier, ng - 1 + ns - 1)

    if late:

        @pl.when(other)
        def _():
            pl.semaphore_wait(barrier, ng + 3)

    def send1(i, _):
        g = lax.rem(t + i, ng)
        to = index_of(g)

        @pl.when(to != t)
        def _():
            remote(s1.at[rows(g, 8)], r1.at[rows(t, 8)], s, to, p_send.at[0], p_recv.at[0]).start()

        return 0

    lax.fori_loop(0, ng, send1, 0)

    @pl.when(owner)
    def _():
        pltpu.make_async_copy(s1.at[rows(mine, 8)], r1.at[rows(t, 8)], p_recv.at[0]).start()

    if late:

        @pl.when(other)
        def _():
            def report(i, _):
                g = index_of(i)
                pl.semaphore_signal(ready, 1, device_id=(s, g), device_id_type=MESH)
                return 0

            lax.fori_loop(0, ng, report, 0)

    for n, buf, first in ((3, it14, 1), (4, c18, 2), (5, u10, 0), (6, v14, 1), (7, w10, 0)):
        loads[n].wait()
        place(n, buf, first)
    place(0, iu10, 0)
    place(1, iv10, 0)
    place(2, iw14, 1)

    pack_x(((iw14, 1, 29, 0, 3), (it14, 1, 29, 3, 3), (iu10, 0, 31, 6, 1), (iv10, 0, 31, 7, 1), (u10, 0, 29, 8, 3), (c18, 2, 27, 11, 5)), xe)
    pack_x(((iw14, 1, 0, 0, 3), (it14, 1, 0, 3, 3), (iu10, 0, 0, 6, 1), (iv10, 0, 0, 7, 1), (u10, 0, 0, 8, 2), (c18, 2, 0, 11, 5)), xw)
    for n in range(3):
        yn2[n] = pair(c18[:, tile(4 + n)], v14[:, tile(3 + n)])
        ys2[n] = pair(c18[:, tile(2 + n)], v14[:, tile(1 + n)])
    for n in range(2):
        yn2[3 + n] = pair(iw14[:, tile(4 + n)], it14[:, tile(4 + n)])
        ys2[3 + n] = pair(iw14[:, tile(1 + n)], it14[:, tile(1 + n)])
    yn2[5] = pair(iu10[:, tile(4)], iv10[:, tile(4)])
    ys2[5] = pair(iu10[:, tile(0)], iv10[:, tile(0)])
    loads[9].wait()

    @pl.when(owner)
    def _():
        pltpu.make_async_copy(r1, r1, p_recv.at[0]).wait()
        x = jnp.concatenate([r1[pl.ds(i, nt, stride=8), :] for i in range(5)], 1)
        y = dot(table(4), x)
        z = dot(table(5), r1[pl.ds(5, nt, stride=8), :])
        first = (lax.broadcasted_iota(jnp.int32, (nt, 128), 1) & 31) == 0
        at = lax.broadcasted_iota(jnp.int32, (ns, 128), 1)
        parts = [y[:, tile(i)] + jnp.where(first, roll(z, -i), 0.0) for i in range(4)]
        for q in range(2):
            for i in range(4):
                s2[pl.ds(4 * q + i, ns, stride=16), :] = parts[i][q * ns : (q + 1) * ns]
        s2[pl.ds(8, ns, stride=16), :] = jnp.where(at < 64, y[:ns, tile(4)], roll(y[ns:, tile(4)], 64))
        for i in range(9, 16):
            s2[pl.ds(i, ns, stride=16), :] = jnp.zeros((ns, 128), F32)

        def send2(i, _):
            j = lax.rem(s + i, ns)
            remote(s2.at[rows(j, 16)], r2.at[rows(s, 16)], j, t, p_send.at[1], p_recv.at[1]).start()
            return 0

        lax.fori_loop(1, ns, send2, 0)
        pltpu.make_async_copy(s2.at[rows(s, 16)], r2.at[rows(s, 16)], p_recv.at[1]).start()

    if late:

        @pl.when(owner)
        def _():
            pl.semaphore_wait(ready, late)

    halos = [
        remote(xe, xfw, s, east, h_send.at[0], h_recv.at[0]),
        remote(yn2, yfs2, north, t, h_send.at[1], h_recv.at[1]),
        remote(xw, xfe, s, west, h_send.at[2], h_recv.at[2]),
        remote(ys2, yfn2, south, t, h_send.at[3], h_recv.at[3]),
    ]
    for copy in halos:
        copy.start()

    @pl.when(owner)
    def _():
        loads[8].wait()
        pltpu.make_async_copy(r2, r2, p_recv.at[1]).wait()
        part = [
            jnp.concatenate([r2[pl.ds(2 * n + i, ns, stride=16), :] for i in range(2)], 0) for n in range(4)
        ]
        group = lax.broadcasted_iota(jnp.int32, (2 * ns, 128), 1) // 32
        x = []
        for r in range(4):
            v = roll(part[0], -32 * r)
            for n in range(1, 4):
                v = jnp.where(group == n, roll(part[n], 32 * (n - r)), v)
            x.append(v)
        x = jnp.concatenate(x, 0)
        y = dot(table(2), x) + dot(table(3), r2[pl.ds(8, ns, stride=16), :])
        inner = spec[0:128, :]
        y = dot(y, inner)
        wide = lax.broadcasted_iota(jnp.int32, (1, 128), 1)
        own = jnp.where((wide & 32) == 0, eig[2 * mine], eig[2 * mine + 1])
        y = -y / (own + table(0) + spec[128:129, :])
        y = dot(table(1), dot_nt(y, inner))
        s3[...] = y

        def send3(i, _):
            j = lax.rem(s + i, ns)
            remote(s3.at[rows(j, 16)], r3.at[rows(s, 16)], j, t, p_send.at[2], p_recv.at[2]).start()
            return 0

        lax.fori_loop(1, ns, send3, 0)
        pltpu.make_async_copy(s3.at[rows(s, 16)], r3.at[rows(s, 16)], p_recv.at[2]).start()

    halos[0].wait_recv()
    unpack_x(xfw, ((iw14, 1, -3, 0, 3), (it14, 1, -3, 3, 3), (iu10, 0, -1, 6, 1), (iv10, 0, -1, 7, 1), (u10, 0, -3, 8, 3), (c18, 2, -5, 11, 5)))
    halos[2].wait_recv()
    unpack_x(xfe, ((iw14, 1, 32, 0, 3), (it14, 1, 32, 3, 3), (iu10, 0, 32, 6, 1), (iv10, 0, 32, 7, 1), (u10, 0, 32, 8, 2), (c18, 2, 32, 11, 5)))

    def x_faces(n, _):
        at = pl.ds(pl.multiple_of(8 * n, 8), 8)
        value, parts = weno_parts(c18[at, 256:896], u10[at, :], 1, lambda f: f)
        wx[at, :] = value
        for o in range(6):
            ax[o, at, :] = parts[o]
        return 0

    lax.fori_loop(0, nz // 8, x_faces, 0)

    halos[1].wait_recv()
    halos[3].wait_recv()
    v = yfs2[5]
    iu10[:, tile(0)] = jnp.where(low, v, iu10[:, tile(0)])
    iv10[:, tile(0)] = jnp.where(low, roll(v, -32), iv10[:, tile(0)])
    v = yfn2[5]
    iu10[:, tile(4)] = jnp.where(low, iu10[:, tile(4)], v)
    iv10[:, tile(4)] = jnp.where(low, iv10[:, tile(4)], roll(v, -32))
    for n in range(3):
        v = yfs2[n]
        for buf, k, f in ((c18, n, v), (v14, n - 1, roll(v, -32))):
            if k >= 0:
                buf[:, tile(k)] = f if n < 2 else jnp.where(low, f, buf[:, tile(k)])
        v = yfn2[n]
        for buf, k, f in ((c18, 6 + n, v), (v14, 5 + n, roll(v, -32))):
            if k < buf.shape[1] // 128:
                buf[:, tile(k)] = f if n > 0 else jnp.where(low, buf[:, tile(k)], f)
    for n in range(2):
        v = yfs2[3 + n]
        for buf, f in ((iw14, v), (it14, roll(v, -32))):
            buf[:, tile(n)] = f if n < 1 else jnp.where(low, f, buf[:, tile(n)])
        v = yfn2[3 + n]
        for buf, f in ((iw14, v), (it14, roll(v, -32))):
            buf[:, tile(5 + n)] = f if n > 0 else jnp.where(low, buf[:, tile(5 + n)], f)

    def y_faces(n, _):
        at = pl.ds(pl.multiple_of(8 * n, 8), 8)
        value, parts = weno_parts(c18[at, :], v14[at, :], 64, lambda f: f[:, 128:1024])
        wy[at, :] = value
        for o in range(6):
            ay[o, at, :] = parts[o]
        return 0

    lax.fori_loop(0, nz // 8, y_faces, 0)

    @pl.when(owner)
    def _():
        pltpu.make_async_copy(r3, r3, p_recv.at[2]).wait()
        left = lax.broadcasted_iota(jnp.int32, (ns, 128), 1) < 64
        cols = []
        for i in range(7):
            one = r3[pl.ds(2 * i, ns, stride=16), :]
            two = r3[pl.ds(2 * i + 1, ns, stride=16), :]
            cols.append(
                jnp.concatenate(
                    [
                        jnp.where(left, one, roll(two, 64)),
                        jnp.where(left, roll(one, 64), two),
                    ],
                    0,
                )
            )
        y = dot(table(6), jnp.concatenate(cols, 1))
        at = lax.broadcasted_iota(jnp.int32, (nt, 128), 1) & 31
        edge = jnp.zeros((nt, 128), F32)
        before, after = roll(y, 1, 0), roll(y, -1, 0)
        for i in range(7):
            s4[pl.ds(i, nt, stride=8), :] = y[:, tile(i)]
            if 1 <= i <= 5:
                k = 3 * (i - 1)
                edge = jnp.where((at >= k) & (at < k + 3), roll(before[:, tile(i)], k - 29), edge)
                edge = jnp.where((at >= 16 + k) & (at < 19 + k), roll(after[:, tile(i)], 16 + k), edge)
        s4[pl.ds(7, nt, stride=8), :] = edge

        def send4(i, _):
            g = lax.rem(t + i, nt)
            remote(s4.at[rows(g, 8)], r4.at[rows(mine, 8)], s, g, p_send.at[3], p_recv.at[3]).start()
            return 0

        lax.fori_loop(1, nt, send4, 0)
        pltpu.make_async_copy(s4.at[rows(t, 8)], r4.at[rows(mine, 8)], p_recv.at[3]).start()

    c10, w = c18[:, 256:896], w10[...]
    ch[0] = jnp.where(level == nz - 1, 0.0, 0.5 * (c10 + roll(c10, -1, 0)))
    ch[1] = jnp.where(level == nz - 1, 0.0, 0.5 * w)

    loads[11].wait()
    loads[12].wait()
    pltpu.make_async_copy(r4, r4, p_recv.at[3]).wait()
    cols = []
    for i in range(8):
        one = r4[pl.ds(i, ng, stride=8), :]
        modal[i, pl.ds(0, ng, stride=2), :] = roll(one, 8)
        modal[i, pl.ds(1, ng, stride=2), :] = roll(one, -24)
        cols.append(modal[i])
    p = dot_tn(mats[1], jnp.concatenate(cols, 1))
    edge = p[:, tile(7)]
    for i in range(7):
        v = p[:, tile(i)]
        if 1 <= i <= 5:
            k = 3 * (i - 1)
            v = jnp.where((slot >= 5) & (slot < 8), roll(edge, -3 - k), v)
            v = jnp.where((slot >= 40) & (slot < 43), roll(edge, 16 - k), v)
        p_buf[:, tile(i)] = v
    p = p_buf[...]
    upper = jnp.where(lax.broadcasted_iota(jnp.int32, p.shape, 0) == nz - 1, 0.0, roll(p, -1, 0))
    mid = iw14[...] - (upper - p)
    mw_buf[...] = mid[:, 128:768]
    d = dot_tn(mats[2], it14[...] + GRAV * DT * mid)
    d_buf[...] = d
    d10 = d[:, 128:768]
    gz = roll(d10, -1, 0) - d10
    wz = ch[1] * gz
    oc[...] = d10 + DT * (wz + roll(wz, 1, 0))
    mw = mw_buf[...]
    ow[...] = mw + DT * NU * spread(mw) + DT * (ch[0] * gz)

    def last(n, _):
        at = pl.ds(pl.multiple_of(8 * n, 8), 8)
        p14, d14 = p_buf[at, :], d_buf[at, :]
        p10, dx = p14[:, 128:768], d14[:, 128:768]
        mu = iu10[at, :] - (roll(p10, -1) - p10)
        mv = iv10[at, :] - (roll(p14, -64)[:, 128:768] - p10)
        gx = roll(dx, -1) - dx
        gy = roll(d14, -64) - d14
        total = KAPPA * spread(dx)
        ty = jnp.zeros_like(d14)
        for o in range(6):
            total = total + roll(ax[o, at, :] * gx, o - 2)
            ty = ty + roll(ay[o, at, :] * gy, 64 * (o - 2))
        ou[at, :] = mu + DT * NU * spread(mu) + DT * (wx[at, :] * gx)
        ov[at, :] = mv + DT * NU * spread(mv) + DT * (wy[at, :] * gy)[:, 128:768]
        oc[at, :] = oc[at, :] + DT * (total + ty[:, 128:768])
        return 0

    lax.fori_loop(0, nz // 8, last, 0)

    for src, dst in ((ou, out_u), (ov, out_v), (ow, out_w), (oc, out_c)):
        for k in range(5):
            v = src[:, tile(k)].T
            if k > 0:
                dst[2 * k - 1] = v[8:40]
            if k < 4:
                dst[2 * k] = v[72:104]

    for copy in halos:
        copy.wait_send()

    @pl.when(owner)
    def _():
        for n, buf, count in ((0, s1, 8 * (ng - 1)), (1, s2, 16 * (ns - 1)), (2, s3, 16 * (ns - 1)), (3, s4, 8 * (nt - 1))):
            part = buf.at[pl.ds(0, count)]
            pltpu.make_async_copy(part, part, p_send.at[n]).wait()

    if late:

        @pl.when(other)
        def _():
            pltpu.make_async_copy(s1, s1, p_send.at[0]).wait()
            loads[8].wait()


def hand_over(a, b, c, d, out_a, out_b, out_c, out_d, sem):
    copies = [
        pltpu.make_async_copy(src, dst, sem.at[n])
        for n, (src, dst) in enumerate(((a, out_a), (b, out_b), (c, out_c), (d, out_d)))
    ]
    for copy in copies:
        copy.start()
    for copy in copies:
        copy.wait()


def call(ns, nt, nz, consts, *args):
    ng = nz // 2
    packed, spectral, places = consts
    vmem, anywhere = pl.BlockSpec(memory_space=pltpu.VMEM), pl.BlockSpec(memory_space=pl.ANY)
    smem = pl.BlockSpec(memory_space=pltpu.SMEM)

    def buf(*shape):
        return pltpu.VMEM(shape, F32)

    out = jax.ShapeDtypeStruct((ROWS, COLS, nz), F32)
    made = pl.pallas_call(
        functools.partial(kernel, ns, nt, nz, places),
        out_shape=[out] * 4,
        in_specs=[anywhere] * 11 + [smem] + [anywhere] * 2,
        out_specs=[vmem] * 4,
        scratch_shapes=[
            buf(8, 10, 64, nz), buf(3, nz, nz), buf(*packed.shape), buf(136, 128), buf(416, nz),
            buf(nz, 640), buf(nz, 896), buf(nz, 640), buf(nz, 1152),
            buf(nz, 640), buf(nz, 640), buf(nz, 896), buf(nz, 896), buf(8, nz, 128),
            buf(nz, 128), buf(nz, 128), buf(nz, 128), buf(nz, 128),
            buf(6, nz, 128), buf(6, nz, 128), buf(6, nz, 128), buf(6, nz, 128),
            buf(8 * ng, 128), buf(8 * nt, 128), buf(16 * ns, 128), buf(16 * ns, 128),
            buf(16 * ns, 128), buf(16 * ns, 128), buf(8 * nt, 128), buf(8 * ng, 128),
            buf(6, nz, 640), buf(nz, 640), buf(6, nz, 896), buf(nz, 896), buf(2, nz, 640),
            buf(nz, 896), buf(nz, 896), buf(nz, 640),
            buf(nz, 640), buf(nz, 640), buf(nz, 640), buf(nz, 640),
            pltpu.SemaphoreType.DMA((13,)), pltpu.SemaphoreType.DMA((4,)), pltpu.SemaphoreType.DMA((4,)),
            pltpu.SemaphoreType.DMA((4,)), pltpu.SemaphoreType.DMA((4,)), pltpu.SemaphoreType.REGULAR,
        ],
        compiler_params=pltpu.CompilerParams(
            collective_id=0, has_side_effects=True, vmem_limit_bytes=60 * 1024 * 1024
        ),
    )(*args, jnp.asarray(packed), jnp.asarray(spectral))
    return pl.pallas_call(
        hand_over,
        out_shape=[out] * 4,
        in_specs=[anywhere] * 4,
        out_specs=[anywhere] * 4,
        scratch_shapes=[pltpu.SemaphoreType.DMA((4,))],
    )(*made)


def solution(mesh):
    ns, nt = mesh.shape["ys"], mesh.shape["xs"]
    consts = tables(ns, nt)

    def shards(*args):
        flat = [v.transpose(1, 2, 0) for v in args[:8]]
        out = call(ns, nt, args[0].shape[0], consts, *flat, *args[8:])
        return tuple(v.transpose(2, 0, 1) for v in out)

    block = P(None, "ys", "xs")
    return jax.shard_map(
        shards, mesh=mesh, in_specs=(block,) * 8 + (P(),) * 4, out_specs=(block,) * 4, check_vma=False
    )
```

```python
import functools

import jax
import jax.numpy as jnp
import numpy as np
from jax import lax
from jax.experimental import pallas as pl
from jax.experimental.pallas import tpu as pltpu
from jax.sharding import PartitionSpec as P

MESH = pl.DeviceIdType.MESH
DT = 0.25
NU = 0.1
KAPPA = 0.1
GRAV = 1.0
EPS = 1e-6
F32 = jnp.float32
HI = lax.Precision.HIGHEST
ROWS, COLS = 8, 32


def tables(ns, nt):
    nx, ny = COLS * nt, ROWS * ns
    t = np.arange(nt)
    ring = np.zeros((2, ns, nt))
    ring[0, 0] = 1 / np.sqrt(nt)
    ring[1, 0] = (-1.0) ** t / np.sqrt(nt)
    for j in range(1, ns):
        ring[0, j] = np.sqrt(2 / nt) * np.cos(2 * np.pi * j * t / nt)
        ring[1, j] = np.sqrt(2 / nt) * np.sin(2 * np.pi * j * t / nt)

    def basis(n, k):
        z = np.arange(n)
        if k == 0 or 2 * k == n:
            return [np.cos(2 * np.pi * k * z / n) / np.sqrt(n)]
        return [
            np.sqrt(2 / n) * np.cos(2 * np.pi * k * z / n),
            np.sqrt(2 / n) * np.sin(2 * np.pi * k * z / n),
        ]

    inner = np.zeros((ns, 2, 2, COLS, 2, 2, COLS))
    lamx = np.zeros((ns, 2, 2, COLS))
    for j in range(ns):
        found, lam = [], []
        for k in range(nx // 2 + 1):
            res = k % nt
            own = res in (0, nt // 2) if j == 0 else res in (j, nt - j)
            if own:
                for vec in basis(nx, k):
                    found.append(np.einsum("qt,tc->qc", ring[:, j], vec.reshape(nt, COLS)))
                    lam.append(4 * np.sin(np.pi * k / nx) ** 2)
        block = np.stack(found, -1).reshape(2, COLS, 2, COLS)
        for m in range(2):
            inner[j, :, m, :, :, m, :] = block
            lamx[j, :, m, :] = np.array(lam).reshape(2, COLS)
    inner = inner.reshape(ns, 4 * COLS, 4 * COLS)
    lamx = np.broadcast_to(lamx.reshape(ns, 1, 4 * COLS), (ns, 8, 4 * COLS))
    spectral = np.concatenate([inner, lamx], 1)

    ybase, ylam = [], []
    for k in range(ny // 2 + 1):
        for vec in basis(ny, k):
            ybase.append(vec)
            ylam.append(4 * np.sin(np.pi * k / ny) ** 2)
    ybase = np.stack(ybase)
    lamy = np.broadcast_to(np.array(ylam)[:, None], (ny, 128))
    yfwd = ybase.reshape(ny, ns, 2, 4).transpose(0, 3, 2, 1).reshape(ny, ny)
    yinv = np.zeros((ns, 16, ny))
    for s in range(ns):
        for r in range(14):
            yinv[s, r] = ybase[:, (ROWS * s - 3 + r) % ny]
    after = ybase[:, (ROWS * np.arange(ns) + ROWS) % ny]
    ring = ring.reshape(nt, nt)
    parts = (lamy, yinv.reshape(16 * ns, ny), yfwd, after, ring, np.roll(ring, -1, 1), ring.T)
    packed = np.zeros((sum(len(v) for v in parts), 128))
    at, places = 0, []
    for v in parts:
        packed[at : at + len(v), : v.shape[1]] = v
        places.append((at, at + len(v), v.shape[1]))
        at += len(v)
    return packed.astype(np.float32), np.ascontiguousarray(spectral).astype(np.float32), tuple(places)


def owners(nt, ng):
    if (nt, ng) != (32, 24):
        return (lambda n: n), (lambda t: t), (lambda t: t < ng)

    def index_of(n):
        h = n // 2
        late = h // 8
        y = h - 8 * late
        y = y + late * 4 * (y // 2)
        return 4 * y + 2 * late + n % 2

    def pair_of(t):
        y, late = t // 4, (t // 2) % 2
        return 2 * (y - late * 4 * (y // 4)) + 16 * late + t % 2

    def has(t):
        y, late = t // 4, (t // 2) % 2
        return (late == 0) | ((y + 2) % 8 < 4)

    return index_of, pair_of, has


def partner(t, i, nt):
    if nt != 32:
        return lax.rem(t + 1 + i, nt)
    flip, k, turn = (31 - i) // 16, (i % 16) // 2, 1 - i % 2
    odd = k % 2
    step = 4 + (1 - odd) * (k // 2) - odd * ((k + 1) // 2)
    return (t // 4 + step) % 8 * 4 + (t // 2 + flip) % 2 * 2 + (t + turn) % 2


def dot(a, b):
    return lax.dot_general(a, b, (((1,), (0,)), ((), ())), precision=HI, preferred_element_type=F32)


def dot_tn(a, b):
    return lax.dot_general(a, b, (((0,), (0,)), ((), ())), precision=HI, preferred_element_type=F32)


def dot_nt(a, b):
    return lax.dot_general(a, b, (((1,), (1,)), ((), ())), precision=HI, preferred_element_type=F32)


def roll(v, shift, axis=1):
    shift = shift % v.shape[axis]
    return v if shift == 0 else pltpu.roll(v, shift, axis)


def weno_parts(c, u, step, cut):
    stencil = [cut(roll(c, -k * step)) for k in range(-2, 4)]
    pos = u >= 0.0
    a = jnp.where(pos, stencil[0], stencil[5])
    b = jnp.where(pos, stencil[1], stencil[4])
    m = jnp.where(pos, stencil[2], stencil[3])
    p = jnp.where(pos, stencil[3], stencil[2])
    q = jnp.where(pos, stencil[4], stencil[1])
    e0, f0 = a - 2.0 * b + m, a - 4.0 * b + 3.0 * m
    e1, f1 = b - 2.0 * m + p, b - p
    e2, f2 = m - 2.0 * p + q, 3.0 * m - 4.0 * p + q
    r0 = 1.0 / (EPS + (13.0 / 12.0 * e0 * e0 + 0.25 * f0 * f0))
    r1 = 1.0 / (EPS + (13.0 / 12.0 * e1 * e1 + 0.25 * f1 * f1))
    r2 = 1.0 / (EPS + (13.0 / 12.0 * e2 * e2 + 0.25 * f2 * f2))
    w0, w1, w2 = 0.1 * r0 * r0, 0.6 * r1 * r1, 0.3 * r2 * r2
    inv = 1.0 / (w0 + w1 + w2)
    w0, w1, w2 = w0 * inv, w1 * inv, w2 * inv
    v0 = (2.0 * a - 7.0 * b + 11.0 * m) * (1.0 / 6.0)
    v1 = (5.0 * m - b + 2.0 * p) * (1.0 / 6.0)
    v2 = (2.0 * m + 5.0 * p - q) * (1.0 / 6.0)
    value = w0 * v0 + w1 * v1 + w2 * v2
    w0, w1, w2 = w0 * u, w1 * u, w2 * u
    h0 = -2.0 * w0 * r0 * (v0 - value)
    h1 = -2.0 * w1 * r1 * (v1 - value)
    h2 = -2.0 * w2 * r2 * (v2 - value)
    e0, f0 = h0 * e0 * (13.0 / 6.0), h0 * f0 * 0.5
    e1, f1 = h1 * e1 * (13.0 / 6.0), h1 * f1 * 0.5
    e2, f2 = h2 * e2 * (13.0 / 6.0), h2 * f2 * 0.5
    w0, w1, w2 = w0 * (1.0 / 6.0), w1 * (1.0 / 6.0), w2 * (1.0 / 6.0)
    ga = 2.0 * w0 + e0 + f0
    gb = -7.0 * w0 - w1 - 2.0 * e0 - 4.0 * f0 + e1 + f1
    gm = 11.0 * w0 + 5.0 * w1 + 2.0 * w2 + e0 + 3.0 * f0 - 2.0 * e1 + e2 + 3.0 * f2
    gp = 2.0 * w1 + 5.0 * w2 + e1 - f1 - 2.0 * e2 - 4.0 * f2
    gq = e2 + f2 - w2
    zero = jnp.zeros_like(ga)
    return value, (
        jnp.where(pos, ga, zero),
        jnp.where(pos, gb, gq),
        jnp.where(pos, gm, gp),
        jnp.where(pos, gp, gm),
        jnp.where(pos, gq, gb),
        jnp.where(pos, zero, ga),
    )


def spread(f):
    return roll(f, 1) + roll(f, -1) + roll(f, 64) + roll(f, -64) - 4.0 * f


def kernel(
    ns, nt, nz, places,
    fu_h, fv_h, fw_h, fc_h, iu_h, iv_h, iw_h, it_h, dinv_h, vecs_h, minv_h, eig, packed_h, spec_h,
    ou, ov, ow, oc,
    raw, mats, packed, spec, rhs, u10, v14, w10, c18, iu10, iv10, iw14, it14, modal,
    xe, xw, xfw, xfe, yn2, ys2, yfs2, yfn2,
    s1, r1, s2, r2, s3, r3, s4, r4,
    ax, wx, ay, wy, ch, d_buf, p_buf, mw_buf,
    in_sem, h_send, h_recv, p_send, p_recv, ready,
):
    ng = nz // 2
    s, t = lax.axis_index("ys"), lax.axis_index("xs")
    index_of, pair_of, has = owners(nt, ng)
    owner = has(t)
    other = jnp.logical_not(owner)
    mine = pair_of(t)
    late = nt - ng

    barrier = pltpu.get_barrier_semaphore()

    def greet(a, b):
        pl.semaphore_signal(barrier, 1, device_id=(a, b), device_id_type=MESH)

    def greet_x(i, _):
        greet(s, lax.rem(t + i, nt))
        return 0

    def greet_y(i, _):
        greet(lax.rem(s + i, ns), t)
        return 0

    east, west = lax.rem(t + 1, nt), lax.rem(t + nt - 1, nt)
    north, south = lax.rem(s + 1, ns), lax.rem(s + ns - 1, ns)
    twin = t + 1 - 2 * lax.rem(t, 2)

    @pl.when(owner)
    def _():
        lax.fori_loop(1, nt, greet_x, 0)
        lax.fori_loop(1, ns, greet_y, 0)

    if late:

        @pl.when(other)
        def _():
            greet(north, t)
            greet(south, t)
            greet(s, twin)

    loads = []
    for n, src in enumerate((iu_h, iv_h, iw_h, it_h, fc_h, fu_h, fv_h, fw_h)):
        dst = raw.at[n, pl.ds(1, ROWS), pl.ds(8, COLS)]
        loads.append(pltpu.make_async_copy(src, dst, in_sem.at[n]))
    loads.append(pltpu.make_async_copy(spec_h.at[s], spec, in_sem.at[8]))
    loads.append(pltpu.make_async_copy(packed_h, packed, in_sem.at[9]))
    for n, src in enumerate((vecs_h, minv_h, dinv_h)):
        loads.append(pltpu.make_async_copy(src, mats.at[n], in_sem.at[10 + n]))
    order = (0, 1, 2, 10, 9, 8, 3, 4, 5, 6, 7, 11, 12)
    for n in order:
        loads[n].start()

    lane = lax.broadcasted_iota(jnp.int32, (nz, 128), 1)
    slot = lane & 63
    low = lane < 64
    core = (slot >= 8) & (slot < 40)
    lane_g = lax.broadcasted_iota(jnp.int32, (ng, 128), 1)
    level = lax.broadcasted_iota(jnp.int32, (nz, 640), 0)

    def rows(n, count):
        return pl.ds(pl.multiple_of(n * count, count), count)

    def tile(n):
        return slice(128 * n, 128 * n + 128)

    def table(n):
        first, end, width = places[n]
        return packed[first:end, :width]

    def place(n, buf, first):
        for k in range(5):
            v = raw[n, 2 * k : 2 * k + 2].reshape(128, nz)
            buf[:, tile(first + k)] = v.T

    def pack_x(fields, out):
        total = jnp.zeros((nz, 128), F32)
        for buf, first, col, at, count in fields:
            for k in range(4):
                if k == 0:
                    v = jnp.where(low, buf[:, tile(first + 4)], buf[:, tile(first)])
                else:
                    v = buf[:, tile(first + k)]
                to = 16 * k + at
                total = jnp.where((slot >= to) & (slot < to + count), roll(v, to - 8 - col), total)
        out[...] = total

    def unpack_x(src, fields):
        v = src[...]
        for buf, first, col, at, count in fields:
            here = (slot >= 8 + col) & (slot < 8 + col + count)
            for k in range(4):
                w = roll(v, 8 + col - 16 * k - at)
                if k == 0:
                    z = tile(first + 4)
                    buf[:, z] = jnp.where(here & low, w, buf[:, z])
                    z = tile(first)
                    buf[:, z] = jnp.where(here & ~low, w, buf[:, z])
                else:
                    z = tile(first + k)
                    buf[:, z] = jnp.where(here, w, buf[:, z])

    def pair(one, two):
        return jnp.where(core, one, roll(two, 32))

    def remote(src, dst, ds, dt, send, recv):
        return pltpu.make_async_remote_copy(
            src_ref=src, dst_ref=dst, send_sem=send, recv_sem=recv, device_id=(ds, dt), device_id_type=MESH
        )

    loads[0].wait()
    loads[1].wait()
    loads[2].wait()
    iu = raw[0, 1:9, 8:40].reshape(ROWS * COLS, nz)
    iv = raw[1, 1:9, 8:40].reshape(ROWS * COLS, nz)
    iw = raw[2, 1:9, 8:40].reshape(ROWS * COLS, nz)
    first_col = lax.broadcasted_iota(jnp.int32, iu.shape, 0) % COLS == 0
    before = jnp.where(first_col, 0.0, roll(iu, 1, 0))
    behind = jnp.concatenate([jnp.zeros((COLS, nz), F32), iv[: 7 * COLS]], 0)
    rhs[0:256, :] = (iu - before) + (iv - behind)
    rhs[256:288, :] = -iv[7 * COLS :]
    rhs[288:416, :] = jnp.zeros((128, nz), F32)
    for r in range(ROWS):
        at = 288 + 32 * (r % 4) + r // 4
        rhs[at : at + 1, :] = -raw[0, r + 1, 39:40, :]
    loads[10].wait()
    vt = mats[0].T
    next_vt = jnp.concatenate([vt[:, 1:], jnp.zeros((nz, 1), F32)], 1)
    main = dot_nt(vt, rhs[0:256, :]) + dot_nt(vt - next_vt, iw)
    extra = dot_nt(vt, rhs[256:416, :])
    modal[0] = main[:, :128]
    modal[1] = main[:, 128:]
    modal[2] = jnp.concatenate([extra[:, :32], jnp.zeros((nz, 96), F32)], 1)
    modal[3] = extra[:, 32:]
    for i in range(4):
        even = modal[i, pl.ds(0, ng, stride=2), :]
        odd = modal[i, pl.ds(1, ng, stride=2), :]
        if i < 2:
            s1[pl.ds(i, ng, stride=8), :] = even
            s1[pl.ds(2 + i, ng, stride=8), :] = odd
        elif i == 2:
            s1[pl.ds(4, ng, stride=8), :] = jnp.where(lane_g < 32, even, roll(odd, 32))
        else:
            s1[pl.ds(5, ng, stride=8), :] = jnp.where((lane_g & 31) < 2, even, roll(odd, 2))
            s1[pl.ds(6, ng, stride=8), :] = jnp.zeros((ng, 128), F32)
            s1[pl.ds(7, ng, stride=8), :] = jnp.zeros((ng, 128), F32)

    @pl.when(owner)
    def _():
        pl.semaphore_wait(barrier, ng - 1 + ns - 1)

    if late:

        @pl.when(other)
        def _():
            pl.semaphore_wait(barrier, ng + 3)

    def send1(i, _):
        to = partner(t, i, nt)

        @pl.when(has(to))
        def _():
            remote(s1.at[rows(pair_of(to), 8)], r1.at[rows(t, 8)], s, to, p_send.at[0], p_recv.at[0]).start()

        return 0

    lax.fori_loop(0, nt - 1, send1, 0)

    @pl.when(owner)
    def _():
        pltpu.make_async_copy(s1.at[rows(mine, 8)], r1.at[rows(t, 8)], p_recv.at[0]).start()

    if late:

        @pl.when(other)
        def _():
            def report(i, _):
                g = index_of(i)
                pl.semaphore_signal(ready, 1, device_id=(s, g), device_id_type=MESH)
                return 0

            lax.fori_loop(0, ng, report, 0)

    for n, buf, first in ((3, it14, 1), (4, c18, 2), (5, u10, 0), (6, v14, 1), (7, w10, 0)):
        loads[n].wait()
        place(n, buf, first)
    place(0, iu10, 0)
    place(1, iv10, 0)
    place(2, iw14, 1)

    pack_x(((iw14, 1, 29, 0, 3), (it14, 1, 29, 3, 3), (iu10, 0, 31, 6, 1), (iv10, 0, 31, 7, 1), (u10, 0, 29, 8, 3), (c18, 2, 27, 11, 5)), xe)
    pack_x(((iw14, 1, 0, 0, 3), (it14, 1, 0, 3, 3), (iu10, 0, 0, 6, 1), (iv10, 0, 0, 7, 1), (u10, 0, 0, 8, 2), (c18, 2, 0, 11, 5)), xw)
    for n in range(3):
        yn2[n] = pair(c18[:, tile(4 + n)], v14[:, tile(3 + n)])
        ys2[n] = pair(c18[:, tile(2 + n)], v14[:, tile(1 + n)])
    for n in range(2):
        yn2[3 + n] = pair(iw14[:, tile(4 + n)], it14[:, tile(4 + n)])
        ys2[3 + n] = pair(iw14[:, tile(1 + n)], it14[:, tile(1 + n)])
    yn2[5] = pair(iu10[:, tile(4)], iv10[:, tile(4)])
    ys2[5] = pair(iu10[:, tile(0)], iv10[:, tile(0)])
    loads[9].wait()

    @pl.when(owner)
    def _():
        pltpu.make_async_copy(r1, r1, p_recv.at[0]).wait()
        x = jnp.concatenate([r1[pl.ds(i, nt, stride=8), :] for i in range(5)], 1)
        y = dot(table(4), x)
        z = dot(table(5), r1[pl.ds(5, nt, stride=8), :])
        first = (lax.broadcasted_iota(jnp.int32, (nt, 128), 1) & 31) == 0
        at = lax.broadcasted_iota(jnp.int32, (ns, 128), 1)
        parts = [y[:, tile(i)] + jnp.where(first, roll(z, -i), 0.0) for i in range(4)]
        for q in range(2):
            for i in range(4):
                s2[pl.ds(4 * q + i, ns, stride=16), :] = parts[i][q * ns : (q + 1) * ns]
        s2[pl.ds(8, ns, stride=16), :] = jnp.where(at < 64, y[:ns, tile(4)], roll(y[ns:, tile(4)], 64))
        for i in range(9, 16):
            s2[pl.ds(i, ns, stride=16), :] = jnp.zeros((ns, 128), F32)

        def send2(i, _):
            j = lax.rem(s + i, ns)
            remote(s2.at[rows(j, 16)], r2.at[rows(s, 16)], j, t, p_send.at[1], p_recv.at[1]).start()
            return 0

        lax.fori_loop(1, ns, send2, 0)
        pltpu.make_async_copy(s2.at[rows(s, 16)], r2.at[rows(s, 16)], p_recv.at[1]).start()

    if late:

        @pl.when(owner)
        def _():
            pl.semaphore_wait(ready, late)

    halos = [
        remote(xe, xfw, s, east, h_send.at[0], h_recv.at[0]),
        remote(yn2, yfs2, north, t, h_send.at[1], h_recv.at[1]),
        remote(xw, xfe, s, west, h_send.at[2], h_recv.at[2]),
        remote(ys2, yfn2, south, t, h_send.at[3], h_recv.at[3]),
    ]
    for copy in halos:
        copy.start()

    @pl.when(owner)
    def _():
        loads[8].wait()
        pltpu.make_async_copy(r2, r2, p_recv.at[1]).wait()
        part = [
            jnp.concatenate([r2[pl.ds(2 * n + i, ns, stride=16), :] for i in range(2)], 0) for n in range(4)
        ]
        group = lax.broadcasted_iota(jnp.int32, (2 * ns, 128), 1) // 32
        x = []
        for r in range(4):
            v = roll(part[0], -32 * r)
            for n in range(1, 4):
                v = jnp.where(group == n, roll(part[n], 32 * (n - r)), v)
            x.append(v)
        x = jnp.concatenate(x, 0)
        y = dot(table(2), x) + dot(table(3), r2[pl.ds(8, ns, stride=16), :])
        inner = spec[0:128, :]
        y = dot(y, inner)
        wide = lax.broadcasted_iota(jnp.int32, (1, 128), 1)
        own = jnp.where((wide & 32) == 0, eig[2 * mine], eig[2 * mine + 1])
        y = -y / (own + table(0) + spec[128:129, :])
        y = dot(table(1), dot_nt(y, inner))
        s3[...] = y

        def send3(i, _):
            j = lax.rem(s + i, ns)
            remote(s3.at[rows(j, 16)], r3.at[rows(s, 16)], j, t, p_send.at[2], p_recv.at[2]).start()
            return 0

        lax.fori_loop(1, ns, send3, 0)
        pltpu.make_async_copy(s3.at[rows(s, 16)], r3.at[rows(s, 16)], p_recv.at[2]).start()

    halos[0].wait_recv()
    unpack_x(xfw, ((iw14, 1, -3, 0, 3), (it14, 1, -3, 3, 3), (iu10, 0, -1, 6, 1), (iv10, 0, -1, 7, 1), (u10, 0, -3, 8, 3), (c18, 2, -5, 11, 5)))
    halos[2].wait_recv()
    unpack_x(xfe, ((iw14, 1, 32, 0, 3), (it14, 1, 32, 3, 3), (iu10, 0, 32, 6, 1), (iv10, 0, 32, 7, 1), (u10, 0, 32, 8, 2), (c18, 2, 32, 11, 5)))

    def x_faces(n, _):
        at = pl.ds(pl.multiple_of(8 * n, 8), 8)
        value, parts = weno_parts(c18[at, 256:896], u10[at, :], 1, lambda f: f)
        wx[at, :] = value
        for o in range(6):
            ax[o, at, :] = parts[o]
        return 0

    lax.fori_loop(0, nz // 8, x_faces, 0)

    halos[1].wait_recv()
    halos[3].wait_recv()
    v = yfs2[5]
    iu10[:, tile(0)] = jnp.where(low, v, iu10[:, tile(0)])
    iv10[:, tile(0)] = jnp.where(low, roll(v, -32), iv10[:, tile(0)])
    v = yfn2[5]
    iu10[:, tile(4)] = jnp.where(low, iu10[:, tile(4)], v)
    iv10[:, tile(4)] = jnp.where(low, iv10[:, tile(4)], roll(v, -32))
    for n in range(3):
        v = yfs2[n]
        for buf, k, f in ((c18, n, v), (v14, n - 1, roll(v, -32))):
            if k >= 0:
                buf[:, tile(k)] = f if n < 2 else jnp.where(low, f, buf[:, tile(k)])
        v = yfn2[n]
        for buf, k, f in ((c18, 6 + n, v), (v14, 5 + n, roll(v, -32))):
            if k < buf.shape[1] // 128:
                buf[:, tile(k)] = f if n > 0 else jnp.where(low, buf[:, tile(k)], f)
    for n in range(2):
        v = yfs2[3 + n]
        for buf, f in ((iw14, v), (it14, roll(v, -32))):
            buf[:, tile(n)] = f if n < 1 else jnp.where(low, f, buf[:, tile(n)])
        v = yfn2[3 + n]
        for buf, f in ((iw14, v), (it14, roll(v, -32))):
            buf[:, tile(5 + n)] = f if n > 0 else jnp.where(low, buf[:, tile(5 + n)], f)

    def y_faces(n, _):
        at = pl.ds(pl.multiple_of(8 * n, 8), 8)
        value, parts = weno_parts(c18[at, :], v14[at, :], 64, lambda f: f[:, 128:1024])
        wy[at, :] = value
        for o in range(6):
            ay[o, at, :] = parts[o]
        return 0

    lax.fori_loop(0, nz // 8, y_faces, 0)

    @pl.when(owner)
    def _():
        pltpu.make_async_copy(r3, r3, p_recv.at[2]).wait()
        left = lax.broadcasted_iota(jnp.int32, (ns, 128), 1) < 64
        cols = []
        for i in range(7):
            one = r3[pl.ds(2 * i, ns, stride=16), :]
            two = r3[pl.ds(2 * i + 1, ns, stride=16), :]
            cols.append(
                jnp.concatenate(
                    [
                        jnp.where(left, one, roll(two, 64)),
                        jnp.where(left, roll(one, 64), two),
                    ],
                    0,
                )
            )
        y = dot(table(6), jnp.concatenate(cols, 1))
        at = lax.broadcasted_iota(jnp.int32, (nt, 128), 1) & 31
        edge = jnp.zeros((nt, 128), F32)
        before, after = roll(y, 1, 0), roll(y, -1, 0)
        for i in range(7):
            s4[pl.ds(i, nt, stride=8), :] = y[:, tile(i)]
            if 1 <= i <= 5:
                k = 3 * (i - 1)
                edge = jnp.where((at >= k) & (at < k + 3), roll(before[:, tile(i)], k - 29), edge)
                edge = jnp.where((at >= 16 + k) & (at < 19 + k), roll(after[:, tile(i)], 16 + k), edge)
        s4[pl.ds(7, nt, stride=8), :] = edge

        def send4(i, _):
            g = partner(t, i, nt)
            remote(s4.at[rows(g, 8)], r4.at[rows(mine, 8)], s, g, p_send.at[3], p_recv.at[3]).start()
            return 0

        lax.fori_loop(0, nt - 1, send4, 0)
        pltpu.make_async_copy(s4.at[rows(t, 8)], r4.at[rows(mine, 8)], p_recv.at[3]).start()

    c10, w = c18[:, 256:896], w10[...]
    ch[0] = jnp.where(level == nz - 1, 0.0, 0.5 * (c10 + roll(c10, -1, 0)))
    ch[1] = jnp.where(level == nz - 1, 0.0, 0.5 * w)

    loads[11].wait()
    loads[12].wait()
    pltpu.make_async_copy(r4, r4, p_recv.at[3]).wait()
    cols = []
    for i in range(8):
        one = r4[pl.ds(i, ng, stride=8), :]
        modal[i, pl.ds(0, ng, stride=2), :] = roll(one, 8)
        modal[i, pl.ds(1, ng, stride=2), :] = roll(one, -24)
        cols.append(modal[i])
    p = dot_tn(mats[1], jnp.concatenate(cols, 1))
    edge = p[:, tile(7)]
    for i in range(7):
        v = p[:, tile(i)]
        if 1 <= i <= 5:
            k = 3 * (i - 1)
            v = jnp.where((slot >= 5) & (slot < 8), roll(edge, -3 - k), v)
            v = jnp.where((slot >= 40) & (slot < 43), roll(edge, 16 - k), v)
        p_buf[:, tile(i)] = v
    p = p_buf[...]
    upper = jnp.where(lax.broadcasted_iota(jnp.int32, p.shape, 0) == nz - 1, 0.0, roll(p, -1, 0))
    mid = iw14[...] - (upper - p)
    mw_buf[...] = mid[:, 128:768]
    d = dot_tn(mats[2], it14[...] + GRAV * DT * mid)
    d_buf[...] = d
    d10 = d[:, 128:768]
    gz = roll(d10, -1, 0) - d10
    wz = ch[1] * gz
    oc[...] = d10 + DT * (wz + roll(wz, 1, 0))
    mw = mw_buf[...]
    ow[...] = mw + DT * NU * spread(mw) + DT * (ch[0] * gz)

    def last(n, _):
        at = pl.ds(pl.multiple_of(8 * n, 8), 8)
        p14, d14 = p_buf[at, :], d_buf[at, :]
        p10, dx = p14[:, 128:768], d14[:, 128:768]
        mu = iu10[at, :] - (roll(p10, -1) - p10)
        mv = iv10[at, :] - (roll(p14, -64)[:, 128:768] - p10)
        gx = roll(dx, -1) - dx
        gy = roll(d14, -64) - d14
        total = KAPPA * spread(dx)
        ty = jnp.zeros_like(d14)
        for o in range(6):
            total = total + roll(ax[o, at, :] * gx, o - 2)
            ty = ty + roll(ay[o, at, :] * gy, 64 * (o - 2))
        ou[at, :] = mu + DT * NU * spread(mu) + DT * (wx[at, :] * gx)
        ov[at, :] = mv + DT * NU * spread(mv) + DT * (wy[at, :] * gy)[:, 128:768]
        oc[at, :] = oc[at, :] + DT * (total + ty[:, 128:768])
        return 0

    lax.fori_loop(0, nz // 8, last, 0)

    for copy in halos:
        copy.wait_send()

    @pl.when(owner)
    def _():
        for n, buf, count in ((0, s1, 8 * (ng - 1)), (1, s2, 16 * (ns - 1)), (2, s3, 16 * (ns - 1)), (3, s4, 8 * (nt - 1))):
            part = buf.at[pl.ds(0, count)]
            pltpu.make_async_copy(part, part, p_send.at[n]).wait()

    if late:

        @pl.when(other)
        def _():
            pltpu.make_async_copy(s1, s1, p_send.at[0]).wait()
            loads[8].wait()


def finish(a, b, c, d, out_a, out_b, out_c, out_d, made, sem):
    copies = []
    for n, (src, dst) in enumerate(((a, out_a), (b, out_b), (c, out_c), (d, out_d))):
        for k in range(5):
            v = src[:, 128 * k : 128 * k + 128].T
            if k > 0:
                made[n, 2 * k - 1] = v[8:40]
            if k < 4:
                made[n, 2 * k] = v[72:104]
        copies.append(pltpu.make_async_copy(made.at[n], dst, sem.at[n]))
        copies[n].start()
    for copy in copies:
        copy.wait()


def call(ns, nt, nz, consts, *args):
    ng = nz // 2
    packed, spectral, places = consts
    vmem, anywhere = pl.BlockSpec(memory_space=pltpu.VMEM), pl.BlockSpec(memory_space=pl.ANY)
    smem = pl.BlockSpec(memory_space=pltpu.SMEM)

    def buf(*shape):
        return pltpu.VMEM(shape, F32)

    out = jax.ShapeDtypeStruct((ROWS, COLS, nz), F32)
    made = pl.pallas_call(
        functools.partial(kernel, ns, nt, nz, places),
        out_shape=[pltpu.VMEM((nz, 640), F32)] * 4,
        in_specs=[anywhere] * 11 + [smem] + [anywhere] * 2,
        out_specs=[vmem] * 4,
        scratch_shapes=[
            buf(8, 10, 64, nz), buf(3, nz, nz), buf(*packed.shape), buf(136, 128), buf(416, nz),
            buf(nz, 640), buf(nz, 896), buf(nz, 640), buf(nz, 1152),
            buf(nz, 640), buf(nz, 640), buf(nz, 896), buf(nz, 896), buf(8, nz, 128),
            buf(nz, 128), buf(nz, 128), buf(nz, 128), buf(nz, 128),
            buf(6, nz, 128), buf(6, nz, 128), buf(6, nz, 128), buf(6, nz, 128),
            buf(8 * ng, 128), buf(8 * nt, 128), buf(16 * ns, 128), buf(16 * ns, 128),
            buf(16 * ns, 128), buf(16 * ns, 128), buf(8 * nt, 128), buf(8 * ng, 128),
            buf(6, nz, 640), buf(nz, 640), buf(6, nz, 896), buf(nz, 896), buf(2, nz, 640),
            buf(nz, 896), buf(nz, 896), buf(nz, 640),
            pltpu.SemaphoreType.DMA((13,)), pltpu.SemaphoreType.DMA((4,)), pltpu.SemaphoreType.DMA((4,)),
            pltpu.SemaphoreType.DMA((4,)), pltpu.SemaphoreType.DMA((4,)), pltpu.SemaphoreType.REGULAR,
        ],
        compiler_params=pltpu.CompilerParams(
            collective_id=0, has_side_effects=True, vmem_limit_bytes=60 * 1024 * 1024
        ),
    )(*args, jnp.asarray(packed), jnp.asarray(spectral))
    return pl.pallas_call(
        finish,
        out_shape=[out] * 4,
        in_specs=[vmem] * 4,
        out_specs=[anywhere] * 4,
        scratch_shapes=[buf(4, ROWS, COLS, nz), pltpu.SemaphoreType.DMA((4,))],
    )(*[pltpu.with_memory_space_constraint(v, pltpu.VMEM) for v in made])


def solution(mesh):
    ns, nt = mesh.shape["ys"], mesh.shape["xs"]
    consts = tables(ns, nt)

    def shards(*args):
        flat = [v.transpose(1, 2, 0) for v in args[:8]]
        out = call(ns, nt, args[0].shape[0], consts, *flat, *args[8:])
        return tuple(v.transpose(2, 0, 1) for v in out)

    block = P(None, "ys", "xs")
    return jax.shard_map(
        shards, mesh=mesh, in_specs=(block,) * 8 + (P(),) * 4, out_specs=(block,) * 4, check_vma=False
    )
```

```python
import functools

import jax
import jax.numpy as jnp
import numpy as np
from jax import lax
from jax.experimental import pallas as pl
from jax.experimental.pallas import tpu as pltpu
from jax.sharding import PartitionSpec as P

MESH = pl.DeviceIdType.MESH
DT = 0.25
NU = 0.1
KAPPA = 0.1
GRAV = 1.0
EPS = 1e-6
F32 = jnp.float32
HI = lax.Precision.HIGHEST
ROWS, COLS = 8, 32


def tables(ns, nt):
    nx, ny = COLS * nt, ROWS * ns
    t = np.arange(nt)
    ring = np.zeros((2, ns, nt))
    ring[0, 0] = 1 / np.sqrt(nt)
    ring[1, 0] = (-1.0) ** t / np.sqrt(nt)
    for j in range(1, ns):
        ring[0, j] = np.sqrt(2 / nt) * np.cos(2 * np.pi * j * t / nt)
        ring[1, j] = np.sqrt(2 / nt) * np.sin(2 * np.pi * j * t / nt)

    def basis(n, k):
        z = np.arange(n)
        if k == 0 or 2 * k == n:
            return [np.cos(2 * np.pi * k * z / n) / np.sqrt(n)]
        return [
            np.sqrt(2 / n) * np.cos(2 * np.pi * k * z / n),
            np.sqrt(2 / n) * np.sin(2 * np.pi * k * z / n),
        ]

    inner = np.zeros((ns, 2, 2, COLS, 2, 2, COLS))
    lamx = np.zeros((ns, 2, 2, COLS))
    for j in range(ns):
        found, lam = [], []
        for k in range(nx // 2 + 1):
            res = k % nt
            own = res in (0, nt // 2) if j == 0 else res in (j, nt - j)
            if own:
                for vec in basis(nx, k):
                    found.append(np.einsum("qt,tc->qc", ring[:, j], vec.reshape(nt, COLS)))
                    lam.append(4 * np.sin(np.pi * k / nx) ** 2)
        block = np.stack(found, -1).reshape(2, COLS, 2, COLS)
        for m in range(2):
            inner[j, :, m, :, :, m, :] = block
            lamx[j, :, m, :] = np.array(lam).reshape(2, COLS)
    inner = inner.reshape(ns, 4 * COLS, 4 * COLS)
    lamx = np.broadcast_to(lamx.reshape(ns, 1, 4 * COLS), (ns, 8, 4 * COLS))
    spectral = np.concatenate([inner, lamx], 1)

    ybase, ylam = [], []
    for k in range(ny // 2 + 1):
        for vec in basis(ny, k):
            ybase.append(vec)
            ylam.append(4 * np.sin(np.pi * k / ny) ** 2)
    ybase = np.stack(ybase)
    lamy = np.broadcast_to(np.array(ylam)[:, None], (ny, 128))
    yfwd = ybase.reshape(ny, ns, 2, 4).transpose(0, 3, 2, 1).reshape(ny, ny)
    yinv = np.zeros((ns, 16, ny))
    for s in range(ns):
        for r in range(14):
            yinv[s, r] = ybase[:, (ROWS * s - 3 + r) % ny]
    after = ybase[:, (ROWS * np.arange(ns) + ROWS) % ny]
    ring = ring.reshape(nt, nt)
    parts = (lamy, yinv.reshape(16 * ns, ny), yfwd, after, ring, np.roll(ring, -1, 1), ring.T)
    packed = np.zeros((sum(len(v) for v in parts), 128))
    at, places = 0, []
    for v in parts:
        packed[at : at + len(v), : v.shape[1]] = v
        places.append((at, at + len(v), v.shape[1]))
        at += len(v)
    return packed.astype(np.float32), np.ascontiguousarray(spectral).astype(np.float32), tuple(places)


def owners(nt, ng):
    if (nt, ng) != (32, 24):
        return (lambda n: n), (lambda t: t), (lambda t: t < ng)

    def index_of(n):
        h = n // 2
        late = h // 8
        y = h - 8 * late
        y = y + late * 4 * (y // 2)
        return 4 * y + 2 * late + n % 2

    def pair_of(t):
        y, late = t // 4, (t // 2) % 2
        return 2 * (y - late * 4 * (y // 4)) + 16 * late + t % 2

    def has(t):
        y, late = t // 4, (t // 2) % 2
        return (late == 0) | ((y + 2) % 8 < 4)

    return index_of, pair_of, has


def partner(t, i, nt):
    if nt != 32:
        return lax.rem(t + 1 + i, nt)
    flip, step, turn = (31 - i) // 16, (4, 3, 5, 2, 6, 1, 7, 0)[i % 16 // 2], 1 - i % 2
    y, z, core = lax.div(t, 4), lax.rem(lax.div(t, 2), 2), lax.rem(t, 2)
    return 4 * lax.rem(y + step, 8) + 2 * lax.rem(z + flip, 2) + lax.rem(core + turn, 2)


def dot(a, b):
    return lax.dot_general(a, b, (((1,), (0,)), ((), ())), precision=HI, preferred_element_type=F32)


def dot_tn(a, b):
    return lax.dot_general(a, b, (((0,), (0,)), ((), ())), precision=HI, preferred_element_type=F32)


def dot_nt(a, b):
    return lax.dot_general(a, b, (((1,), (1,)), ((), ())), precision=HI, preferred_element_type=F32)


def roll(v, shift, axis=1):
    shift = shift % v.shape[axis]
    return v if shift == 0 else pltpu.roll(v, shift, axis)


def weno_parts(c, u, step, cut):
    stencil = [cut(roll(c, -k * step)) for k in range(-2, 4)]
    pos = u >= 0.0
    a = jnp.where(pos, stencil[0], stencil[5])
    b = jnp.where(pos, stencil[1], stencil[4])
    m = jnp.where(pos, stencil[2], stencil[3])
    p = jnp.where(pos, stencil[3], stencil[2])
    q = jnp.where(pos, stencil[4], stencil[1])
    e0, f0 = a - 2.0 * b + m, a - 4.0 * b + 3.0 * m
    e1, f1 = b - 2.0 * m + p, b - p
    e2, f2 = m - 2.0 * p + q, 3.0 * m - 4.0 * p + q
    r0 = 1.0 / (EPS + (13.0 / 12.0 * e0 * e0 + 0.25 * f0 * f0))
    r1 = 1.0 / (EPS + (13.0 / 12.0 * e1 * e1 + 0.25 * f1 * f1))
    r2 = 1.0 / (EPS + (13.0 / 12.0 * e2 * e2 + 0.25 * f2 * f2))
    w0, w1, w2 = 0.1 * r0 * r0, 0.6 * r1 * r1, 0.3 * r2 * r2
    inv = 1.0 / (w0 + w1 + w2)
    w0, w1, w2 = w0 * inv, w1 * inv, w2 * inv
    v0 = (2.0 * a - 7.0 * b + 11.0 * m) * (1.0 / 6.0)
    v1 = (5.0 * m - b + 2.0 * p) * (1.0 / 6.0)
    v2 = (2.0 * m + 5.0 * p - q) * (1.0 / 6.0)
    value = w0 * v0 + w1 * v1 + w2 * v2
    w0, w1, w2 = w0 * u, w1 * u, w2 * u
    h0 = -2.0 * w0 * r0 * (v0 - value)
    h1 = -2.0 * w1 * r1 * (v1 - value)
    h2 = -2.0 * w2 * r2 * (v2 - value)
    e0, f0 = h0 * e0 * (13.0 / 6.0), h0 * f0 * 0.5
    e1, f1 = h1 * e1 * (13.0 / 6.0), h1 * f1 * 0.5
    e2, f2 = h2 * e2 * (13.0 / 6.0), h2 * f2 * 0.5
    w0, w1, w2 = w0 * (1.0 / 6.0), w1 * (1.0 / 6.0), w2 * (1.0 / 6.0)
    ga = 2.0 * w0 + e0 + f0
    gb = -7.0 * w0 - w1 - 2.0 * e0 - 4.0 * f0 + e1 + f1
    gm = 11.0 * w0 + 5.0 * w1 + 2.0 * w2 + e0 + 3.0 * f0 - 2.0 * e1 + e2 + 3.0 * f2
    gp = 2.0 * w1 + 5.0 * w2 + e1 - f1 - 2.0 * e2 - 4.0 * f2
    gq = e2 + f2 - w2
    zero = jnp.zeros_like(ga)
    return value, (
        jnp.where(pos, ga, zero),
        jnp.where(pos, gb, gq),
        jnp.where(pos, gm, gp),
        jnp.where(pos, gp, gm),
        jnp.where(pos, gq, gb),
        jnp.where(pos, zero, ga),
    )


def spread(f):
    return roll(f, 1) + roll(f, -1) + roll(f, 64) + roll(f, -64) - 4.0 * f


def kernel(
    ns, nt, nz, places,
    fu_h, fv_h, fw_h, fc_h, iu_h, iv_h, iw_h, it_h, dinv_h, vecs_h, minv_h, eig, packed_h, spec_h,
    ou, ov, ow, oc,
    raw, mats, packed, spec, rhs, u10, v14, w10, c18, iu10, iv10, iw14, it14, modal,
    xe, xw, xfw, xfe, yn2, ys2, yfs2, yfn2,
    s1, r1, s2, r2, s3, r3, s4, r4,
    ax, wx, ay, wy, ch, d_buf, vert,
    in_sem, h_send, h_recv, p_send, p_recv, ready,
):
    ng = nz // 2
    s, t = lax.axis_index("ys"), lax.axis_index("xs")
    index_of, pair_of, has = owners(nt, ng)
    owner = has(t)
    other = jnp.logical_not(owner)
    mine = pair_of(t)
    late = nt - ng

    loads = []
    for n, src in enumerate((iu_h, iv_h, iw_h, it_h, fc_h, fu_h, fv_h, fw_h)):
        dst = raw.at[n, pl.ds(1, ROWS), pl.ds(8, COLS)]
        loads.append(pltpu.make_async_copy(src, dst, in_sem.at[n]))
    loads.append(pltpu.make_async_copy(spec_h.at[s], spec, in_sem.at[8]))
    loads.append(pltpu.make_async_copy(packed_h, packed, in_sem.at[9]))
    for n, src in enumerate((vecs_h, minv_h, dinv_h)):
        loads.append(pltpu.make_async_copy(src, mats.at[n], in_sem.at[10 + n]))
    order = (10, 0, 1, 2, 9, 8, 3, 4, 5, 6, 7, 11, 12)
    for n in order:
        loads[n].start()

    barrier = pltpu.get_barrier_semaphore()

    def greet(a, b):
        pl.semaphore_signal(barrier, 1, device_id=(a, b), device_id_type=MESH)

    east, west = lax.rem(t + 1, nt), lax.rem(t + nt - 1, nt)
    north, south = lax.rem(s + 1, ns), lax.rem(s + ns - 1, ns)
    twin = t + 1 - 2 * lax.rem(t, 2)

    @pl.when(owner)
    def _():
        for i in range(nt - 1):
            greet(s, partner(t, i, nt))
        for i in range(1, ns):
            greet(lax.rem(s + i, ns), t)

    if late:

        @pl.when(other)
        def _():
            greet(north, t)
            greet(south, t)
            greet(s, twin)

    lane = lax.broadcasted_iota(jnp.int32, (nz, 128), 1)
    slot = lane & 63
    low = lane < 64
    core = (slot >= 8) & (slot < 40)
    lane_g = lax.broadcasted_iota(jnp.int32, (ng, 128), 1)
    level = lax.broadcasted_iota(jnp.int32, (nz, 640), 0)

    def rows(n, count):
        return pl.ds(pl.multiple_of(n * count, count), count)

    def tile(n):
        return slice(128 * n, 128 * n + 128)

    def table(n):
        first, end, width = places[n]
        return packed[first:end, :width]

    def place(n, buf, first):
        for k in range(5):
            v = raw[n, 2 * k : 2 * k + 2].reshape(128, nz)
            buf[:, tile(first + k)] = v.T

    def pack_x(fields, out):
        total = jnp.zeros((nz, 128), F32)
        for buf, first, col, at, count in fields:
            for k in range(4):
                if k == 0:
                    v = jnp.where(low, buf[:, tile(first + 4)], buf[:, tile(first)])
                else:
                    v = buf[:, tile(first + k)]
                to = 16 * k + at
                total = jnp.where((slot >= to) & (slot < to + count), roll(v, to - 8 - col), total)
        out[...] = total

    def unpack_x(src, fields):
        v = src[...]
        for buf, first, col, at, count in fields:
            here = (slot >= 8 + col) & (slot < 8 + col + count)
            for k in range(4):
                w = roll(v, 8 + col - 16 * k - at)
                if k == 0:
                    z = tile(first + 4)
                    buf[:, z] = jnp.where(here & low, w, buf[:, z])
                    z = tile(first)
                    buf[:, z] = jnp.where(here & ~low, w, buf[:, z])
                else:
                    z = tile(first + k)
                    buf[:, z] = jnp.where(here, w, buf[:, z])

    def pair(one, two):
        return jnp.where(core, one, roll(two, 32))

    def remote(src, dst, ds, dt, send, recv):
        return pltpu.make_async_remote_copy(
            src_ref=src, dst_ref=dst, send_sem=send, recv_sem=recv, device_id=(ds, dt), device_id_type=MESH
        )

    loads[0].wait()
    loads[1].wait()
    loads[2].wait()
    iu = raw[0, 1:9, 8:40].reshape(ROWS * COLS, nz)
    iv = raw[1, 1:9, 8:40].reshape(ROWS * COLS, nz)
    iw = raw[2, 1:9, 8:40].reshape(ROWS * COLS, nz)
    first_col = lax.broadcasted_iota(jnp.int32, iu.shape, 0) % COLS == 0
    before = jnp.where(first_col, 0.0, roll(iu, 1, 0))
    behind = jnp.concatenate([jnp.zeros((COLS, nz), F32), iv[: 7 * COLS]], 0)
    rhs[0:256, :] = (iu - before) + (iv - behind)
    rhs[256:288, :] = -iv[7 * COLS :]
    rhs[288:416, :] = jnp.zeros((128, nz), F32)
    for r in range(ROWS):
        at = 288 + 32 * (r % 4) + r // 4
        rhs[at : at + 1, :] = -raw[0, r + 1, 39:40, :]
    loads[10].wait()
    vt = mats[0].T
    next_vt = jnp.concatenate([vt[:, 1:], jnp.zeros((nz, 1), F32)], 1)
    main = dot_nt(vt, rhs[0:256, :]) + dot_nt(vt - next_vt, iw)
    extra = dot_nt(vt, rhs[256:416, :])
    modal[0] = main[:, :128]
    modal[1] = main[:, 128:]
    modal[2] = jnp.concatenate([extra[:, :32], jnp.zeros((nz, 96), F32)], 1)
    modal[3] = extra[:, 32:]
    for i in range(4):
        even = modal[i, pl.ds(0, ng, stride=2), :]
        odd = modal[i, pl.ds(1, ng, stride=2), :]
        if i < 2:
            s1[pl.ds(i, ng, stride=8), :] = even
            s1[pl.ds(2 + i, ng, stride=8), :] = odd
        elif i == 2:
            s1[pl.ds(4, ng, stride=8), :] = jnp.where(lane_g < 32, even, roll(odd, 32))
        else:
            s1[pl.ds(5, ng, stride=8), :] = jnp.where((lane_g & 31) < 2, even, roll(odd, 2))
            s1[pl.ds(6, ng, stride=8), :] = jnp.zeros((ng, 128), F32)
            s1[pl.ds(7, ng, stride=8), :] = jnp.zeros((ng, 128), F32)

    @pl.when(owner)
    def _():
        pl.semaphore_wait(barrier, ng - 1 + ns - 1)

    if late:

        @pl.when(other)
        def _():
            pl.semaphore_wait(barrier, ng + 3)

    def send1(to):
        @pl.when(has(to))
        def _():
            remote(s1.at[rows(pair_of(to), 8)], r1.at[rows(t, 8)], s, to, p_send.at[0], p_recv.at[0]).start()

    for i in range(nt - 1):
        send1(partner(t, i, nt))

    @pl.when(owner)
    def _():
        pltpu.make_async_copy(s1.at[rows(mine, 8)], r1.at[rows(t, 8)], p_recv.at[0]).start()

    if late:

        @pl.when(other)
        def _():
            def report(i, _):
                g = index_of(i)
                pl.semaphore_signal(ready, 1, device_id=(s, g), device_id_type=MESH)
                return 0

            lax.fori_loop(0, ng, report, 0)

    for n, buf, first in ((3, it14, 1), (4, c18, 2), (5, u10, 0), (6, v14, 1), (7, w10, 0)):
        loads[n].wait()
        place(n, buf, first)
    place(0, iu10, 0)
    place(1, iv10, 0)
    place(2, iw14, 1)

    pack_x(((iw14, 1, 29, 0, 3), (it14, 1, 29, 3, 3), (iu10, 0, 31, 6, 1), (iv10, 0, 31, 7, 1), (u10, 0, 29, 8, 3), (c18, 2, 27, 11, 5)), xe)
    pack_x(((iw14, 1, 0, 0, 3), (it14, 1, 0, 3, 3), (iu10, 0, 0, 6, 1), (iv10, 0, 0, 7, 1), (u10, 0, 0, 8, 2), (c18, 2, 0, 11, 5)), xw)
    for n in range(3):
        yn2[n] = pair(c18[:, tile(4 + n)], v14[:, tile(3 + n)])
        ys2[n] = pair(c18[:, tile(2 + n)], v14[:, tile(1 + n)])
    for n in range(2):
        yn2[3 + n] = pair(iw14[:, tile(4 + n)], it14[:, tile(4 + n)])
        ys2[3 + n] = pair(iw14[:, tile(1 + n)], it14[:, tile(1 + n)])
    yn2[5] = pair(iu10[:, tile(4)], iv10[:, tile(4)])
    ys2[5] = pair(iu10[:, tile(0)], iv10[:, tile(0)])
    halos = [
        remote(xe, xfw, s, east, h_send.at[0], h_recv.at[0]),
        remote(yn2, yfs2, north, t, h_send.at[1], h_recv.at[1]),
        remote(xw, xfe, s, west, h_send.at[2], h_recv.at[2]),
        remote(ys2, yfn2, south, t, h_send.at[3], h_recv.at[3]),
    ]
    halos[1].start()
    halos[3].start()
    loads[9].wait()

    @pl.when(owner)
    def _():
        pltpu.make_async_copy(r1, r1, p_recv.at[0]).wait()
        x = jnp.concatenate([r1[pl.ds(i, nt, stride=8), :] for i in range(5)], 1)
        y = dot(table(4), x)
        z = dot(table(5), r1[pl.ds(5, nt, stride=8), :])
        first = (lax.broadcasted_iota(jnp.int32, (nt, 128), 1) & 31) == 0
        at = lax.broadcasted_iota(jnp.int32, (ns, 128), 1)
        parts = [y[:, tile(i)] + jnp.where(first, roll(z, -i), 0.0) for i in range(4)]
        for q in range(2):
            for i in range(4):
                s2[pl.ds(4 * q + i, ns, stride=16), :] = parts[i][q * ns : (q + 1) * ns]
        s2[pl.ds(8, ns, stride=16), :] = jnp.where(at < 64, y[:ns, tile(4)], roll(y[ns:, tile(4)], 64))
        for i in range(9, 16):
            s2[pl.ds(i, ns, stride=16), :] = jnp.zeros((ns, 128), F32)

        for i in range(1, ns):
            j = lax.rem(s + i, ns)
            remote(s2.at[rows(j, 16)], r2.at[rows(s, 16)], j, t, p_send.at[1], p_recv.at[1]).start()
        pltpu.make_async_copy(s2.at[rows(s, 16)], r2.at[rows(s, 16)], p_recv.at[1]).start()

    if late:

        @pl.when(owner)
        def _():
            pl.semaphore_wait(ready, late)

    halos[0].start()
    halos[2].start()

    @pl.when(owner)
    def _():
        loads[8].wait()
        pltpu.make_async_copy(r2, r2, p_recv.at[1]).wait()
        part = [
            jnp.concatenate([r2[pl.ds(2 * n + i, ns, stride=16), :] for i in range(2)], 0) for n in range(4)
        ]
        group = lax.broadcasted_iota(jnp.int32, (2 * ns, 128), 1) // 32
        x = []
        for r in range(4):
            v = roll(part[0], -32 * r)
            for n in range(1, 4):
                v = jnp.where(group == n, roll(part[n], 32 * (n - r)), v)
            x.append(v)
        x = jnp.concatenate(x, 0)
        y = dot(table(2), x) + dot(table(3), r2[pl.ds(8, ns, stride=16), :])
        inner = spec[0:128, :]
        y = dot(y, inner)
        wide = lax.broadcasted_iota(jnp.int32, (1, 128), 1)
        own = jnp.where((wide & 32) == 0, eig[2 * mine], eig[2 * mine + 1])
        y = -y / (own + table(0) + spec[128:129, :])
        y = dot(table(1), dot_nt(y, inner))
        s3[...] = y

        for i in range(1, ns):
            j = lax.rem(s + i, ns)
            remote(s3.at[rows(j, 16)], r3.at[rows(s, 16)], j, t, p_send.at[2], p_recv.at[2]).start()
        pltpu.make_async_copy(s3.at[rows(s, 16)], r3.at[rows(s, 16)], p_recv.at[2]).start()

    diffusion = (0.0, 0.0, KAPPA, -KAPPA, 0.0, 0.0)
    halos[0].wait_recv()
    unpack_x(xfw, ((iw14, 1, -3, 0, 3), (it14, 1, -3, 3, 3), (iu10, 0, -1, 6, 1), (iv10, 0, -1, 7, 1), (u10, 0, -3, 8, 3), (c18, 2, -5, 11, 5)))
    halos[2].wait_recv()
    unpack_x(xfe, ((iw14, 1, 32, 0, 3), (it14, 1, 32, 3, 3), (iu10, 0, 32, 6, 1), (iv10, 0, 32, 7, 1), (u10, 0, 32, 8, 2), (c18, 2, 32, 11, 5)))

    def x_faces(n, _):
        at = pl.ds(pl.multiple_of(8 * n, 8), 8)
        value, parts = weno_parts(c18[at, 256:896], u10[at, :], 1, lambda f: f)
        wx[at, :] = DT * value
        for o in range(6):
            ax[o, at, :] = roll(DT * (parts[o] + diffusion[o]), o - 2)
        return 0

    lax.fori_loop(0, nz // 8, x_faces, 0)

    halos[1].wait_recv()
    halos[3].wait_recv()
    v = yfs2[5]
    iu10[:, tile(0)] = jnp.where(low, v, iu10[:, tile(0)])
    iv10[:, tile(0)] = jnp.where(low, roll(v, -32), iv10[:, tile(0)])
    v = yfn2[5]
    iu10[:, tile(4)] = jnp.where(low, iu10[:, tile(4)], v)
    iv10[:, tile(4)] = jnp.where(low, iv10[:, tile(4)], roll(v, -32))
    for n in range(3):
        v = yfs2[n]
        for buf, k, f in ((c18, n, v), (v14, n - 1, roll(v, -32))):
            if k >= 0:
                buf[:, tile(k)] = f if n < 2 else jnp.where(low, f, buf[:, tile(k)])
        v = yfn2[n]
        for buf, k, f in ((c18, 6 + n, v), (v14, 5 + n, roll(v, -32))):
            if k < buf.shape[1] // 128:
                buf[:, tile(k)] = f if n > 0 else jnp.where(low, buf[:, tile(k)], f)
    for n in range(2):
        v = yfs2[3 + n]
        for buf, f in ((iw14, v), (it14, roll(v, -32))):
            buf[:, tile(n)] = f if n < 1 else jnp.where(low, f, buf[:, tile(n)])
        v = yfn2[3 + n]
        for buf, f in ((iw14, v), (it14, roll(v, -32))):
            buf[:, tile(5 + n)] = f if n > 0 else jnp.where(low, buf[:, tile(5 + n)], f)

    def y_faces(n, _):
        at = pl.ds(pl.multiple_of(8 * n, 8), 8)
        value, parts = weno_parts(c18[at, :], v14[at, :], 64, lambda f: f[:, 128:1024])
        wy[at, :] = DT * value[:, 128:768]
        for o in range(6):
            ay[o, at, :] = roll(DT * (parts[o] + diffusion[o]), 64 * (o - 2))[:, 128:768]
        return 0

    lax.fori_loop(0, nz // 8, y_faces, 0)

    @pl.when(owner)
    def _():
        pltpu.make_async_copy(r3, r3, p_recv.at[2]).wait()
        left = lax.broadcasted_iota(jnp.int32, (ns, 128), 1) < 64
        cols = []
        for i in range(7):
            one = r3[pl.ds(2 * i, ns, stride=16), :]
            two = r3[pl.ds(2 * i + 1, ns, stride=16), :]
            cols.append(
                jnp.concatenate(
                    [
                        jnp.where(left, one, roll(two, 64)),
                        jnp.where(left, roll(one, 64), two),
                    ],
                    0,
                )
            )
        y = dot(table(6), jnp.concatenate(cols, 1))
        at = lax.broadcasted_iota(jnp.int32, (nt, 128), 1) & 31
        edge = jnp.zeros((nt, 128), F32)
        before, after = roll(y, 1, 0), roll(y, -1, 0)
        for i in range(7):
            s4[pl.ds(i, nt, stride=8), :] = y[:, tile(i)]
            if 1 <= i <= 5:
                k = 3 * (i - 1)
                edge = jnp.where((at >= k) & (at < k + 3), roll(before[:, tile(i)], k - 29), edge)
                edge = jnp.where((at >= 16 + k) & (at < 19 + k), roll(after[:, tile(i)], 16 + k), edge)
        s4[pl.ds(7, nt, stride=8), :] = edge

        for i in range(nt - 1):
            g = partner(t, i, nt)
            remote(s4.at[rows(g, 8)], r4.at[rows(mine, 8)], s, g, p_send.at[3], p_recv.at[3]).start()
        pltpu.make_async_copy(s4.at[rows(t, 8)], r4.at[rows(mine, 8)], p_recv.at[3]).start()

    c10 = c18[:, 256:896]
    ch[0] = jnp.where(level == nz - 1, 0.0, 0.5 * DT * (c10 + roll(c10, -1, 0)))
    ch[1] = jnp.where(level == nz - 1, 0.0, 0.5 * DT * w10[...])
    iw = iw14[:, 128:768]
    it14[...] = it14[...] + GRAV * DT * iw14[...]
    w10[...] = iw + DT * NU * spread(iw)
    iu10[...] = iu10[...] + DT * NU * spread(iu10[...])
    iv10[...] = iv10[...] + DT * NU * spread(iv10[...])
    loads[11].wait()
    loads[12].wait()
    vert[0] = jnp.concatenate([mats[1, pl.ds(0, ng, stride=2), :], mats[1, pl.ds(1, ng, stride=2), :]], 0).T
    vert[1] = mats[2].T

    pltpu.make_async_copy(r4, r4, p_recv.at[3]).wait()
    cols = []
    for i in range(8):
        one = r4[pl.ds(i, ng, stride=8), :]
        cols.append(jnp.concatenate([roll(one, 8), roll(one, -24)], 0))
    p = dot(vert[0], jnp.concatenate(cols, 1))
    edge = p[:, tile(7)]
    cols = []
    for i in range(7):
        v = p[:, tile(i)]
        if 1 <= i <= 5:
            k = 3 * (i - 1)
            v = jnp.where((slot >= 5) & (slot < 8), roll(edge, -3 - k), v)
            v = jnp.where((slot >= 40) & (slot < 43), roll(edge, 16 - k), v)
        cols.append(v)
    p = jnp.concatenate(cols, 1)
    top = lax.broadcasted_iota(jnp.int32, p.shape, 0) == nz - 1
    upper = jnp.where(top, 0.0, roll(p, -1, 0))
    d_buf[...] = dot(vert[1], it14[...] - GRAV * DT * (upper - p))
    p = p + DT * NU * spread(p)
    p10 = p[:, 128:768]
    ow[...] = w10[...] - (jnp.where(level == nz - 1, 0.0, roll(p10, -1, 0)) - p10)
    ou[...] = iu10[...] - (roll(p10, -1) - p10)
    ov[...] = iv10[...] - (roll(p, -64)[:, 128:768] - p10)
    d10 = d_buf[:, 128:768]
    gz = roll(d10, -1, 0) - d10
    wz = ch[1] * gz
    oc[...] = d10 + (wz + roll(wz, 1, 0))
    ow[...] = ow[...] + ch[0] * gz

    for n in range(nz // 8):
        at = slice(8 * n, 8 * n + 8)
        d14 = d_buf[at, :]
        dx = d14[:, 128:768]
        gx = roll(dx, -1) - dx
        ahead = roll(d14, -64)
        gy, gy_back = ahead - d14, d14 - roll(d14, 64)
        total = oc[at, :]
        for o in range(6):
            total = total + ax[o, at, :] * roll(gx, o - 2)
            first = 128 - 64 * (o - 2)
            g = gy if o % 2 == 0 else gy_back
            first = first if o % 2 == 0 else first + 64
            total = total + ay[o, at, :] * g[:, first : first + 640]
        ou[at, :] = ou[at, :] + wx[at, :] * gx
        ov[at, :] = ov[at, :] + wy[at, :] * gy[:, 128:768]
        oc[at, :] = total

    for copy in halos:
        copy.wait_send()

    @pl.when(owner)
    def _():
        for n, buf, count in ((0, s1, 8 * (ng - 1)), (1, s2, 16 * (ns - 1)), (2, s3, 16 * (ns - 1)), (3, s4, 8 * (nt - 1))):
            part = buf.at[pl.ds(0, count)]
            pltpu.make_async_copy(part, part, p_send.at[n]).wait()

    if late:

        @pl.when(other)
        def _():
            pltpu.make_async_copy(s1, s1, p_send.at[0]).wait()
            loads[8].wait()


def finish(a, b, c, d, out_a, out_b, out_c, out_d, made, sem):
    copies = []
    for n, (src, dst) in enumerate(((a, out_a), (b, out_b), (c, out_c), (d, out_d))):
        for k in range(5):
            v = src[:, 128 * k : 128 * k + 128].T
            if k > 0:
                made[n, 2 * k - 1] = v[8:40]
            if k < 4:
                made[n, 2 * k] = v[72:104]
        copies.append(pltpu.make_async_copy(made.at[n], dst, sem.at[n]))
        copies[n].start()
    for copy in copies:
        copy.wait()


def call(ns, nt, nz, consts, *args):
    ng = nz // 2
    packed, spectral, places = consts
    vmem, anywhere = pl.BlockSpec(memory_space=pltpu.VMEM), pl.BlockSpec(memory_space=pl.ANY)
    smem = pl.BlockSpec(memory_space=pltpu.SMEM)

    def buf(*shape):
        return pltpu.VMEM(shape, F32)

    out = jax.ShapeDtypeStruct((ROWS, COLS, nz), F32)
    made = pl.pallas_call(
        functools.partial(kernel, ns, nt, nz, places),
        out_shape=[pltpu.VMEM((nz, 640), F32)] * 4,
        in_specs=[anywhere] * 11 + [smem] + [anywhere] * 2,
        out_specs=[vmem] * 4,
        scratch_shapes=[
            buf(8, 10, 64, nz), buf(3, nz, nz), buf(*packed.shape), buf(136, 128), buf(416, nz),
            buf(nz, 640), buf(nz, 896), buf(nz, 640), buf(nz, 1152),
            buf(nz, 640), buf(nz, 640), buf(nz, 896), buf(nz, 896), buf(8, nz, 128),
            buf(nz, 128), buf(nz, 128), buf(nz, 128), buf(nz, 128),
            buf(6, nz, 128), buf(6, nz, 128), buf(6, nz, 128), buf(6, nz, 128),
            buf(8 * ng, 128), buf(8 * nt, 128), buf(16 * ns, 128), buf(16 * ns, 128),
            buf(16 * ns, 128), buf(16 * ns, 128), buf(8 * nt, 128), buf(8 * ng, 128),
            buf(6, nz, 640), buf(nz, 640), buf(6, nz, 640), buf(nz, 640), buf(2, nz, 640),
            buf(nz, 896), buf(2, nz, nz),
            pltpu.SemaphoreType.DMA((13,)), pltpu.SemaphoreType.DMA((4,)), pltpu.SemaphoreType.DMA((4,)),
            pltpu.SemaphoreType.DMA((4,)), pltpu.SemaphoreType.DMA((4,)), pltpu.SemaphoreType.REGULAR,
        ],
        compiler_params=pltpu.CompilerParams(
            collective_id=0, has_side_effects=True, vmem_limit_bytes=60 * 1024 * 1024
        ),
    )(*args, jnp.asarray(packed), jnp.asarray(spectral))
    return pl.pallas_call(
        finish,
        out_shape=[out] * 4,
        in_specs=[vmem] * 4,
        out_specs=[anywhere] * 4,
        scratch_shapes=[buf(4, ROWS, COLS, nz), pltpu.SemaphoreType.DMA((4,))],
    )(*[pltpu.with_memory_space_constraint(v, pltpu.VMEM) for v in made])


def solution(mesh):
    ns, nt = mesh.shape["ys"], mesh.shape["xs"]
    consts = tables(ns, nt)

    def shards(*args):
        flat = [v.transpose(1, 2, 0) for v in args[:8]]
        out = call(ns, nt, args[0].shape[0], consts, *flat, *args[8:])
        return tuple(v.transpose(2, 0, 1) for v in out)

    block = P(None, "ys", "xs")
    return jax.shard_map(
        shards, mesh=mesh, in_specs=(block,) * 8 + (P(),) * 4, out_specs=(block,) * 4, check_vma=False
    )
```

```python
import functools

import jax
import jax.numpy as jnp
import numpy as np
from jax import lax
from jax.experimental import pallas as pl
from jax.experimental.pallas import tpu as pltpu
from jax.sharding import PartitionSpec as P

MESH = pl.DeviceIdType.MESH
DT = 0.25
NU = 0.1
KAPPA = 0.1
GRAV = 1.0
EPS = 1e-6
F32 = jnp.float32
HI = lax.Precision.HIGHEST
ROWS, COLS = 8, 32


def tables(ns, nt):
    nx, ny = COLS * nt, ROWS * ns
    t = np.arange(nt)
    ring = np.zeros((2, ns, nt))
    ring[0, 0] = 1 / np.sqrt(nt)
    ring[1, 0] = (-1.0) ** t / np.sqrt(nt)
    for j in range(1, ns):
        ring[0, j] = np.sqrt(2 / nt) * np.cos(2 * np.pi * j * t / nt)
        ring[1, j] = np.sqrt(2 / nt) * np.sin(2 * np.pi * j * t / nt)

    def basis(n, k):
        z = np.arange(n)
        if k == 0 or 2 * k == n:
            return [np.cos(2 * np.pi * k * z / n) / np.sqrt(n)]
        return [
            np.sqrt(2 / n) * np.cos(2 * np.pi * k * z / n),
            np.sqrt(2 / n) * np.sin(2 * np.pi * k * z / n),
        ]

    inner = np.zeros((ns, 2, 2, COLS, 2, 2, COLS))
    lamx = np.zeros((ns, 2, 2, COLS))
    for j in range(ns):
        found, lam = [], []
        for k in range(nx // 2 + 1):
            res = k % nt
            own = res in (0, nt // 2) if j == 0 else res in (j, nt - j)
            if own:
                for vec in basis(nx, k):
                    found.append(np.einsum("qt,tc->qc", ring[:, j], vec.reshape(nt, COLS)))
                    lam.append(4 * np.sin(np.pi * k / nx) ** 2)
        block = np.stack(found, -1).reshape(2, COLS, 2, COLS)
        for m in range(2):
            inner[j, :, m, :, :, m, :] = block
            lamx[j, :, m, :] = np.array(lam).reshape(2, COLS)
    inner = inner.reshape(ns, 4 * COLS, 4 * COLS)
    lamx = np.broadcast_to(lamx.reshape(ns, 1, 4 * COLS), (ns, 8, 4 * COLS))
    spectral = np.concatenate([inner, lamx], 1)

    ybase, ylam = [], []
    for k in range(ny // 2 + 1):
        for vec in basis(ny, k):
            ybase.append(vec)
            ylam.append(4 * np.sin(np.pi * k / ny) ** 2)
    ybase = np.stack(ybase)
    lamy = np.broadcast_to(np.array(ylam)[:, None], (ny, 128))
    yfwd = ybase.reshape(ny, ns, 2, 4).transpose(0, 3, 2, 1).reshape(ny, ny)
    yinv = np.zeros((ns, 16, ny))
    for s in range(ns):
        for r in range(14):
            yinv[s, r] = ybase[:, (ROWS * s - 3 + r) % ny]
    after = ybase[:, (ROWS * np.arange(ns) + ROWS) % ny]
    ring = ring.reshape(nt, nt)
    parts = (lamy, yinv.reshape(16 * ns, ny), yfwd, after, ring, np.roll(ring, -1, 1), ring.T)
    packed = np.zeros((sum(len(v) for v in parts), 128))
    at, places = 0, []
    for v in parts:
        packed[at : at + len(v), : v.shape[1]] = v
        places.append((at, at + len(v), v.shape[1]))
        at += len(v)
    return packed.astype(np.float32), np.ascontiguousarray(spectral).astype(np.float32), tuple(places)


def owners(nt, ng):
    if (nt, ng) != (32, 24):
        return (lambda n: n), (lambda t: t), (lambda t: t < ng)

    def index_of(n):
        h = n // 2
        late = h // 8
        y = h - 8 * late
        y = y + late * 4 * (y // 2)
        return 4 * y + 2 * late + n % 2

    def pair_of(t):
        y, late = t // 4, (t // 2) % 2
        return 2 * (y - late * 4 * (y // 4)) + 16 * late + t % 2

    def has(t):
        y, late = t // 4, (t // 2) % 2
        return (late == 0) | ((y + 2) % 8 < 4)

    return index_of, pair_of, has


def partner(t, i, nt):
    if nt != 32:
        return lax.rem(t + 1 + i, nt)
    flip, step, turn = (31 - i) // 16, (4, 3, 5, 2, 6, 1, 7, 0)[i % 16 // 2], 1 - i % 2
    y, z, core = lax.div(t, 4), lax.rem(lax.div(t, 2), 2), lax.rem(t, 2)
    return 4 * lax.rem(y + step, 8) + 2 * lax.rem(z + flip, 2) + lax.rem(core + turn, 2)


def dot(a, b):
    return lax.dot_general(a, b, (((1,), (0,)), ((), ())), precision=HI, preferred_element_type=F32)


def dot_tn(a, b):
    return lax.dot_general(a, b, (((0,), (0,)), ((), ())), precision=HI, preferred_element_type=F32)


def dot_nt(a, b):
    return lax.dot_general(a, b, (((1,), (1,)), ((), ())), precision=HI, preferred_element_type=F32)


def roll(v, shift, axis=1):
    shift = shift % v.shape[axis]
    return v if shift == 0 else pltpu.roll(v, shift, axis)


def weno_parts(c, u, step, cut):
    stencil = [cut(roll(c, -k * step)) for k in range(-2, 4)]
    pos = u >= 0.0
    a = jnp.where(pos, stencil[0], stencil[5])
    b = jnp.where(pos, stencil[1], stencil[4])
    m = jnp.where(pos, stencil[2], stencil[3])
    p = jnp.where(pos, stencil[3], stencil[2])
    q = jnp.where(pos, stencil[4], stencil[1])
    e0, f0 = a - 2.0 * b + m, a - 4.0 * b + 3.0 * m
    e1, f1 = b - 2.0 * m + p, b - p
    e2, f2 = m - 2.0 * p + q, 3.0 * m - 4.0 * p + q
    r0 = 1.0 / (EPS + (13.0 / 12.0 * e0 * e0 + 0.25 * f0 * f0))
    r1 = 1.0 / (EPS + (13.0 / 12.0 * e1 * e1 + 0.25 * f1 * f1))
    r2 = 1.0 / (EPS + (13.0 / 12.0 * e2 * e2 + 0.25 * f2 * f2))
    w0, w1, w2 = 0.1 * r0 * r0, 0.6 * r1 * r1, 0.3 * r2 * r2
    inv = 1.0 / (w0 + w1 + w2)
    w0, w1, w2 = w0 * inv, w1 * inv, w2 * inv
    v0 = (2.0 * a - 7.0 * b + 11.0 * m) * (1.0 / 6.0)
    v1 = (5.0 * m - b + 2.0 * p) * (1.0 / 6.0)
    v2 = (2.0 * m + 5.0 * p - q) * (1.0 / 6.0)
    value = w0 * v0 + w1 * v1 + w2 * v2
    w0, w1, w2 = w0 * u, w1 * u, w2 * u
    h0 = -2.0 * w0 * r0 * (v0 - value)
    h1 = -2.0 * w1 * r1 * (v1 - value)
    h2 = -2.0 * w2 * r2 * (v2 - value)
    e0, f0 = h0 * e0 * (13.0 / 6.0), h0 * f0 * 0.5
    e1, f1 = h1 * e1 * (13.0 / 6.0), h1 * f1 * 0.5
    e2, f2 = h2 * e2 * (13.0 / 6.0), h2 * f2 * 0.5
    w0, w1, w2 = w0 * (1.0 / 6.0), w1 * (1.0 / 6.0), w2 * (1.0 / 6.0)
    ga = 2.0 * w0 + e0 + f0
    gb = -7.0 * w0 - w1 - 2.0 * e0 - 4.0 * f0 + e1 + f1
    gm = 11.0 * w0 + 5.0 * w1 + 2.0 * w2 + e0 + 3.0 * f0 - 2.0 * e1 + e2 + 3.0 * f2
    gp = 2.0 * w1 + 5.0 * w2 + e1 - f1 - 2.0 * e2 - 4.0 * f2
    gq = e2 + f2 - w2
    zero = jnp.zeros_like(ga)
    return value, (
        jnp.where(pos, ga, zero),
        jnp.where(pos, gb, gq),
        jnp.where(pos, gm, gp),
        jnp.where(pos, gp, gm),
        jnp.where(pos, gq, gb),
        jnp.where(pos, zero, ga),
    )


def spread(f):
    return roll(f, 1) + roll(f, -1) + roll(f, 64) + roll(f, -64) - 4.0 * f


def kernel(
    ns, nt, nz, places,
    fu_h, fv_h, fw_h, fc_h, iu_h, iv_h, iw_h, it_h, dinv_h, vecs_h, minv_h, eig_h, packed_h, spec_h,
    ou, ov, ow, oc,
    eig, raw, mats, packed, spec, rhs, u10, v14, w10, c18, iu10, iv10, iw14, it14, modal,
    xe, xw, xfw, xfe, yn2, ys2, yfs2, yfn2,
    s1, r1, s2, r2, s3, r3, s4, r4,
    ax, wx, ay, wy, ch, d_buf, vert, yfwd,
    in_sem, h_send, h_recv, p_send, p_recv, ready,
):
    ng = nz // 2
    s, t = lax.axis_index("ys"), lax.axis_index("xs")
    index_of, pair_of, has = owners(nt, ng)
    owner = has(t)
    other = jnp.logical_not(owner)
    mine = pair_of(t)
    late = nt - ng

    barrier = pltpu.get_barrier_semaphore()

    def greet(a, b):
        pl.semaphore_signal(barrier, 1, device_id=(a, b), device_id_type=MESH)

    east, west = lax.rem(t + 1, nt), lax.rem(t + nt - 1, nt)
    north, south = lax.rem(s + 1, ns), lax.rem(s + ns - 1, ns)
    twin = t + 1 - 2 * lax.rem(t, 2)

    @pl.when(owner)
    def _():
        for i in range(nt - 1):
            greet(s, partner(t, i, nt))
        for i in range(1, ns):
            greet(lax.rem(s + i, ns), t)

    if late:

        @pl.when(other)
        def _():
            greet(north, t)
            greet(south, t)
            greet(s, twin)

    loads = []
    for n, src in enumerate((iu_h, iv_h, iw_h, it_h, fc_h, fu_h, fv_h, fw_h)):
        dst = raw.at[n, pl.ds(1, ROWS), pl.ds(8, COLS)]
        loads.append(pltpu.make_async_copy(src, dst, in_sem.at[n]))
    loads.append(pltpu.make_async_copy(spec_h.at[s], spec, in_sem.at[8]))
    loads.append(pltpu.make_async_copy(packed_h, packed, in_sem.at[9]))
    for n, src in enumerate((vecs_h, minv_h, dinv_h)):
        loads.append(pltpu.make_async_copy(src, mats.at[n], in_sem.at[10 + n]))
    loads.append(pltpu.make_async_copy(eig_h, eig, in_sem.at[13]))
    order = (10, 0, 1, 2, 9, 8, 3, 4, 5, 6, 7, 11, 12, 13)
    for n in order:
        loads[n].start()

    lane = lax.broadcasted_iota(jnp.int32, (nz, 128), 1)
    slot = lane & 63
    low = lane < 64
    core = (slot >= 8) & (slot < 40)
    lane_g = lax.broadcasted_iota(jnp.int32, (ng, 128), 1)
    level = lax.broadcasted_iota(jnp.int32, (nz, 640), 0)

    def rows(n, count, used=None):
        return pl.ds(pl.multiple_of(n * count, count), used or count)

    def drain(buf, count, sem):
        part = buf.at[pl.ds(0, count)]
        pltpu.make_async_copy(part, part, sem).wait()

    def tile(n):
        return slice(128 * n, 128 * n + 128)

    def table(n):
        first, end, width = places[n]
        return packed[first:end, :width]

    def place(n, buf, first):
        for k in range(5):
            v = raw[n, 2 * k : 2 * k + 2].reshape(128, nz)
            buf[:, tile(first + k)] = v.T

    def pack_x(fields, out):
        total = jnp.zeros((nz, 128), F32)
        for buf, first, col, at, count in fields:
            for k in range(4):
                if k == 0:
                    v = jnp.where(low, buf[:, tile(first + 4)], buf[:, tile(first)])
                else:
                    v = buf[:, tile(first + k)]
                to = 16 * k + at
                total = jnp.where((slot >= to) & (slot < to + count), roll(v, to - 8 - col), total)
        out[...] = total

    def unpack_x(src, fields):
        v = src[...]
        for buf, first, col, at, count in fields:
            here = (slot >= 8 + col) & (slot < 8 + col + count)
            for k in range(4):
                w = roll(v, 8 + col - 16 * k - at)
                if k == 0:
                    z = tile(first + 4)
                    buf[:, z] = jnp.where(here & low, w, buf[:, z])
                    z = tile(first)
                    buf[:, z] = jnp.where(here & ~low, w, buf[:, z])
                else:
                    z = tile(first + k)
                    buf[:, z] = jnp.where(here, w, buf[:, z])

    def pair(one, two):
        return jnp.where(core, one, roll(two, 32))

    def remote(src, dst, ds, dt, send, recv):
        return pltpu.make_async_remote_copy(
            src_ref=src, dst_ref=dst, send_sem=send, recv_sem=recv, device_id=(ds, dt), device_id_type=MESH
        )

    loads[0].wait()
    loads[1].wait()
    loads[2].wait()
    iu = raw[0, 1:9, 8:40].reshape(ROWS * COLS, nz)
    iv = raw[1, 1:9, 8:40].reshape(ROWS * COLS, nz)
    iw = raw[2, 1:9, 8:40].reshape(ROWS * COLS, nz)
    first_col = lax.broadcasted_iota(jnp.int32, iu.shape, 0) % COLS == 0
    before = jnp.where(first_col, 0.0, roll(iu, 1, 0))
    behind = jnp.concatenate([jnp.zeros((COLS, nz), F32), iv[: 7 * COLS]], 0)
    rhs[0:256, :] = (iu - before) + (iv - behind)
    rhs[256:288, :] = -iv[7 * COLS :]
    rhs[288:416, :] = jnp.zeros((128, nz), F32)
    for r in range(ROWS):
        at = 288 + 32 * (r % 4) + r // 4
        rhs[at : at + 1, :] = -raw[0, r + 1, 39:40, :]
    loads[10].wait()
    vt = mats[0].T
    next_vt = jnp.concatenate([vt[:, 1:], jnp.zeros((nz, 1), F32)], 1)
    both = dot_nt(vt, rhs[...])
    main, extra = both[:, :256] + dot_nt(vt - next_vt, iw), both[:, 256:]
    modal[0] = main[:, :128]
    modal[1] = main[:, 128:]
    modal[2] = jnp.concatenate([extra[:, :32], jnp.zeros((nz, 96), F32)], 1)
    modal[3] = extra[:, 32:]
    for i in range(4):
        even = modal[i, pl.ds(0, ng, stride=2), :]
        odd = modal[i, pl.ds(1, ng, stride=2), :]
        if i < 2:
            s1[pl.ds(i, ng, stride=8), :] = even
            s1[pl.ds(2 + i, ng, stride=8), :] = odd
        elif i == 2:
            s1[pl.ds(4, ng, stride=8), :] = jnp.where(lane_g < 32, even, roll(odd, 32))
        else:
            s1[pl.ds(5, ng, stride=8), :] = jnp.where((lane_g & 31) < 2, even, roll(odd, 2))

    @pl.when(owner)
    def _():
        pl.semaphore_wait(barrier, ng - 1 + ns - 1)

    if late:

        @pl.when(other)
        def _():
            pl.semaphore_wait(barrier, ng + 3)

    def send1(to):
        @pl.when(has(to))
        def _():
            remote(s1.at[rows(pair_of(to), 8, 6)], r1.at[rows(t, 8, 6)], s, to, p_send.at[0], p_recv.at[0]).start()

    for i in range(nt - 1):
        send1(partner(t, i, nt))

    @pl.when(owner)
    def _():
        pltpu.make_async_copy(s1.at[rows(mine, 8, 6)], r1.at[rows(t, 8, 6)], p_recv.at[0]).start()

    if late:

        @pl.when(other)
        def _():
            def report(i, _):
                g = index_of(i)
                pl.semaphore_signal(ready, 1, device_id=(s, g), device_id_type=MESH)
                return 0

            lax.fori_loop(0, ng, report, 0)

    for n, buf, first in ((3, it14, 1), (4, c18, 2), (5, u10, 0), (6, v14, 1), (7, w10, 0)):
        loads[n].wait()
        place(n, buf, first)
    place(0, iu10, 0)
    place(1, iv10, 0)
    place(2, iw14, 1)

    pack_x(((iw14, 1, 29, 0, 3), (it14, 1, 29, 3, 3), (iu10, 0, 31, 6, 1), (iv10, 0, 31, 7, 1), (u10, 0, 29, 8, 3), (c18, 2, 27, 11, 5)), xe)
    pack_x(((iw14, 1, 0, 0, 3), (it14, 1, 0, 3, 3), (iu10, 0, 0, 6, 1), (iv10, 0, 0, 7, 1), (u10, 0, 0, 8, 2), (c18, 2, 0, 11, 5)), xw)
    for n in range(3):
        yn2[n] = pair(c18[:, tile(4 + n)], v14[:, tile(3 + n)])
        ys2[n] = pair(c18[:, tile(2 + n)], v14[:, tile(1 + n)])
    for n in range(2):
        yn2[3 + n] = pair(iw14[:, tile(4 + n)], it14[:, tile(4 + n)])
        ys2[3 + n] = pair(iw14[:, tile(1 + n)], it14[:, tile(1 + n)])
    yn2[5] = pair(iu10[:, tile(4)], iv10[:, tile(4)])
    ys2[5] = pair(iu10[:, tile(0)], iv10[:, tile(0)])
    halos = [
        remote(xe, xfw, s, east, h_send.at[0], h_recv.at[0]),
        remote(yn2, yfs2, north, t, h_send.at[1], h_recv.at[1]),
        remote(xw, xfe, s, west, h_send.at[2], h_recv.at[2]),
        remote(ys2, yfn2, south, t, h_send.at[3], h_recv.at[3]),
    ]
    halos[1].start()
    halos[3].start()
    loads[9].wait()
    yfwd[...] = jnp.concatenate([table(2), table(3)], 1)

    @pl.when(owner)
    def _():
        drain(r1, 6 * nt, p_recv.at[0])
        x = jnp.concatenate([r1[pl.ds(i, nt, stride=8), :] for i in range(5)], 1)
        y = dot(table(4), x)
        z = dot(table(5), r1[pl.ds(5, nt, stride=8), :])
        first = (lax.broadcasted_iota(jnp.int32, (nt, 128), 1) & 31) == 0
        at = lax.broadcasted_iota(jnp.int32, (ns, 128), 1)
        parts = [y[:, tile(i)] + jnp.where(first, roll(z, -i), 0.0) for i in range(4)]
        for q in range(2):
            for i in range(4):
                s2[pl.ds(4 * q + i, ns, stride=16), :] = parts[i][q * ns : (q + 1) * ns]
        s2[pl.ds(8, ns, stride=16), :] = jnp.where(at < 64, y[:ns, tile(4)], roll(y[ns:, tile(4)], 64))

        for i in range(1, ns):
            j = lax.rem(s + i, ns)
            remote(s2.at[rows(j, 16, 9)], r2.at[rows(s, 16, 9)], j, t, p_send.at[1], p_recv.at[1]).start()
        pltpu.make_async_copy(s2.at[rows(s, 16, 9)], r2.at[rows(s, 16, 9)], p_recv.at[1]).start()

    if late:

        @pl.when(owner)
        def _():
            pl.semaphore_wait(ready, late)

    halos[0].start()
    halos[2].start()

    diffusion = (0.0, 0.0, KAPPA, -KAPPA, 0.0, 0.0)
    halos[1].wait_recv()
    halos[3].wait_recv()
    v = yfs2[5]
    iu10[:, tile(0)] = jnp.where(low, v, iu10[:, tile(0)])
    iv10[:, tile(0)] = jnp.where(low, roll(v, -32), iv10[:, tile(0)])
    v = yfn2[5]
    iu10[:, tile(4)] = jnp.where(low, iu10[:, tile(4)], v)
    iv10[:, tile(4)] = jnp.where(low, iv10[:, tile(4)], roll(v, -32))
    for n in range(3):
        v = yfs2[n]
        for buf, k, f in ((c18, n, v), (v14, n - 1, roll(v, -32))):
            if k >= 0:
                buf[:, tile(k)] = f if n < 2 else jnp.where(low, f, buf[:, tile(k)])
        v = yfn2[n]
        for buf, k, f in ((c18, 6 + n, v), (v14, 5 + n, roll(v, -32))):
            if k < buf.shape[1] // 128:
                buf[:, tile(k)] = f if n > 0 else jnp.where(low, buf[:, tile(k)], f)
    for n in range(2):
        v = yfs2[3 + n]
        for buf, f in ((iw14, v), (it14, roll(v, -32))):
            buf[:, tile(n)] = f if n < 1 else jnp.where(low, f, buf[:, tile(n)])
        v = yfn2[3 + n]
        for buf, f in ((iw14, v), (it14, roll(v, -32))):
            buf[:, tile(5 + n)] = f if n > 0 else jnp.where(low, buf[:, tile(5 + n)], f)

    def y_faces(n, _):
        at = pl.ds(pl.multiple_of(8 * n, 8), 8)
        value, parts = weno_parts(c18[at, :], v14[at, :], 64, lambda f: f[:, 128:1024])
        wy[at, :] = DT * value[:, 128:768]
        for o in range(6):
            ay[o, at, :] = roll(DT * (parts[o] + diffusion[o]), 64 * (o - 2))[:, 128:768]
        return 0

    lax.fori_loop(0, nz // 8, y_faces, 0)

    @pl.when(owner)
    def _():
        loads[8].wait()
        loads[13].wait()
        drain(r2, 9 * ns, p_recv.at[1])
        part = [
            jnp.concatenate([r2[pl.ds(2 * n + i, ns, stride=16), :] for i in range(2)], 0) for n in range(4)
        ]
        group = lax.broadcasted_iota(jnp.int32, (2 * ns, 128), 1) // 32
        x = []
        for r in range(4):
            v = roll(part[0], -32 * r)
            for n in range(1, 4):
                v = jnp.where(group == n, roll(part[n], 32 * (n - r)), v)
            x.append(v)
        x.append(r2[pl.ds(8, ns, stride=16), :])
        y = dot(yfwd[...], jnp.concatenate(x, 0))
        inner = spec[0:128, :]
        y = dot(y, inner)
        wide = lax.broadcasted_iota(jnp.int32, (1, 128), 1)
        own = jnp.where((wide & 32) == 0, eig[2 * mine], eig[2 * mine + 1])
        y = -y / (own + table(0) + spec[128:129, :])
        y = dot(table(1), dot_nt(y, inner))
        s3[...] = y

        for i in range(1, ns):
            j = lax.rem(s + i, ns)
            remote(s3.at[rows(j, 16, 14)], r3.at[rows(s, 16, 14)], j, t, p_send.at[2], p_recv.at[2]).start()
        pltpu.make_async_copy(s3.at[rows(s, 16, 14)], r3.at[rows(s, 16, 14)], p_recv.at[2]).start()

    halos[0].wait_recv()
    unpack_x(xfw, ((iw14, 1, -3, 0, 3), (it14, 1, -3, 3, 3), (iu10, 0, -1, 6, 1), (iv10, 0, -1, 7, 1), (u10, 0, -3, 8, 3), (c18, 2, -5, 11, 5)))
    halos[2].wait_recv()
    unpack_x(xfe, ((iw14, 1, 32, 0, 3), (it14, 1, 32, 3, 3), (iu10, 0, 32, 6, 1), (iv10, 0, 32, 7, 1), (u10, 0, 32, 8, 2), (c18, 2, 32, 11, 5)))

    def x_faces(n, _):
        at = pl.ds(pl.multiple_of(8 * n, 8), 8)
        value, parts = weno_parts(c18[at, 256:896], u10[at, :], 1, lambda f: f)
        wx[at, :] = DT * value
        for o in range(6):
            ax[o, at, :] = roll(DT * (parts[o] + diffusion[o]), o - 2)
        return 0

    lax.fori_loop(0, nz // 8, x_faces, 0)

    @pl.when(owner)
    def _():
        drain(r3, 14 * ns, p_recv.at[2])
        left = lax.broadcasted_iota(jnp.int32, (ns, 128), 1) < 64
        cols = []
        for i in range(7):
            one = r3[pl.ds(2 * i, ns, stride=16), :]
            two = r3[pl.ds(2 * i + 1, ns, stride=16), :]
            cols.append(
                jnp.concatenate(
                    [
                        jnp.where(left, one, roll(two, 64)),
                        jnp.where(left, roll(one, 64), two),
                    ],
                    0,
                )
            )
        y = dot(table(6), jnp.concatenate(cols, 1))
        at = lax.broadcasted_iota(jnp.int32, (nt, 128), 1) & 31
        edge = jnp.zeros((nt, 128), F32)
        before, after = roll(y, 1, 0), roll(y, -1, 0)
        for i in range(7):
            s4[pl.ds(i, nt, stride=8), :] = y[:, tile(i)]
            if 1 <= i <= 5:
                k = 3 * (i - 1)
                edge = jnp.where((at >= k) & (at < k + 3), roll(before[:, tile(i)], k - 29), edge)
                edge = jnp.where((at >= 16 + k) & (at < 19 + k), roll(after[:, tile(i)], 16 + k), edge)
        s4[pl.ds(7, nt, stride=8), :] = edge

        for i in range(nt - 1):
            g = partner(t, i, nt)
            remote(s4.at[rows(g, 8)], r4.at[rows(mine, 8)], s, g, p_send.at[3], p_recv.at[3]).start()
        pltpu.make_async_copy(s4.at[rows(t, 8)], r4.at[rows(mine, 8)], p_recv.at[3]).start()

    c10 = c18[:, 256:896]
    ch[0] = jnp.where(level == nz - 1, 0.0, 0.5 * DT * (c10 + roll(c10, -1, 0)))
    ch[1] = jnp.where(level == nz - 1, 0.0, 0.5 * DT * w10[...])
    iw = iw14[:, 128:768]
    it14[...] = it14[...] + GRAV * DT * iw14[...]
    w10[...] = iw + DT * NU * spread(iw)
    iu10[...] = iu10[...] + DT * NU * spread(iu10[...])
    iv10[...] = iv10[...] + DT * NU * spread(iv10[...])
    for n in (11, 12):
        loads[n].wait()
    vert[0] = jnp.concatenate([mats[1, pl.ds(0, ng, stride=2), :], mats[1, pl.ds(1, ng, stride=2), :]], 0).T
    vert[1] = mats[2].T

    pltpu.make_async_copy(r4, r4, p_recv.at[3]).wait()
    cols = []
    for i in range(8):
        one = r4[pl.ds(i, ng, stride=8), :]
        cols.append(jnp.concatenate([roll(one, 8), roll(one, -24)], 0))
    p = dot(vert[0], jnp.concatenate(cols, 1))
    edge = p[:, tile(7)]
    cols = []
    for i in range(7):
        v = p[:, tile(i)]
        if 1 <= i <= 5:
            k = 3 * (i - 1)
            v = jnp.where((slot >= 5) & (slot < 8), roll(edge, -3 - k), v)
            v = jnp.where((slot >= 40) & (slot < 43), roll(edge, 16 - k), v)
        cols.append(v)
    p = jnp.concatenate(cols, 1)
    top = lax.broadcasted_iota(jnp.int32, p.shape, 0) == nz - 1
    upper = jnp.where(top, 0.0, roll(p, -1, 0))
    d_buf[...] = dot(vert[1], it14[...] - GRAV * DT * (upper - p))
    p = p + DT * NU * spread(p)
    p10 = p[:, 128:768]
    ow[...] = w10[...] - (jnp.where(level == nz - 1, 0.0, roll(p10, -1, 0)) - p10)
    ou[...] = iu10[...] - (roll(p10, -1) - p10)
    ov[...] = iv10[...] - (roll(p, -64)[:, 128:768] - p10)
    d10 = d_buf[:, 128:768]
    gz = roll(d10, -1, 0) - d10
    wz = ch[1] * gz
    oc[...] = d10 + (wz + roll(wz, 1, 0))
    ow[...] = ow[...] + ch[0] * gz

    for n in range(nz // 8):
        at = slice(8 * n, 8 * n + 8)
        d14 = d_buf[at, :]
        dx = d14[:, 128:768]
        gx = roll(dx, -1) - dx
        ahead = roll(d14, -64)
        gy, gy_back = ahead - d14, d14 - roll(d14, 64)
        total = oc[at, :]
        for o in range(6):
            total = total + ax[o, at, :] * roll(gx, o - 2)
            first = 128 - 64 * (o - 2)
            g = gy if o % 2 == 0 else gy_back
            first = first if o % 2 == 0 else first + 64
            total = total + ay[o, at, :] * g[:, first : first + 640]
        ou[at, :] = ou[at, :] + wx[at, :] * gx
        ov[at, :] = ov[at, :] + wy[at, :] * gy[:, 128:768]
        oc[at, :] = total

    for copy in halos:
        copy.wait_send()

    @pl.when(owner)
    def _():
        for n, buf, count in ((0, s1, 6 * (ng - 1)), (1, s2, 9 * (ns - 1)), (2, s3, 14 * (ns - 1)), (3, s4, 8 * (nt - 1))):
            drain(buf, count, p_send.at[n])

    if late:

        @pl.when(other)
        def _():
            drain(s1, 6 * ng, p_send.at[0])
            loads[13].wait()
            loads[8].wait()


def finish(a, b, c, d, out_a, out_b, out_c, out_d, made, sem):
    copies = []
    for n, (src, dst) in enumerate(((a, out_a), (b, out_b), (c, out_c), (d, out_d))):
        for k in range(5):
            v = src[:, 128 * k : 128 * k + 128].T
            if k > 0:
                made[n, 2 * k - 1] = v[8:40]
            if k < 4:
                made[n, 2 * k] = v[72:104]
        copies.append(pltpu.make_async_copy(made.at[n], dst, sem.at[n]))
        copies[n].start()
    for copy in copies:
        copy.wait()


def call(ns, nt, nz, consts, *args):
    ng = nz // 2
    packed, spectral, places = consts
    vmem, anywhere = pl.BlockSpec(memory_space=pltpu.VMEM), pl.BlockSpec(memory_space=pl.ANY)

    def buf(*shape):
        return pltpu.VMEM(shape, F32)

    out = jax.ShapeDtypeStruct((ROWS, COLS, nz), F32)
    made = pl.pallas_call(
        functools.partial(kernel, ns, nt, nz, places),
        out_shape=[pltpu.VMEM((nz, 640), F32)] * 4,
        in_specs=[anywhere] * 14,
        out_specs=[vmem] * 4,
        scratch_shapes=[
            pltpu.SMEM((nz,), F32), buf(8, 10, 64, nz), buf(3, nz, nz), buf(*packed.shape), buf(136, 128), buf(416, nz),
            buf(nz, 640), buf(nz, 896), buf(nz, 640), buf(nz, 1152),
            buf(nz, 640), buf(nz, 640), buf(nz, 896), buf(nz, 896), buf(8, nz, 128),
            buf(nz, 128), buf(nz, 128), buf(nz, 128), buf(nz, 128),
            buf(6, nz, 128), buf(6, nz, 128), buf(6, nz, 128), buf(6, nz, 128),
            buf(8 * ng, 128), buf(8 * nt, 128), buf(16 * ns, 128), buf(16 * ns, 128),
            buf(16 * ns, 128), buf(16 * ns, 128), buf(8 * nt, 128), buf(8 * ng, 128),
            buf(6, nz, 640), buf(nz, 640), buf(6, nz, 640), buf(nz, 640), buf(2, nz, 640),
            buf(nz, 896), buf(2, nz, nz), buf(ROWS * ns, ROWS * ns + ns),
            pltpu.SemaphoreType.DMA((14,)), pltpu.SemaphoreType.DMA((4,)), pltpu.SemaphoreType.DMA((4,)),
            pltpu.SemaphoreType.DMA((4,)), pltpu.SemaphoreType.DMA((4,)), pltpu.SemaphoreType.REGULAR,
        ],
        compiler_params=pltpu.CompilerParams(
            collective_id=0, has_side_effects=True, vmem_limit_bytes=60 * 1024 * 1024
        ),
    )(*args, jnp.asarray(packed), jnp.asarray(spectral))
    return pl.pallas_call(
        finish,
        out_shape=[out] * 4,
        in_specs=[vmem] * 4,
        out_specs=[anywhere] * 4,
        scratch_shapes=[buf(4, ROWS, COLS, nz), pltpu.SemaphoreType.DMA((4,))],
    )(*[pltpu.with_memory_space_constraint(v, pltpu.VMEM) for v in made])


def solution(mesh):
    ns, nt = mesh.shape["ys"], mesh.shape["xs"]
    consts = tables(ns, nt)

    def shards(*args):
        flat = [v.transpose(1, 2, 0) for v in args[:8]]
        out = call(ns, nt, args[0].shape[0], consts, *flat, *args[8:])
        return tuple(v.transpose(2, 0, 1) for v in out)

    block = P(None, "ys", "xs")
    return jax.shard_map(
        shards, mesh=mesh, in_specs=(block,) * 8 + (P(),) * 4, out_specs=(block,) * 4, check_vma=False
    )
```

```python
import functools

import jax
import jax.numpy as jnp
import numpy as np
from jax import lax
from jax.experimental import pallas as pl
from jax.experimental.pallas import tpu as pltpu
from jax.sharding import PartitionSpec as P

MESH = pl.DeviceIdType.MESH
DT = 0.25
NU = 0.1
KAPPA = 0.1
GRAV = 1.0
EPS = 1e-6
F32 = jnp.float32
HI = lax.Precision.HIGHEST
ROWS, COLS = 8, 32


def tables(ns, nt):
    nx, ny = COLS * nt, ROWS * ns
    t = np.arange(nt)
    ring = np.zeros((2, ns, nt))
    ring[0, 0] = 1 / np.sqrt(nt)
    ring[1, 0] = (-1.0) ** t / np.sqrt(nt)
    for j in range(1, ns):
        ring[0, j] = np.sqrt(2 / nt) * np.cos(2 * np.pi * j * t / nt)
        ring[1, j] = np.sqrt(2 / nt) * np.sin(2 * np.pi * j * t / nt)

    def basis(n, k):
        z = np.arange(n)
        if k == 0 or 2 * k == n:
            return [np.cos(2 * np.pi * k * z / n) / np.sqrt(n)]
        return [
            np.sqrt(2 / n) * np.cos(2 * np.pi * k * z / n),
            np.sqrt(2 / n) * np.sin(2 * np.pi * k * z / n),
        ]

    inner = np.zeros((ns, 2, 2, COLS, 2, 2, COLS))
    lamx = np.zeros((ns, 2, 2, COLS))
    for j in range(ns):
        found, lam = [], []
        for k in range(nx // 2 + 1):
            res = k % nt
            own = res in (0, nt // 2) if j == 0 else res in (j, nt - j)
            if own:
                for vec in basis(nx, k):
                    found.append(np.einsum("qt,tc->qc", ring[:, j], vec.reshape(nt, COLS)))
                    lam.append(4 * np.sin(np.pi * k / nx) ** 2)
        block = np.stack(found, -1).reshape(2, COLS, 2, COLS)
        for m in range(2):
            inner[j, :, m, :, :, m, :] = block
            lamx[j, :, m, :] = np.array(lam).reshape(2, COLS)
    inner = inner.reshape(ns, 4 * COLS, 4 * COLS)
    lamx = np.broadcast_to(lamx.reshape(ns, 1, 4 * COLS), (ns, 8, 4 * COLS))
    spectral = np.concatenate([inner, lamx], 1)

    ybase, ylam = [], []
    for k in range(ny // 2 + 1):
        for vec in basis(ny, k):
            ybase.append(vec)
            ylam.append(4 * np.sin(np.pi * k / ny) ** 2)
    ybase = np.stack(ybase)
    lamy = np.broadcast_to(np.array(ylam)[:, None], (ny, 128))
    yfwd = ybase.reshape(ny, ns, 2, 4).transpose(0, 3, 2, 1).reshape(ny, ny)
    yinv = np.zeros((ns, 16, ny))
    for s in range(ns):
        for r in range(14):
            yinv[s, r] = ybase[:, (ROWS * s - 3 + r) % ny]
    after = ybase[:, (ROWS * np.arange(ns) + ROWS) % ny]
    ring = ring.reshape(nt, nt)
    parts = (lamy, yinv.reshape(16 * ns, ny), yfwd, after, ring, np.roll(ring, -1, 1), ring.T)
    packed = np.zeros((sum(len(v) for v in parts), 128))
    at, places = 0, []
    for v in parts:
        packed[at : at + len(v), : v.shape[1]] = v
        places.append((at, at + len(v), v.shape[1]))
        at += len(v)
    return packed.astype(np.float32), np.ascontiguousarray(spectral).astype(np.float32), tuple(places)


def owners(nt, ng):
    if (nt, ng) != (32, 24):
        return (lambda n: n), (lambda t: t), (lambda t: t < ng)

    def index_of(n):
        h = n // 2
        late = h // 8
        y = h - 8 * late
        y = y + late * 4 * (y // 2)
        return 4 * y + 2 * late + n % 2

    def pair_of(t):
        y, late = t // 4, (t // 2) % 2
        return 2 * (y - late * 4 * (y // 4)) + 16 * late + t % 2

    def has(t):
        y, late = t // 4, (t // 2) % 2
        return (late == 0) | ((y + 2) % 8 < 4)

    return index_of, pair_of, has


def partner(t, i, nt):
    if nt != 32:
        return lax.rem(t + 1 + i, nt)
    flip, step, turn = (31 - i) // 16, (4, 3, 5, 2, 6, 1, 7, 0)[i % 16 // 2], 1 - i % 2
    y, z, core = lax.div(t, 4), lax.rem(lax.div(t, 2), 2), lax.rem(t, 2)
    return 4 * lax.rem(y + step, 8) + 2 * lax.rem(z + flip, 2) + lax.rem(core + turn, 2)


def dot(a, b):
    return lax.dot_general(a, b, (((1,), (0,)), ((), ())), precision=HI, preferred_element_type=F32)


def dot_tn(a, b):
    return lax.dot_general(a, b, (((0,), (0,)), ((), ())), precision=HI, preferred_element_type=F32)


def dot_nt(a, b):
    return lax.dot_general(a, b, (((1,), (1,)), ((), ())), precision=HI, preferred_element_type=F32)


def roll(v, shift, axis=1):
    shift = shift % v.shape[axis]
    return v if shift == 0 else pltpu.roll(v, shift, axis)


def weno_parts(c, u, step, cut):
    stencil = [cut(roll(c, -k * step)) for k in range(-2, 4)]
    pos = u >= 0.0
    a = jnp.where(pos, stencil[0], stencil[5])
    b = jnp.where(pos, stencil[1], stencil[4])
    m = jnp.where(pos, stencil[2], stencil[3])
    p = jnp.where(pos, stencil[3], stencil[2])
    q = jnp.where(pos, stencil[4], stencil[1])
    e0, f0 = a - 2.0 * b + m, a - 4.0 * b + 3.0 * m
    e1, f1 = b - 2.0 * m + p, b - p
    e2, f2 = m - 2.0 * p + q, 3.0 * m - 4.0 * p + q
    r0 = 1.0 / (EPS + (13.0 / 12.0 * e0 * e0 + 0.25 * f0 * f0))
    r1 = 1.0 / (EPS + (13.0 / 12.0 * e1 * e1 + 0.25 * f1 * f1))
    r2 = 1.0 / (EPS + (13.0 / 12.0 * e2 * e2 + 0.25 * f2 * f2))
    w0, w1, w2 = 0.1 * r0 * r0, 0.6 * r1 * r1, 0.3 * r2 * r2
    inv = 1.0 / (w0 + w1 + w2)
    w0, w1, w2 = w0 * inv, w1 * inv, w2 * inv
    v0 = (2.0 * a - 7.0 * b + 11.0 * m) * (1.0 / 6.0)
    v1 = (5.0 * m - b + 2.0 * p) * (1.0 / 6.0)
    v2 = (2.0 * m + 5.0 * p - q) * (1.0 / 6.0)
    value = w0 * v0 + w1 * v1 + w2 * v2
    w0, w1, w2 = w0 * u, w1 * u, w2 * u
    h0 = -2.0 * w0 * r0 * (v0 - value)
    h1 = -2.0 * w1 * r1 * (v1 - value)
    h2 = -2.0 * w2 * r2 * (v2 - value)
    e0, f0 = h0 * e0 * (13.0 / 6.0), h0 * f0 * 0.5
    e1, f1 = h1 * e1 * (13.0 / 6.0), h1 * f1 * 0.5
    e2, f2 = h2 * e2 * (13.0 / 6.0), h2 * f2 * 0.5
    w0, w1, w2 = w0 * (1.0 / 6.0), w1 * (1.0 / 6.0), w2 * (1.0 / 6.0)
    ga = 2.0 * w0 + e0 + f0
    gb = -7.0 * w0 - w1 - 2.0 * e0 - 4.0 * f0 + e1 + f1
    gm = 11.0 * w0 + 5.0 * w1 + 2.0 * w2 + e0 + 3.0 * f0 - 2.0 * e1 + e2 + 3.0 * f2
    gp = 2.0 * w1 + 5.0 * w2 + e1 - f1 - 2.0 * e2 - 4.0 * f2
    gq = e2 + f2 - w2
    zero = jnp.zeros_like(ga)
    return value, (
        jnp.where(pos, ga, zero),
        jnp.where(pos, gb, gq),
        jnp.where(pos, gm, gp),
        jnp.where(pos, gp, gm),
        jnp.where(pos, gq, gb),
        jnp.where(pos, zero, ga),
    )


def spread(f):
    return roll(f, 1) + roll(f, -1) + roll(f, 64) + roll(f, -64) - 4.0 * f


def kernel(
    ns, nt, nz, places,
    fu_h, fv_h, fw_h, fc_h, iu_h, iv_h, iw_h, it_h, dinv_h, vecs_h, minv_h, eig_h, packed_h, spec_h,
    ou, ov, ow, oc,
    eig, raw, mats, packed, spec, rhs, u10, v14, w10, c18, iu10, iv10, iw14, it14, modal,
    xe, xw, xfw, xfe, yn2, ys2, yfs2, yfn2,
    s1, r1, s2, r2, s3, r3, s4, r4,
    ax, wx, ay, wy, ch, d_buf, vert, yfwd,
    in_sem, h_send, h_recv, p_send, p_recv, ready,
):
    ng = nz // 2
    s, t = lax.axis_index("ys"), lax.axis_index("xs")
    index_of, pair_of, has = owners(nt, ng)
    owner = has(t)
    other = jnp.logical_not(owner)
    mine = pair_of(t)
    late = nt - ng

    barrier = pltpu.get_barrier_semaphore()

    def greet(a, b):
        pl.semaphore_signal(barrier, 1, device_id=(a, b), device_id_type=MESH)

    east, west = lax.rem(t + 1, nt), lax.rem(t + nt - 1, nt)
    north, south = lax.rem(s + 1, ns), lax.rem(s + ns - 1, ns)
    twin = t + 1 - 2 * lax.rem(t, 2)

    @pl.when(owner)
    def _():
        for i in range(nt - 1):
            greet(s, partner(t, i, nt))
        for i in range(1, ns):
            greet(lax.rem(s + i, ns), t)

    if late:

        @pl.when(other)
        def _():
            greet(north, t)
            greet(south, t)
            greet(s, twin)

    loads = []
    for n, src in enumerate((iu_h, iv_h, iw_h, it_h, fc_h, fu_h, fv_h, fw_h)):
        dst = raw.at[n, pl.ds(1, ROWS), pl.ds(8, COLS)]
        loads.append(pltpu.make_async_copy(src, dst, in_sem.at[n]))
    loads.append(pltpu.make_async_copy(spec_h.at[s], spec, in_sem.at[8]))
    loads.append(pltpu.make_async_copy(packed_h, packed, in_sem.at[9]))
    for n, src in enumerate((vecs_h, minv_h, dinv_h)):
        loads.append(pltpu.make_async_copy(src, mats.at[n], in_sem.at[10 + n]))
    loads.append(pltpu.make_async_copy(eig_h, eig, in_sem.at[13]))
    order = (10, 0, 1, 2, 9, 8, 3, 4, 5, 6, 7, 11, 12, 13)
    for n in order:
        loads[n].start()

    lane = lax.broadcasted_iota(jnp.int32, (nz, 128), 1)
    slot = lane & 63
    low = lane < 64
    core = (slot >= 8) & (slot < 40)
    lane_g = lax.broadcasted_iota(jnp.int32, (ng, 128), 1)
    level = lax.broadcasted_iota(jnp.int32, (nz, 640), 0)

    def rows(n, count, used=None):
        return pl.ds(pl.multiple_of(n * count, count), used or count)

    def drain(buf, count, sem):
        part = buf.at[pl.ds(0, count)]
        pltpu.make_async_copy(part, part, sem).wait()

    def tile(n):
        return slice(128 * n, 128 * n + 128)

    def table(n):
        first, end, width = places[n]
        return packed[first:end, :width]

    def place(n, buf, first):
        for k in range(5):
            v = raw[n, 2 * k : 2 * k + 2].reshape(128, nz)
            buf[:, tile(first + k)] = v.T

    def pack_x(fields, out):
        total = jnp.zeros((nz, 128), F32)
        for buf, first, col, at, count in fields:
            for k in range(4):
                if k == 0:
                    v = jnp.where(low, buf[:, tile(first + 4)], buf[:, tile(first)])
                else:
                    v = buf[:, tile(first + k)]
                to = 16 * k + at
                total = jnp.where((slot >= to) & (slot < to + count), roll(v, to - 8 - col), total)
        out[...] = total

    def unpack_x(src, fields):
        v = src[...]
        for buf, first, col, at, count in fields:
            here = (slot >= 8 + col) & (slot < 8 + col + count)
            for k in range(4):
                w = roll(v, 8 + col - 16 * k - at)
                if k == 0:
                    z = tile(first + 4)
                    buf[:, z] = jnp.where(here & low, w, buf[:, z])
                    z = tile(first)
                    buf[:, z] = jnp.where(here & ~low, w, buf[:, z])
                else:
                    z = tile(first + k)
                    buf[:, z] = jnp.where(here, w, buf[:, z])

    def pair(one, two):
        return jnp.where(core, one, roll(two, 32))

    def remote(src, dst, ds, dt, send, recv):
        return pltpu.make_async_remote_copy(
            src_ref=src, dst_ref=dst, send_sem=send, recv_sem=recv, device_id=(ds, dt), device_id_type=MESH
        )

    loads[0].wait()
    loads[1].wait()
    loads[2].wait()
    iu = raw[0, 1:9, 8:40].reshape(ROWS * COLS, nz)
    iv = raw[1, 1:9, 8:40].reshape(ROWS * COLS, nz)
    iw = raw[2, 1:9, 8:40].reshape(ROWS * COLS, nz)
    first_col = lax.broadcasted_iota(jnp.int32, iu.shape, 0) % COLS == 0
    before = jnp.where(first_col, 0.0, roll(iu, 1, 0))
    behind = jnp.concatenate([jnp.zeros((COLS, nz), F32), iv[: 7 * COLS]], 0)
    rhs[0:256, :] = (iu - before) + (iv - behind)
    rhs[256:288, :] = -iv[7 * COLS :]
    rhs[288:416, :] = jnp.zeros((128, nz), F32)
    for r in range(ROWS):
        at = 288 + 32 * (r % 4) + r // 4
        rhs[at : at + 1, :] = -raw[0, r + 1, 39:40, :]
    loads[10].wait()
    vt = mats[0].T
    next_vt = jnp.concatenate([vt[:, 1:], jnp.zeros((nz, 1), F32)], 1)
    both = dot_nt(vt, rhs[...])
    main, extra = both[:, :256] + dot_nt(vt - next_vt, iw), both[:, 256:]
    modal[0] = main[:, :128]
    modal[1] = main[:, 128:]
    modal[2] = jnp.concatenate([extra[:, :32], jnp.zeros((nz, 96), F32)], 1)
    modal[3] = extra[:, 32:]
    for i in range(4):
        even = modal[i, pl.ds(0, ng, stride=2), :]
        odd = modal[i, pl.ds(1, ng, stride=2), :]
        if i < 2:
            s1[pl.ds(i, ng, stride=8), :] = even
            s1[pl.ds(2 + i, ng, stride=8), :] = odd
        elif i == 2:
            s1[pl.ds(4, ng, stride=8), :] = jnp.where(lane_g < 32, even, roll(odd, 32))
        else:
            s1[pl.ds(5, ng, stride=8), :] = jnp.where((lane_g & 31) < 2, even, roll(odd, 2))

    @pl.when(owner)
    def _():
        pl.semaphore_wait(barrier, ng - 1 + ns - 1)

    if late:

        @pl.when(other)
        def _():
            pl.semaphore_wait(barrier, ng + 3)

    def send1(to):
        @pl.when(has(to))
        def _():
            remote(s1.at[rows(pair_of(to), 8, 6)], r1.at[rows(t, 8, 6)], s, to, p_send.at[0], p_recv.at[0]).start()

    for i in range(nt - 1):
        send1(partner(t, i, nt))

    @pl.when(owner)
    def _():
        pltpu.make_async_copy(s1.at[rows(mine, 8, 6)], r1.at[rows(t, 8, 6)], p_recv.at[0]).start()

    if late:

        @pl.when(other)
        def _():
            def report(i, _):
                g = index_of(i)
                pl.semaphore_signal(ready, 1, device_id=(s, g), device_id_type=MESH)
                return 0

            lax.fori_loop(0, ng, report, 0)

    for n, buf, first in ((3, it14, 1), (4, c18, 2), (5, u10, 0), (6, v14, 1), (7, w10, 0)):
        loads[n].wait()
        place(n, buf, first)
    place(0, iu10, 0)
    place(1, iv10, 0)
    place(2, iw14, 1)

    pack_x(((iw14, 1, 29, 0, 3), (it14, 1, 29, 3, 3), (iu10, 0, 31, 6, 1), (iv10, 0, 31, 7, 1), (u10, 0, 29, 8, 3), (c18, 2, 27, 11, 5)), xe)
    pack_x(((iw14, 1, 0, 0, 3), (it14, 1, 0, 3, 3), (iu10, 0, 0, 6, 1), (iv10, 0, 0, 7, 1), (u10, 0, 0, 8, 2), (c18, 2, 0, 11, 5)), xw)
    for n in range(3):
        yn2[n] = pair(c18[:, tile(4 + n)], v14[:, tile(3 + n)])
        ys2[n] = pair(c18[:, tile(2 + n)], v14[:, tile(1 + n)])
    for n in range(2):
        yn2[3 + n] = pair(iw14[:, tile(4 + n)], it14[:, tile(4 + n)])
        ys2[3 + n] = pair(iw14[:, tile(1 + n)], it14[:, tile(1 + n)])
    yn2[5] = pair(iu10[:, tile(4)], iv10[:, tile(4)])
    ys2[5] = pair(iu10[:, tile(0)], iv10[:, tile(0)])
    halos = [
        remote(xe, xfw, s, east, h_send.at[0], h_recv.at[0]),
        remote(yn2, yfs2, north, t, h_send.at[1], h_recv.at[1]),
        remote(xw, xfe, s, west, h_send.at[2], h_recv.at[2]),
        remote(ys2, yfn2, south, t, h_send.at[3], h_recv.at[3]),
    ]
    halos[1].start()
    halos[3].start()
    loads[9].wait()
    yfwd[...] = jnp.concatenate([table(2), table(3)], 1)

    @pl.when(owner)
    def _():
        drain(r1, 6 * nt, p_recv.at[0])
        x = jnp.concatenate([r1[pl.ds(i, nt, stride=8), :] for i in range(6)], 1)
        both = dot(packed[places[4][0] : places[5][1], :nt], x)
        y, z = both[:nt], both[nt:, tile(5)]
        first = (lax.broadcasted_iota(jnp.int32, (nt, 128), 1) & 31) == 0
        at = lax.broadcasted_iota(jnp.int32, (ns, 128), 1)
        parts = [y[:, tile(i)] + jnp.where(first, roll(z, -i), 0.0) for i in range(4)]
        for q in range(2):
            for i in range(4):
                s2[pl.ds(4 * q + i, ns, stride=16), :] = parts[i][q * ns : (q + 1) * ns]
        s2[pl.ds(8, ns, stride=16), :] = jnp.where(at < 64, y[:ns, tile(4)], roll(y[ns:, tile(4)], 64))

        for i in range(1, ns):
            j = lax.rem(s + i, ns)
            remote(s2.at[rows(j, 16, 9)], r2.at[rows(s, 16, 9)], j, t, p_send.at[1], p_recv.at[1]).start()
        pltpu.make_async_copy(s2.at[rows(s, 16, 9)], r2.at[rows(s, 16, 9)], p_recv.at[1]).start()

    if late:

        @pl.when(owner)
        def _():
            pl.semaphore_wait(ready, late)

    halos[0].start()
    halos[2].start()

    diffusion = (0.0, 0.0, KAPPA, -KAPPA, 0.0, 0.0)
    halos[1].wait_recv()
    halos[3].wait_recv()
    v = yfs2[5]
    iu10[:, tile(0)] = jnp.where(low, v, iu10[:, tile(0)])
    iv10[:, tile(0)] = jnp.where(low, roll(v, -32), iv10[:, tile(0)])
    v = yfn2[5]
    iu10[:, tile(4)] = jnp.where(low, iu10[:, tile(4)], v)
    iv10[:, tile(4)] = jnp.where(low, iv10[:, tile(4)], roll(v, -32))
    for n in range(3):
        v = yfs2[n]
        for buf, k, f in ((c18, n, v), (v14, n - 1, roll(v, -32))):
            if k >= 0:
                buf[:, tile(k)] = f if n < 2 else jnp.where(low, f, buf[:, tile(k)])
        v = yfn2[n]
        for buf, k, f in ((c18, 6 + n, v), (v14, 5 + n, roll(v, -32))):
            if k < buf.shape[1] // 128:
                buf[:, tile(k)] = f if n > 0 else jnp.where(low, buf[:, tile(k)], f)
    for n in range(2):
        v = yfs2[3 + n]
        for buf, f in ((iw14, v), (it14, roll(v, -32))):
            buf[:, tile(n)] = f if n < 1 else jnp.where(low, f, buf[:, tile(n)])
        v = yfn2[3 + n]
        for buf, f in ((iw14, v), (it14, roll(v, -32))):
            buf[:, tile(5 + n)] = f if n > 0 else jnp.where(low, buf[:, tile(5 + n)], f)

    def y_faces(n, _):
        at = pl.ds(pl.multiple_of(8 * n, 8), 8)
        value, parts = weno_parts(c18[at, :], v14[at, :], 64, lambda f: f[:, 128:1024])
        wy[at, :] = DT * value[:, 128:768]
        for o in range(6):
            ay[o, at, :] = roll(DT * (parts[o] + diffusion[o]), 64 * (o - 2))[:, 128:768]
        return 0

    lax.fori_loop(0, nz // 8, y_faces, 0)

    @pl.when(owner)
    def _():
        loads[8].wait()
        loads[13].wait()
        drain(r2, 9 * ns, p_recv.at[1])
        part = [
            jnp.concatenate([r2[pl.ds(2 * n + i, ns, stride=16), :] for i in range(2)], 0) for n in range(4)
        ]
        group = lax.broadcasted_iota(jnp.int32, (2 * ns, 128), 1) // 32
        x = []
        for r in range(4):
            v = roll(part[0], -32 * r)
            for n in range(1, 4):
                v = jnp.where(group == n, roll(part[n], 32 * (n - r)), v)
            x.append(v)
        x.append(r2[pl.ds(8, ns, stride=16), :])
        y = dot(yfwd[...], jnp.concatenate(x, 0))
        inner = spec[0:128, :]
        y = dot(y, inner)
        wide = lax.broadcasted_iota(jnp.int32, (1, 128), 1)
        own = jnp.where((wide & 32) == 0, eig[2 * mine], eig[2 * mine + 1])
        y = -y / (own + table(0) + spec[128:129, :])
        y = dot(table(1), dot_nt(y, inner))
        s3[...] = y

        for i in range(1, ns):
            j = lax.rem(s + i, ns)
            remote(s3.at[rows(j, 16, 14)], r3.at[rows(s, 16, 14)], j, t, p_send.at[2], p_recv.at[2]).start()
        pltpu.make_async_copy(s3.at[rows(s, 16, 14)], r3.at[rows(s, 16, 14)], p_recv.at[2]).start()

    halos[0].wait_recv()
    unpack_x(xfw, ((iw14, 1, -3, 0, 3), (it14, 1, -3, 3, 3), (iu10, 0, -1, 6, 1), (iv10, 0, -1, 7, 1), (u10, 0, -3, 8, 3), (c18, 2, -5, 11, 5)))
    halos[2].wait_recv()
    unpack_x(xfe, ((iw14, 1, 32, 0, 3), (it14, 1, 32, 3, 3), (iu10, 0, 32, 6, 1), (iv10, 0, 32, 7, 1), (u10, 0, 32, 8, 2), (c18, 2, 32, 11, 5)))

    def x_faces(n, _):
        at = pl.ds(pl.multiple_of(8 * n, 8), 8)
        value, parts = weno_parts(c18[at, 256:896], u10[at, :], 1, lambda f: f)
        wx[at, :] = DT * value
        for o in range(6):
            ax[o, at, :] = roll(DT * (parts[o] + diffusion[o]), o - 2)
        return 0

    lax.fori_loop(0, nz // 8, x_faces, 0)

    @pl.when(owner)
    def _():
        drain(r3, 14 * ns, p_recv.at[2])
        left = lax.broadcasted_iota(jnp.int32, (ns, 128), 1) < 64
        cols = []
        for i in range(7):
            one = r3[pl.ds(2 * i, ns, stride=16), :]
            two = r3[pl.ds(2 * i + 1, ns, stride=16), :]
            cols.append(
                jnp.concatenate(
                    [
                        jnp.where(left, one, roll(two, 64)),
                        jnp.where(left, roll(one, 64), two),
                    ],
                    0,
                )
            )
        y = dot(table(6), jnp.concatenate(cols, 1))
        at = lax.broadcasted_iota(jnp.int32, (nt, 128), 1) & 31
        edge = jnp.zeros((nt, 128), F32)
        before, after = roll(y, 1, 0), roll(y, -1, 0)
        for i in range(7):
            s4[pl.ds(i, nt, stride=8), :] = y[:, tile(i)]
            if 1 <= i <= 5:
                k = 3 * (i - 1)
                edge = jnp.where((at >= k) & (at < k + 3), roll(before[:, tile(i)], k - 29), edge)
                edge = jnp.where((at >= 16 + k) & (at < 19 + k), roll(after[:, tile(i)], 16 + k), edge)
        s4[pl.ds(7, nt, stride=8), :] = edge

        for i in range(nt - 1):
            g = partner(t, i, nt)
            remote(s4.at[rows(g, 8)], r4.at[rows(mine, 8)], s, g, p_send.at[3], p_recv.at[3]).start()
        pltpu.make_async_copy(s4.at[rows(t, 8)], r4.at[rows(mine, 8)], p_recv.at[3]).start()

    c10 = c18[:, 256:896]
    ch[0] = jnp.where(level == nz - 1, 0.0, 0.5 * DT * (c10 + roll(c10, -1, 0)))
    ch[1] = jnp.where(level == nz - 1, 0.0, 0.5 * DT * w10[...])
    iw = iw14[:, 128:768]
    it14[...] = it14[...] + GRAV * DT * iw14[...]
    w10[...] = iw + DT * NU * spread(iw)
    iu10[...] = iu10[...] + DT * NU * spread(iu10[...])
    iv10[...] = iv10[...] + DT * NU * spread(iv10[...])
    for n in (11, 12):
        loads[n].wait()
    vert[0] = jnp.concatenate([mats[1, pl.ds(0, ng, stride=2), :], mats[1, pl.ds(1, ng, stride=2), :]], 0).T
    vert[1] = mats[2].T

    pltpu.make_async_copy(r4, r4, p_recv.at[3]).wait()
    cols = []
    for i in range(8):
        one = r4[pl.ds(i, ng, stride=8), :]
        cols.append(jnp.concatenate([roll(one, 8), roll(one, -24)], 0))
    p = dot(vert[0], jnp.concatenate(cols, 1))
    edge = p[:, tile(7)]
    cols = []
    for i in range(7):
        v = p[:, tile(i)]
        if 1 <= i <= 5:
            k = 3 * (i - 1)
            v = jnp.where((slot >= 5) & (slot < 8), roll(edge, -3 - k), v)
            v = jnp.where((slot >= 40) & (slot < 43), roll(edge, 16 - k), v)
        cols.append(v)
    p = jnp.concatenate(cols, 1)
    top = lax.broadcasted_iota(jnp.int32, p.shape, 0) == nz - 1
    upper = jnp.where(top, 0.0, roll(p, -1, 0))
    d_buf[...] = dot(vert[1], it14[...] - GRAV * DT * (upper - p))
    p = p + DT * NU * spread(p)
    p10 = p[:, 128:768]
    ow[...] = w10[...] - (jnp.where(level == nz - 1, 0.0, roll(p10, -1, 0)) - p10)
    ou[...] = iu10[...] - (roll(p10, -1) - p10)
    ov[...] = iv10[...] - (roll(p, -64)[:, 128:768] - p10)
    d10 = d_buf[:, 128:768]
    gz = roll(d10, -1, 0) - d10
    wz = ch[1] * gz
    oc[...] = d10 + (wz + roll(wz, 1, 0))
    ow[...] = ow[...] + ch[0] * gz

    for n in range(nz // 8):
        at = slice(8 * n, 8 * n + 8)
        d14 = d_buf[at, :]
        dx = d14[:, 128:768]
        gx = roll(dx, -1) - dx
        ahead = roll(d14, -64)
        gy, gy_back = ahead - d14, d14 - roll(d14, 64)
        total = oc[at, :]
        for o in range(6):
            total = total + ax[o, at, :] * roll(gx, o - 2)
            first = 128 - 64 * (o - 2)
            g = gy if o % 2 == 0 else gy_back
            first = first if o % 2 == 0 else first + 64
            total = total + ay[o, at, :] * g[:, first : first + 640]
        ou[at, :] = ou[at, :] + wx[at, :] * gx
        ov[at, :] = ov[at, :] + wy[at, :] * gy[:, 128:768]
        oc[at, :] = total

    for copy in halos:
        copy.wait_send()

    @pl.when(owner)
    def _():
        for n, buf, count in ((0, s1, 6 * (ng - 1)), (1, s2, 9 * (ns - 1)), (2, s3, 14 * (ns - 1)), (3, s4, 8 * (nt - 1))):
            drain(buf, count, p_send.at[n])

    if late:

        @pl.when(other)
        def _():
            drain(s1, 6 * ng, p_send.at[0])
            loads[13].wait()
            loads[8].wait()


def finish(a, b, c, d, out_a, out_b, out_c, out_d, made, sem):
    copies = []
    for n, (src, dst) in enumerate(((a, out_a), (b, out_b), (c, out_c), (d, out_d))):
        for k in range(5):
            v = src[:, 128 * k : 128 * k + 128].T
            if k > 0:
                made[n, 2 * k - 1] = v[8:40]
            if k < 4:
                made[n, 2 * k] = v[72:104]
            if k in (2, 4):
                part = pl.ds(2 * (k - 2), 4)
                copy = pltpu.make_async_copy(made.at[n, part], dst.at[part], sem.at[n, k // 2 - 1])
                copy.start()
                copies.append(copy)
    for copy in copies:
        copy.wait()


def call(ns, nt, nz, consts, *args):
    ng = nz // 2
    packed, spectral, places = consts
    vmem, anywhere = pl.BlockSpec(memory_space=pltpu.VMEM), pl.BlockSpec(memory_space=pl.ANY)

    def buf(*shape):
        return pltpu.VMEM(shape, F32)

    out = jax.ShapeDtypeStruct((ROWS, COLS, nz), F32)
    made = pl.pallas_call(
        functools.partial(kernel, ns, nt, nz, places),
        out_shape=[pltpu.VMEM((nz, 640), F32)] * 4,
        in_specs=[anywhere] * 14,
        out_specs=[vmem] * 4,
        scratch_shapes=[
            pltpu.SMEM((nz,), F32), buf(8, 10, 64, nz), buf(3, nz, nz), buf(*packed.shape), buf(136, 128), buf(416, nz),
            buf(nz, 640), buf(nz, 896), buf(nz, 640), buf(nz, 1152),
            buf(nz, 640), buf(nz, 640), buf(nz, 896), buf(nz, 896), buf(8, nz, 128),
            buf(nz, 128), buf(nz, 128), buf(nz, 128), buf(nz, 128),
            buf(6, nz, 128), buf(6, nz, 128), buf(6, nz, 128), buf(6, nz, 128),
            buf(8 * ng, 128), buf(8 * nt, 128), buf(16 * ns, 128), buf(16 * ns, 128),
            buf(16 * ns, 128), buf(16 * ns, 128), buf(8 * nt, 128), buf(8 * ng, 128),
            buf(6, nz, 640), buf(nz, 640), buf(6, nz, 640), buf(nz, 640), buf(2, nz, 640),
            buf(nz, 896), buf(2, nz, nz), buf(ROWS * ns, ROWS * ns + ns),
            pltpu.SemaphoreType.DMA((14,)), pltpu.SemaphoreType.DMA((4,)), pltpu.SemaphoreType.DMA((4,)),
            pltpu.SemaphoreType.DMA((4,)), pltpu.SemaphoreType.DMA((4,)), pltpu.SemaphoreType.REGULAR,
        ],
        compiler_params=pltpu.CompilerParams(
            collective_id=0, has_side_effects=True, vmem_limit_bytes=60 * 1024 * 1024
        ),
    )(*args, jnp.asarray(packed), jnp.asarray(spectral))
    return pl.pallas_call(
        finish,
        out_shape=[out] * 4,
        in_specs=[vmem] * 4,
        out_specs=[anywhere] * 4,
        scratch_shapes=[buf(4, ROWS, COLS, nz), pltpu.SemaphoreType.DMA((4, 2))],
    )(*[pltpu.with_memory_space_constraint(v, pltpu.VMEM) for v in made])


def solution(mesh):
    ns, nt = mesh.shape["ys"], mesh.shape["xs"]
    consts = tables(ns, nt)

    def shards(*args):
        flat = [v.transpose(1, 2, 0) for v in args[:8]]
        out = call(ns, nt, args[0].shape[0], consts, *flat, *args[8:])
        return tuple(v.transpose(2, 0, 1) for v in out)

    block = P(None, "ys", "xs")
    return jax.shard_map(
        shards, mesh=mesh, in_specs=(block,) * 8 + (P(),) * 4, out_specs=(block,) * 4, check_vma=False
    )
```
